32 devices in a mesh: gx: 16 (over z, y, x), gz: 2 (over core).
Axes of the slice: x: 2, y: 2, z: 4, core: 2. Of those that a mesh axis runs over, the one named last changes fastest.
Arguments:
- state: float32 [16, 4, 4, 64, 128], P('gx', 'gz'), may hold values from -6 to 6
- target: float32 [16, 4, 4, 64, 128], P('gx', 'gz'), may hold values from -6 to 6
- coarse_logk: float32 [1024], P(('gx', 'gz')), may hold values from -1 to 1
- cell_slot: int32 [1024], replicated, may hold values from 0 to 1023, each once
- cell_of: int32 [16, 4, 128], P('gx', 'gz'), may hold values from 0 to 1023, as said below
- wall_flags_xaxis: int32 [2, 4, 128], P(None, 'gz'), may hold values 0 or 1
- z_wall: int32 [2, 16, 128], P(None, 'gx'), may hold values 0 or 1
Outputs:
- adjoint_field: float32 [16, 4, 4, 64, 128], P('gx', 'gz')
- coarse_gradient: float32 [1024], P(('gx', 'gz'))
The draws below stay inside these ranges and needn't reach their ends.
Inputs may be any that keep to these rules, and one draw needn't show every extreme that they name: `cell_of`: element (x, z, y) lies in coarse cell (q * 2 + z // 2) * 128 + y, where q = x // 4, except that q may be x // 4 - 1 when x % 4 == 0 and x // 4 + 1 when x % 4 == 3, always within 0 to 3. A permutation: coarse cell c is held at position cell_slot[c] of coarse_logk and coarse_gradient.
All inputs are finite; a program needn't handle non-finite values. No bound on the sum of `wall_flags_xaxis` or of `z_wall` on one device may be relied on, other than what follows from the above.
Results may differ from the reference program's by a relative error of at most 0.0003.
Values sent between devices are 32-bit elements; how exact they have to be, the bound alone decides.
No kernel may reach another device: no remote copies, remote signals or barrier semaphores. Data moves between devices by JAX's collectives and lax.ppermute only.
A program may use at most 64 MiB of HBM per device.

```python
import math
import jax
import jax.numpy as jnp
import numpy as np
from jax import lax

ELEMENTS_Y = 128
ELEMENT_FIELDS = 4
ELEMENT_NODES = 64
ELEMENTS_X = 16
ELEMENTS_Z = 4
KX = 4
KZ = 2
CELLS = 1024


def draw_cell_of(key, part):
    along_x = jnp.arange(ELEMENTS_X, dtype=jnp.int32)[:, None, None]
    through_zaxis = jnp.arange(ELEMENTS_Z, dtype=jnp.int32)[None, :, None]
    along_y = jnp.arange(ELEMENTS_Y, dtype=jnp.int32)[None, None, :]
    shifted_result = jax.random.randint(key, (ELEMENTS_X, ELEMENTS_Z, ELEMENTS_Y), 0, 2).astype(jnp.int32)
    remainder = along_x % 4
    offset = jnp.where(remainder == 0, -shifted_result, jnp.where(remainder == 3, shifted_result, 0))
    coarse_x = jnp.clip(along_x // 4 + offset, 0, KX - 1)
    return ((coarse_x * KZ + through_zaxis // 2) * ELEMENTS_Y + along_y).astype(jnp.int32)


def touch_ends(values, key, least, high):
    spot = [jax.random.randint(jax.random.fold_in(key, axis), (), 0, length) for axis, length in enumerate(values.shape)]
    widest = values.shape.index(max(values.shape))
    neighbour = spot[:widest] + [(spot[widest] + 1) % values.shape[widest]] + spot[widest + 1:]
    return values.at[tuple(spot)].set(least).at[tuple(neighbour)].set(high)


def levels(own_key, shape, pieces, low, top_value):
    factor_of = 1.0
    for axis_at, shards_of in pieces:
        draws = jax.random.uniform(jax.random.fold_in(jax.random.fold_in(own_key, 6), axis_at), (shards_of,), jnp.float32, low / len(pieces), top_value / len(pieces))
        factor_of = factor_of * jnp.repeat(jnp.exp(draws), shape[axis_at] // shards_of).reshape((-1,) + (1,) * (len(shape) - 1 - axis_at))
    return factor_of


def scatter_about(stream_key, extent, scale, reach, split=(), kind=jnp.bfloat16):
    loudness = levels(stream_key, extent, split, -0.22, 0.18) if split else 1.0
    values = jax.random.normal(stream_key, extent, jnp.float32) * scale * loudness
    return jnp.minimum(jnp.maximum(values, -reach), reach).astype(kind)


def setup_inputs(seed: int = 0) -> dict:
    key_of = jax.random.split(jax.random.key(seed), 8)
    return {
        "state": scatter_about(key_of[0], (ELEMENTS_X, ELEMENTS_Z, ELEMENT_FIELDS, ELEMENT_NODES, ELEMENTS_Y), 1.0, 6.0, ((0, 16), (1, 2)), jnp.float32),
        "target": scatter_about(key_of[1], (ELEMENTS_X, ELEMENTS_Z, ELEMENT_FIELDS, ELEMENT_NODES, ELEMENTS_Y), 1.0, 6.0, ((0, 16), (1, 2)), jnp.float32),
        "coarse_logk": jnp.clip(jax.random.uniform(key_of[2], (CELLS,), jnp.float32, -1.0, 1.0) * levels(key_of[2], (CELLS,), ((0, 32),), -0.4, 0.0), -1.0, 1.0),
        "cell_slot": jax.random.permutation(key_of[3], CELLS).astype(jnp.int32),
        "cell_of": draw_cell_of(jax.random.fold_in(key_of[7], 71), 0),
        "wall_flags_xaxis": touch_ends((jax.random.randint(key_of[5], (2, ELEMENTS_Z, ELEMENTS_Y), 0, 2) < 1).astype(jnp.int32), jax.random.fold_in(key_of[5], 1), 0, 1),
        "z_wall": touch_ends((jax.random.randint(key_of[6], (2, ELEMENTS_X, ELEMENTS_Y), 0, 2) < 1).astype(jnp.int32), jax.random.fold_in(key_of[6], 1), 0, 1),
    }


penalty = 0.5
operator_scale = 0.25
lift_factor = 6.0

def derivative_tables():
    points = np.array([-1.0, -math.sqrt(0.2), math.sqrt(0.2), 1.0])
    products = np.array([np.prod([points[first] - points[other] for other in range(4) if other != first]) for first in range(4)])
    matrix = np.zeros((4, 4))
    for first in range(4):
        for second in range(4):
            if first != second:
                matrix[first, second] = products[first] / products[second] / (points[first] - points[second])
        matrix[first, first] = sum((1.0 / (points[first] - points[other]) for other in range(4) if other != first))
    identity = np.eye(4)
    tables = np.stack([np.kron(np.kron(matrix, identity), identity), np.kron(np.kron(identity, matrix), identity), np.kron(np.kron(identity, identity), matrix)])
    return jnp.asarray(tables, jnp.float32)

def flux_matrix(axis, sign):
    matrix = -penalty * np.eye(4)
    matrix[axis, 3] = 0.5 * sign
    matrix[3, axis] = 0.5 * sign
    return jnp.asarray(matrix, jnp.float32)

def flux(axis, sign, values):
    return jnp.einsum('gf,xzfpqy->xzgpqy', flux_matrix(axis, sign), values, precision=lax.Precision.HIGHEST)

def sign_fields(flags, axis):
    wall = np.ones(4)
    wall[axis] = -1.0
    opened = np.ones(4)
    opened[3] = -1.0
    wall = jnp.asarray(wall, jnp.float32)[None, :, None]
    opened = jnp.asarray(opened, jnp.float32)[None, :, None]
    return flags[:, None, :] * wall + (1.0 - flags[:, None, :]) * opened

def volume_terms(field, resistance, adjoint):
    tables = derivative_tables()
    velocity = field[:, :, 0:3]
    pressure = field[:, :, 3]
    if adjoint:
        grads = jnp.einsum('knm,xzny->xzkmy', tables, pressure, precision=lax.Precision.HIGHEST)
        divergence = jnp.einsum('knm,xzkny->xzmy', tables, velocity, precision=lax.Precision.HIGHEST)
    else:
        grads = jnp.einsum('kmn,xzny->xzkmy', tables, pressure, precision=lax.Precision.HIGHEST)
        divergence = jnp.einsum('kmn,xzkny->xzmy', tables, velocity, precision=lax.Precision.HIGHEST)
    shifted_result = resistance[:, :, None, None, :] * velocity + grads
    return jnp.concatenate([shifted_result, divergence[:, :, None]], axis=2)

def face_traces(field7):
    return {(0, -1): field7[:, :, :, 0], (0, 1): field7[:, :, :, 3], (1, -1): field7[:, :, :, :, 0], (1, 1): field7[:, :, :, :, 3], (2, -1): field7[:, :, :, :, :, 0], (2, 1): field7[:, :, :, :, :, 3]}

def add_face(result7, axis, sign, values):
    position = 0 if sign < 0 else 3
    index = (slice(None),) * (3 + axis) + (position,)
    return result7.at[index].add(values)

def edge(values, dim, sign):
    length = values.shape[dim]
    if sign < 0:
        return lax.slice_in_dim(values, 0, 1, axis=dim)
    return lax.slice_in_dim(values, length - 1, length, axis=dim)

def neighbour_shift(values, dim, sign, fill):
    length = values.shape[dim]
    if sign < 0:
        return jnp.concatenate([fill, lax.slice_in_dim(values, 0, length - 1, axis=dim)], axis=dim)
    return jnp.concatenate([lax.slice_in_dim(values, 1, length, axis=dim), fill], axis=dim)

def apply_operator(field, resistance, wall_flags_xaxis, z_wall, adjoint):
    x_count, z_count, _, _, y_count = field.shape
    field7 = field.reshape(x_count, z_count, 4, 4, 4, 4, y_count)
    result7 = volume_terms(field, resistance, adjoint).reshape(x_count, z_count, 4, 4, 4, 4, y_count)
    faces = face_traces(field7)
    if adjoint:
        payload = {key: flux(key[0], key[1], value) for key, value in faces.items()}
    else:
        payload = faces
    x_flags = wall_flags_xaxis.astype(jnp.float32)
    z_flags = z_wall.astype(jnp.float32)
    for axis in range(3):
        for sign in (-1, 1):
            face = faces[axis, sign]
            inner = payload[axis, -sign]
            base = payload[axis, sign]
            if axis == 1:
                outer = jnp.roll(inner, -sign, axis=5)
            elif axis == 0:
                signs = sign_fields(x_flags[(sign + 1) // 2], 0)[None, :, :, None, None, :]
                outer = neighbour_shift(inner, 0, sign, signs * edge(base, 0, sign))
            else:
                signs = sign_fields(z_flags[(sign + 1) // 2], 2)[:, None, :, None, None, :]
                outer = neighbour_shift(inner, 1, sign, signs * edge(base, 1, sign))
            if adjoint:
                jump = outer - base
            else:
                jump = flux(axis, sign, outer - face)
            result7 = add_face(result7, axis, sign, lift_factor * jump)
    return operator_scale * result7.reshape(x_count, z_count, 4, 64, y_count)

def reference(state, target, coarse_logk, cell_slot, cell_of, wall_flags_xaxis, z_wall):
    slots = cell_slot[cell_of]
    resistance = jnp.exp(-coarse_logk[slots])
    residual = apply_operator(state, resistance, wall_flags_xaxis, z_wall, False) - target
    adjoint_field = apply_operator(residual, resistance, wall_flags_xaxis, z_wall, True)
    term = -(operator_scale / 64.0) * resistance * lax.optimization_barrier(jnp.sum(residual[:, :, 0:3] * state[:, :, 0:3], axis=(2, 3)))
    coarse_gradient = jnp.zeros(coarse_logk.shape, jnp.float32).at[slots.reshape(-1)].add(term.reshape(-1))
    return (adjoint_field, coarse_gradient)
```

```python
import functools
import math

import jax
import jax.numpy as jnp
import numpy as np
from jax import lax
from jax.experimental import pallas as pl
from jax.experimental.pallas import tpu as pltpu
from jax.sharding import PartitionSpec as P

SCALE = 0.25
JUMP = 0.75
LANES = 128
VMEM = pl.BlockSpec(memory_space=pltpu.VMEM)

X_FIELDS, X_TRACES, X_SLOTS, X_BLOCKS = 0, 16, 28, 29
Z_SLOTS, Z_BLOCKS = 32, 33
W_CORNERS, W_BLOCKS = 32, 48


def derivative_matrix():
    points = np.array([-1.0, -math.sqrt(0.2), math.sqrt(0.2), 1.0])
    products = np.array(
        [
            np.prod([points[first] - points[other] for other in range(4) if other != first])
            for first in range(4)
        ]
    )
    matrix = np.zeros((4, 4))
    for first in range(4):
        for second in range(4):
            if first != second:
                matrix[first, second] = (
                    products[first] / products[second] / (points[first] - points[second])
                )
        matrix[first, first] = sum(
            (1.0 / (points[first] - points[other]) for other in range(4) if other != first)
        )
    return matrix


class Rows:
    def __init__(self):
        row = lax.broadcasted_iota(jnp.int32, (8, LANES), 0)
        self.upper = row >= 4
        self.c = row & 3

    def halves(self, low, high):
        return jnp.where(self.upper, jnp.float32(high), jnp.float32(low))

    def by_c(self, values):
        result = jnp.full((8, LANES), values[0], jnp.float32)
        for c in range(1, 4):
            result = jnp.where(self.c == c, jnp.float32(values[c]), result)
        return result


class Derivative:
    def __init__(self, rows, matrix):
        self.matrix = matrix
        self.same = [
            [rows.halves(matrix[2 * h, 2 * g], matrix[2 * h + 1, 2 * g + 1]) for g in range(2)]
            for h in range(2)
        ]
        self.cross = [
            [rows.halves(matrix[2 * h, 2 * g + 1], matrix[2 * h + 1, 2 * g]) for g in range(2)]
            for h in range(2)
        ]
        self.shift = {
            delta: rows.by_c(
                [matrix[c, c + delta] if 0 <= c + delta < 4 else 0.0 for c in range(4)]
            )
            for delta in range(-3, 4)
        }

    def along(self, axis, u):
        if axis == 0:
            return jnp.stack(
                [sum(float(self.matrix[a, j]) * u[j] for j in range(4)) for a in range(4)]
            )
        if axis == 1:
            swapped = pltpu.roll(u, 4, 2)
            return jnp.stack(
                [
                    sum(self.same[h][g] * u[:, g] + self.cross[h][g] * swapped[:, g] for g in range(2))
                    for h in range(2)
                ],
                axis=1,
            )
        return sum(
            coefficient * (u if delta == 0 else pltpu.roll(u, -delta % 8, 2))
            for delta, coefficient in self.shift.items()
        )


def traces(fields, axis, sign):
    others = [fields[f] for f in range(3) if f != axis]
    return others + [fields[axis] + sign * fields[3]]


def face_terms(inner, outer, axis, sign, weight, adjoint):
    tangential = [weight * (i - o) for i, o in zip(inner[:2], outer[:2])]
    normal = weight * (inner[2] - outer[2])
    if adjoint:
        pressure = (-sign) * (weight * (inner[2] + outer[2]))
    else:
        pressure = (-sign) * normal
    terms = tangential[:]
    terms.insert(axis, normal)
    return terms + [pressure]


def y_terms(fields, rows, adjoint):
    high_weight = rows.halves(0.0, JUMP)
    low_weight = rows.halves(JUMP, 0.0)
    first = [field[:, 0] for field in fields]
    second = [field[:, 1] for field in fields]
    moved = lambda value, step: pltpu.roll(pltpu.roll(value, 4, 1), step, 2)
    flip = 1.0 if adjoint else -1.0
    high_out = [moved(t, LANES - 1) for t in traces(first, 1, flip)]
    high = face_terms(traces(second, 1, -1.0), high_out, 1, 1.0, high_weight, adjoint)
    low_out = [moved(t, 1) for t in traces(second, 1, -flip)]
    low = face_terms(traces(first, 1, 1.0), low_out, 1, -1.0, low_weight, adjoint)
    return [jnp.stack([l, h], axis=1) for l, h in zip(low, high)]


def z_terms(inner, outer_fields, sign, weight, adjoint):
    flip = sign if adjoint else -sign
    outer = [pltpu.roll(t, 3 if sign > 0 else 5, t.ndim - 2) for t in traces(outer_fields, 2, flip)]
    return face_terms(traces(inner, 2, -sign), outer, 2, sign, weight, adjoint)


def wall_terms(fields, axis, sign, weight, flag, adjoint):
    inner = traces(fields, axis, -sign)
    image = inner[2] if adjoint else fields[axis] + sign * fields[3]
    outer = inner[:2] + [(1.0 - 2.0 * flag) * image]
    return face_terms(inner, outer, axis, sign, weight, adjoint)


def z_weights(rows):
    return {-1: jnp.where(rows.c == 0, JUMP, 0.0), 1: jnp.where(rows.c == 3, JUMP, 0.0)}


def load(ref, z):
    return [ref[z, f] for f in range(4)]


def local_kernel(sizes, state, target, cell_of, cell_slot, z_wall, local, pay_a, pay_b, *z_pay):
    nx, nz = sizes
    x_place, z_place = lax.axis_index("gx"), lax.axis_index("gz")
    rows = Rows()
    derivative = Derivative(rows, derivative_matrix())
    weights = z_weights(rows)
    cell_rows = cell_slot.shape[0]
    slots = []
    for z in range(2):
        row_of = lax.shift_right_logical(cell_of[z : z + 1, :], 7)
        slot = jnp.zeros((1, LANES), jnp.int32)
        for step in (-1, 0, 1):
            row = (x_place // 4 + step) * nz + z_place
            row = jnp.clip(row, 0, cell_rows - 1)
            slot = jnp.where(row_of == row, cell_slot[pl.ds(row, 1), :], slot)
        slots.append(slot.astype(jnp.float32))
    row = lax.broadcasted_iota(jnp.int32, (8, LANES), 0)
    slot_block = jnp.where(row == 0, slots[0], jnp.where(row == 1, slots[1], 0.0))
    even = x_place % 2 == 0
    pay_a[X_SLOTS] = slot_block
    pay_b[X_SLOTS] = slot_block
    for z in range(2):
        u = load(state, z)
        other = load(state, 1 - z)
        grads = [derivative.along(k, u[3]) for k in range(3)]
        divergence = sum(derivative.along(k, u[k]) for k in range(3))
        jumps = y_terms(u, rows, False)
        sign = 1.0 if z == 0 else -1.0
        across = z_terms(u, other, sign, weights[int(sign)], False)
        end = (z_place == 0) if z == 0 else (z_place == nz - 1)
        weight = weights[-int(sign)] * jnp.where(end, 1.0, 0.0)
        flag = z_wall[z : z + 1, :].astype(jnp.float32)
        wall = wall_terms(u, 2, -sign, weight, flag, False)
        result = [
            SCALE * v + j + a + w - target[z, f]
            for f, (v, j, a, w) in enumerate(zip(grads + [divergence], jumps, across, wall))
        ]
        for f in range(4):
            local[z, f] = result[f]
        low = [u[f][0] for f in range(4)] + traces([r[0] for r in result], 0, 1.0)[2:] + [
            result[f][0] for f in (1, 2)
        ]
        high = [u[f][3] for f in range(4)] + traces([r[3] for r in result], 0, -1.0)[2:] + [
            result[f][3] for f in (1, 2)
        ]
        for j in range(7):
            pay_a[pl.ds(4 * j + 2 * z, 2)] = jnp.where(even, high[j], low[j])
            pay_b[pl.ds(4 * j + 2 * z, 2)] = jnp.where(even, low[j], high[j])
    if nz == 2:
        layer = 1 - z_place
        for f in range(4):
            z_pay[0][pl.ds(8 * f, 8)] = state[layer, f].reshape(8, 8, LANES)
        z_pay[0][Z_SLOTS] = jnp.broadcast_to(jnp.where(layer == 0, slots[0], slots[1]), (8, LANES))
    else:
        for direction in range(2):
            layer = 1 - direction
            for f in range(4):
                z_pay[direction][pl.ds(8 * f, 8)] = state[layer, f].reshape(8, 8, LANES)
            z_pay[direction][Z_SLOTS] = jnp.broadcast_to(slots[layer], (8, LANES))


def x_side(side, even, got_a, got_b, block):
    a, b = got_a[pl.ds(block, 2)], got_b[pl.ds(block, 2)]
    return jnp.where(even, b, a) if side == 0 else jnp.where(even, a, b)


def sums_kernel(
    sizes, state, local, got_a, got_b, x_wall, logk, own_slots, *refs
):
    nx, nz = sizes
    count = 1 if nz == 2 else 2
    z_got, (whole, send), z_pay = refs[:count], refs[count : count + 2], refs[count + 2 :]
    z_from = [z_got[0], z_got[-1]]
    x_place, z_place = lax.axis_index("gx"), lax.axis_index("gz")
    even = x_place % 2 == 0
    rows = Rows()
    weights = z_weights(rows)
    corners = {}
    first_sums, second_sums = [], []
    for z in range(2):
        u = load(state, z)
        for f in range(4):
            whole[z, f] = local[z, f]
        sign = -1 if z == 0 else 1
        inside = (z_place > 0) if z == 0 else (z_place < nz - 1)
        outer = [z_from[z][pl.ds(8 * f, 8)].reshape(4, 2, 8, LANES) for f in range(4)]
        terms = z_terms(u, outer, float(sign), weights[sign] * jnp.where(inside, 1.0, 0.0), False)
        for f in range(4):
            whole[z, f] += terms[f]
        for side in range(2):
            sign = 1.0 if side else -1.0
            a = 3 * side
            end = (x_place == nx - 1) if side else (x_place == 0)
            mine = [u[f][a] for f in range(4)]
            theirs = [x_side(side, even, got_a, got_b, 4 * f + 2 * z) for f in range(4)]
            corners[side, z] = theirs
            flag = x_wall[side, z : z + 1, :].astype(jnp.float32)
            inner = traces(mine, 0, -sign)
            image = (1.0 - 2.0 * flag) * (mine[0] + sign * mine[3])
            outer = [
                jnp.where(end, e, o)
                for e, o in zip(inner[:2] + [image], traces(theirs, 0, -sign))
            ]
            terms = face_terms(inner, outer, 0, sign, JUMP, False)
            for f in range(4):
                whole[z, f, a] += terms[f]
        first = sum(whole[z, k] * u[k] for k in range(3))
        second = sum(u[k] * u[k] for k in range(3))
        first_sums.append(jnp.sum(first, axis=(0, 1, 2))[None])
        second_sums.append(jnp.sum(second, axis=(0, 1, 2))[None])
    length = logk.shape[1]
    devices = send.shape[0]
    slots = own_slots[X_SLOTS].astype(jnp.int32)
    total = jnp.zeros((devices, LANES), jnp.float32)
    place = lax.broadcasted_iota(jnp.int32, (LANES, LANES), 0)
    owner = lax.broadcasted_iota(jnp.int32, (devices, LANES), 0)
    for z in range(2):
        slot = slots[z : z + 1, :]
        chosen = jnp.where(owner == slot // length, 1.0, 0.0).astype(jnp.bfloat16)
        position = slot % length
        values = jnp.where(
            place == position + length,
            first_sums[z],
            jnp.where(place == position + 2 * length, second_sums[z], 0.0),
        )
        for _ in range(3):
            piece = values.astype(jnp.bfloat16)
            total += lax.dot_general(
                chosen, piece, (((1,), (1,)), ((), ())), preferred_element_type=jnp.float32
            )
            values = values - piece.astype(jnp.float32)
    send[...] = total
    send[:, 0:length] = jnp.broadcast_to(logk[...], (devices, length))
    for direction in range(count):
        layer = 1 - z_place if nz == 2 else 1 - direction
        for f in range(4):
            z_pay[direction][pl.ds(8 * f, 8)] = whole[layer, f].reshape(8, 8, LANES)
            for side in range(2):
                if nz == 2:
                    value = jnp.where(layer == 0, corners[side, 0][f], corners[side, 1][f])
                else:
                    value = corners[side, layer][f]
                z_pay[direction][pl.ds(W_CORNERS + 8 * side + 2 * f, 2)] = value


def look_up(table, length, slots):
    devices = table.shape[0]
    fold = LANES // length
    table_rows = devices // fold
    chunk = min(8, table_rows)
    lane = lax.broadcasted_iota(jnp.int32, (chunk, LANES), 1)
    in_lane = slots & (LANES - 1)
    in_row = lax.shift_right_logical(slots, 7)

    def step(index, result):
        rows = jnp.zeros((chunk, LANES), jnp.float32)
        for j in range(fold):
            part = table[pl.ds(index * chunk * fold + j, chunk, stride=fold), :]
            rows += pltpu.roll(jnp.where(lane < length, part, 0.0), j * length, 1)
        for i in range(chunk):
            wide = jnp.broadcast_to(rows[i : i + 1, :], (8, LANES))
            taken = jnp.take_along_axis(wide, in_lane, axis=1)
            result = jnp.where(in_row == index * chunk + i, taken, result)
        return result

    result = jnp.zeros((8, LANES), jnp.float32)
    if table_rows == chunk:
        return step(0, result)
    return lax.fori_loop(0, table_rows // chunk, step, result)


def adjoint_kernel(sizes, state, whole, got_a, got_b, own_slots, x_wall, z_wall, received, logk, *refs):
    nx, nz = sizes
    count = 1 if nz == 2 else 2
    z_got, w_got, (adjoint, gradient) = refs[:count], refs[count : 2 * count], refs[2 * count :]
    z_from, w_from = [z_got[0], z_got[-1]], [w_got[0], w_got[-1]]
    x_place, z_place = lax.axis_index("gx"), lax.axis_index("gz")
    even = x_place % 2 == 0
    rows = Rows()
    weights = z_weights(rows)
    derivative = Derivative(rows, derivative_matrix().T)
    length = logk.shape[1]
    held = jnp.exp(-logk[...])
    summed = jnp.sum(received[...], axis=0, keepdims=True)
    first, second = summed[:, length : 2 * length], summed[:, 2 * length : 3 * length]
    gradient[...] = -(SCALE / 64.0) * held * (first + SCALE * held * second)
    slot_a, slot_b = got_a[X_SLOTS], got_b[X_SLOTS]
    row = lax.broadcasted_iota(jnp.int32, (8, LANES), 0)
    slots = own_slots[X_SLOTS]
    slots = jnp.where(row // 2 == 1, pltpu.roll(jnp.where(even, slot_b, slot_a), 2, 0), slots)
    slots = jnp.where(row // 2 == 2, pltpu.roll(jnp.where(even, slot_a, slot_b), 4, 0), slots)
    slots = jnp.where(row == 6, z_from[0][Z_SLOTS], slots)
    slots = jnp.where(row == 7, z_from[1][Z_SLOTS], slots)
    quarter = jnp.exp(-look_up(received, length, slots.astype(jnp.int32)))
    resistance = [quarter[i : i + 1, :] for i in range(8)]
    residual = []
    for z in range(2):
        scaled = SCALE * resistance[z]
        residual.append(
            [whole[z, k] + scaled * state[z, k] for k in range(3)] + [whole[z, 3]]
        )
    for z in range(2):
        w = residual[z]
        jumps = y_terms(w, rows, True)
        sign = 1 if z == 0 else -1
        across = z_terms(w, residual[1 - z], float(sign), weights[sign], True)
        sign = -sign
        end = (z_place == 0) if z == 0 else (z_place == nz - 1)
        scaled = SCALE * resistance[6 + z]
        theirs = [w_from[z][pl.ds(8 * f, 8)].reshape(4, 2, 8, LANES) for f in range(4)]
        for k in range(3):
            field = z_from[z][pl.ds(8 * k, 8)].reshape(4, 2, 8, LANES)
            theirs[k] = theirs[k] + scaled * field
        flag = z_wall[z : z + 1, :].astype(jnp.float32)
        inner = traces(w, 2, -float(sign))
        outer = [
            pltpu.roll(t, 3 if sign > 0 else 5, 2) for t in traces(theirs, 2, float(sign))
        ]
        image = inner[:2] + [(1.0 - 2.0 * flag) * inner[2]]
        outer = [jnp.where(end, i, o) for i, o in zip(image, outer)]
        beyond = face_terms(inner, outer, 2, float(sign), weights[sign], True)
        grads = [derivative.along(k, w[3]) for k in range(3)]
        divergence = sum(derivative.along(k, w[k]) for k in range(3))
        volume = [SCALE * (resistance[z] * w[k] + grads[k]) for k in range(3)]
        volume.append(SCALE * divergence)
        for f in range(4):
            adjoint[z, f] = volume[f] + jumps[f] + across[f] + beyond[f]
        for side in range(2):
            a = 3 * side
            s = 1.0 if side else -1.0
            u_out = [x_side(side, even, got_a, got_b, 4 * f + 2 * z) for f in range(4)]
            trace = [
                x_side(side, even, got_a, got_b, X_TRACES + 4 * j + 2 * z) for j in range(3)
            ]
            normal, tangential = trace[0], trace[1:]
            mine = traces([state[z, f, a] for f in range(4)], 0, s)
            there = traces(u_out, 0, s)
            normal = normal - (2.0 * JUMP) * (mine[2] - there[2])
            tangential = [t - JUMP * (m - o) for t, m, o in zip(tangential, mine[:2], there[:2])]
            t = float(sign)
            weight = weights[sign] * jnp.where(end, 0.0, 1.0)
            corner = [
                w_from[z][pl.ds(W_CORNERS + 8 * side + 2 * f, 2)] for f in range(4)
            ]
            edge = z_terms(u_out, corner, t, weight, False)
            normal = normal + edge[0] + s * edge[3]
            tangential = [tangential[0] + edge[1], tangential[1] + edge[2]]
            scaled = SCALE * resistance[2 + 2 * side + z]
            normal = normal + scaled * u_out[0]
            tangential = [v + scaled * u_out[1 + j] for j, v in enumerate(tangential)]
            inner = traces([w[f][a] for f in range(4)], 0, -s)
            flag = x_wall[side, z : z + 1, :].astype(jnp.float32)
            image = inner[:2] + [(1.0 - 2.0 * flag) * inner[2]]
            last = (x_place == nx - 1) if side else (x_place == 0)
            outer = [jnp.where(last, i, o) for i, o in zip(image, tangential + [normal])]
            terms = face_terms(inner, outer, 0, s, JUMP, True)
            for f in range(4):
                adjoint[z, f, a] += terms[f]


def call(kernel, shapes, operands, flops):
    return pl.pallas_call(
        kernel,
        out_shape=[jax.ShapeDtypeStruct(shape, jnp.float32) for shape in shapes],
        in_specs=[VMEM] * len(operands),
        out_specs=[VMEM] * len(shapes),
        compiler_params=pltpu.CompilerParams(vmem_limit_bytes=32 * 1024 * 1024),
        cost_estimate=pl.CostEstimate(flops=flops, bytes_accessed=800000, transcendentals=0),
    )(*operands)


def both_ways(pairs):
    return pairs + [(second, first) for first, second in pairs]


def along_z(payloads, nz):
    if nz == 2:
        return [lax.ppermute(payloads[0], "gz", [(0, 1), (1, 0)])]
    up = [(i, i + 1) for i in range(nz - 1)]
    down = [(second, first) for first, second in up]
    return [lax.ppermute(payloads[0], "gz", up), lax.ppermute(payloads[1], "gz", down)]


def shards(nx, nz, state, target, coarse_logk, cell_slot, cell_of, wall_flags_xaxis, z_wall):
    sizes = (nx, nz)
    shape = (2, 4, 4, 2, 8, LANES)
    state6 = state.reshape(shape)
    target6 = target.reshape(shape)
    logk = coarse_logk.reshape(1, -1)
    slots2 = cell_slot.reshape(-1, LANES)
    cells2 = cell_of.reshape(2, LANES)
    z_flags = z_wall.reshape(2, LANES)
    count = 1 if nz == 2 else 2
    x_shape, z_shape, w_shape = ((n, 8, LANES) for n in (X_BLOCKS, Z_BLOCKS, W_BLOCKS))
    local, pay_a, pay_b, *z_pay = call(
        functools.partial(local_kernel, sizes),
        [shape, x_shape, x_shape] + [z_shape] * count,
        [state6, target6, cells2, slots2, z_flags],
        2000000,
    )
    pairs_b = both_ways([(i, i + 1) for i in range(1, nx - 1, 2)])
    pairs_a = both_ways([(i, i + 1) for i in range(0, nx - 1, 2)])
    got_b = lax.ppermute(pay_b, "gx", pairs_b)
    got_a = lax.ppermute(pay_a, "gx", pairs_a)
    z_got = along_z(z_pay, nz)
    whole, send, *w_pay = call(
        functools.partial(sums_kernel, sizes),
        [shape, (nx * nz, LANES)] + [w_shape] * count,
        [state6, local, got_a, got_b, wall_flags_xaxis, logk, pay_a] + z_got,
        2000000,
    )
    w_got = along_z(w_pay, nz)
    received = lax.all_to_all(send, ("gx", "gz"), 0, 0, tiled=True)
    adjoint, gradient = call(
        functools.partial(adjoint_kernel, sizes),
        [shape, logk.shape],
        [state6, whole, got_a, got_b, pay_a, wall_flags_xaxis, z_flags, received, logk]
        + z_got
        + w_got,
        2000000,
    )
    return adjoint.reshape(state.shape), gradient.reshape(-1)


def solution(mesh):
    placed = (
        P("gx", "gz", None, None, None),
        P("gx", "gz", None, None, None),
        P(("gx", "gz")),
        P(),
        P("gx", "gz", None),
        P(None, "gz", None),
        P(None, "gx", None),
    )
    return jax.shard_map(
        functools.partial(shards, mesh.shape["gx"], mesh.shape["gz"]),
        mesh=mesh,
        in_specs=placed,
        out_specs=(P("gx", "gz", None, None, None), P(("gx", "gz"))),
        check_vma=False,
    )
```

```python
import functools
import math

import jax
import jax.numpy as jnp
import numpy as np
from jax import lax
from jax.experimental import pallas as pl
from jax.experimental.pallas import tpu as pltpu
from jax.sharding import PartitionSpec as P

SCALE = 0.25
JUMP = 0.75
LANES = 128
VMEM = pl.BlockSpec(memory_space=pltpu.VMEM)
HBM = pl.BlockSpec(memory_space=pltpu.HBM)

X_FIELDS, X_TRACES, X_SLOTS, X_BLOCKS = 0, 16, 28, 29
Z_SLOTS, Z_BLOCKS = 32, 33
W_CORNERS, W_BLOCKS = 32, 48
X_WALL, Z_WALL, LOGK = 0, 4, 6


def derivative_matrix():
    points = np.array([-1.0, -math.sqrt(0.2), math.sqrt(0.2), 1.0])
    products = np.array(
        [
            np.prod([points[first] - points[other] for other in range(4) if other != first])
            for first in range(4)
        ]
    )
    matrix = np.zeros((4, 4))
    for first in range(4):
        for second in range(4):
            if first != second:
                matrix[first, second] = (
                    products[first] / products[second] / (points[first] - points[second])
                )
        matrix[first, first] = sum(
            (1.0 / (points[first] - points[other]) for other in range(4) if other != first)
        )
    return matrix


class Rows:
    def __init__(self):
        row = lax.broadcasted_iota(jnp.int32, (8, LANES), 0)
        self.upper = row >= 4
        self.c = row & 3

    def halves(self, low, high):
        return jnp.where(self.upper, jnp.float32(high), jnp.float32(low))

    def by_c(self, values):
        result = jnp.full((8, LANES), values[0], jnp.float32)
        for c in range(1, 4):
            result = jnp.where(self.c == c, jnp.float32(values[c]), result)
        return result


class Derivative:
    def __init__(self, rows, matrix):
        self.matrix = matrix
        self.same = [
            [rows.halves(matrix[2 * h, 2 * g], matrix[2 * h + 1, 2 * g + 1]) for g in range(2)]
            for h in range(2)
        ]
        self.cross = [
            [rows.halves(matrix[2 * h, 2 * g + 1], matrix[2 * h + 1, 2 * g]) for g in range(2)]
            for h in range(2)
        ]
        self.shift = {
            delta: rows.by_c(
                [matrix[c, c + delta] if 0 <= c + delta < 4 else 0.0 for c in range(4)]
            )
            for delta in range(-3, 4)
        }

    def along(self, axis, u):
        if axis == 0:
            return jnp.stack(
                [sum(float(self.matrix[a, j]) * u[j] for j in range(4)) for a in range(4)]
            )
        if axis == 1:
            swapped = pltpu.roll(u, 4, 2)
            return jnp.stack(
                [
                    sum(self.same[h][g] * u[:, g] + self.cross[h][g] * swapped[:, g] for g in range(2))
                    for h in range(2)
                ],
                axis=1,
            )
        return sum(
            coefficient * (u if delta == 0 else pltpu.roll(u, -delta % 8, 2))
            for delta, coefficient in self.shift.items()
        )


def traces(fields, axis, sign):
    others = [fields[f] for f in range(3) if f != axis]
    return others + [fields[axis] + sign * fields[3]]


def face_terms(inner, outer, axis, sign, weight, adjoint):
    tangential = [weight * (i - o) for i, o in zip(inner[:2], outer[:2])]
    normal = weight * (inner[2] - outer[2])
    if adjoint:
        pressure = (-sign) * (weight * (inner[2] + outer[2]))
    else:
        pressure = (-sign) * normal
    terms = tangential[:]
    terms.insert(axis, normal)
    return terms + [pressure]


def y_terms(fields, rows, adjoint):
    high_weight = rows.halves(0.0, JUMP)
    low_weight = rows.halves(JUMP, 0.0)
    first = [field[:, 0] for field in fields]
    second = [field[:, 1] for field in fields]
    moved = lambda value, step: pltpu.roll(pltpu.roll(value, 4, 1), step, 2)
    flip = 1.0 if adjoint else -1.0
    high_out = [moved(t, LANES - 1) for t in traces(first, 1, flip)]
    high = face_terms(traces(second, 1, -1.0), high_out, 1, 1.0, high_weight, adjoint)
    low_out = [moved(t, 1) for t in traces(second, 1, -flip)]
    low = face_terms(traces(first, 1, 1.0), low_out, 1, -1.0, low_weight, adjoint)
    return [jnp.stack([l, h], axis=1) for l, h in zip(low, high)]


def z_terms(inner, outer_fields, sign, weight, adjoint):
    flip = sign if adjoint else -sign
    outer = [pltpu.roll(t, 3 if sign > 0 else 5, t.ndim - 2) for t in traces(outer_fields, 2, flip)]
    return face_terms(traces(inner, 2, -sign), outer, 2, sign, weight, adjoint)


def wall_terms(fields, axis, sign, weight, flag, adjoint):
    inner = traces(fields, axis, -sign)
    image = inner[2] if adjoint else fields[axis] + sign * fields[3]
    outer = inner[:2] + [(1.0 - 2.0 * flag) * image]
    return face_terms(inner, outer, axis, sign, weight, adjoint)


def z_weights(rows):
    return {-1: jnp.where(rows.c == 0, JUMP, 0.0), 1: jnp.where(rows.c == 3, JUMP, 0.0)}


def load(ref, z):
    return [ref[z, f] for f in range(4)]


def local_kernel(sizes, *refs):
    nx, nz = sizes
    count = 1 if nz == 2 else 2
    sources, refs = refs[:7], refs[7:]
    (state, small, local, pay_a, pay_b), refs = refs[:5], refs[5:]
    z_pay, places, arrived = refs[:count], refs[count:-1], refs[-1]
    target, cell_of, cell_slot, x_wall, z_wall, logk = places
    copies = [
        pltpu.make_async_copy(source, place, arrived.at[i])
        for i, (source, place) in enumerate(zip(sources, (state,) + tuple(places)))
    ]
    for copy in copies:
        copy.start()
    for copy in copies:
        copy.wait()
    x_place, z_place = lax.axis_index("gx"), lax.axis_index("gz")
    rows = Rows()
    derivative = Derivative(rows, derivative_matrix())
    weights = z_weights(rows)
    cell_rows = cell_slot.shape[0]
    slots = []
    for z in range(2):
        row_of = lax.shift_right_logical(cell_of[z : z + 1, :], 7)
        slot = jnp.zeros((1, LANES), jnp.int32)
        for step in (-1, 0, 1):
            row = (x_place // 4 + step) * nz + z_place
            row = jnp.clip(row, 0, cell_rows - 1)
            slot = jnp.where(row_of == row, cell_slot[pl.ds(row, 1), :], slot)
        slots.append(slot.astype(jnp.float32))
    row = lax.broadcasted_iota(jnp.int32, (8, LANES), 0)
    slot_block = jnp.where(row == 0, slots[0], jnp.where(row == 1, slots[1], 0.0))
    even = x_place % 2 == 0
    pay_a[X_SLOTS] = slot_block
    pay_b[X_SLOTS] = slot_block
    small[0] = slot_block
    for side in range(2):
        small[1, X_WALL + 2 * side : X_WALL + 2 * side + 2, :] = x_wall[side].astype(jnp.float32)
    small[1, Z_WALL : Z_WALL + 2, :] = z_wall[...].astype(jnp.float32)
    small[1, LOGK : LOGK + 1, 0 : logk.shape[1]] = logk[...]
    for z in range(2):
        u = load(state, z)
        other = load(state, 1 - z)
        grads = [derivative.along(k, u[3]) for k in range(3)]
        divergence = sum(derivative.along(k, u[k]) for k in range(3))
        jumps = y_terms(u, rows, False)
        sign = 1.0 if z == 0 else -1.0
        across = z_terms(u, other, sign, weights[int(sign)], False)
        end = (z_place == 0) if z == 0 else (z_place == nz - 1)
        weight = weights[-int(sign)] * jnp.where(end, 1.0, 0.0)
        flag = small[1, Z_WALL + z : Z_WALL + z + 1, :]
        wall = wall_terms(u, 2, -sign, weight, flag, False)
        result = [
            SCALE * v + j + a + w - target[z, f]
            for f, (v, j, a, w) in enumerate(zip(grads + [divergence], jumps, across, wall))
        ]
        for f in range(4):
            local[z, f] = result[f]
        low = [u[f][0] for f in range(4)] + traces([r[0] for r in result], 0, 1.0)[2:] + [
            result[f][0] for f in (1, 2)
        ]
        high = [u[f][3] for f in range(4)] + traces([r[3] for r in result], 0, -1.0)[2:] + [
            result[f][3] for f in (1, 2)
        ]
        for j in range(7):
            pay_a[pl.ds(4 * j + 2 * z, 2)] = jnp.where(even, high[j], low[j])
            pay_b[pl.ds(4 * j + 2 * z, 2)] = jnp.where(even, low[j], high[j])
    if nz == 2:
        layer = 1 - z_place
        for f in range(4):
            z_pay[0][pl.ds(8 * f, 8)] = state[layer, f].reshape(8, 8, LANES)
        z_pay[0][Z_SLOTS] = jnp.broadcast_to(jnp.where(layer == 0, slots[0], slots[1]), (8, LANES))
    else:
        for direction in range(2):
            layer = 1 - direction
            for f in range(4):
                z_pay[direction][pl.ds(8 * f, 8)] = state[layer, f].reshape(8, 8, LANES)
            z_pay[direction][Z_SLOTS] = jnp.broadcast_to(slots[layer], (8, LANES))


def x_side(side, even, got_a, got_b, block):
    a, b = got_a[pl.ds(block, 2)], got_b[pl.ds(block, 2)]
    return jnp.where(even, b, a) if side == 0 else jnp.where(even, a, b)


def sums_kernel(sizes, length, state, small, local, got_a, got_b, *refs):
    nx, nz = sizes
    count = 1 if nz == 2 else 2
    z_got, (whole, send), z_pay = refs[:count], refs[count : count + 2], refs[count + 2 :]
    z_from = [z_got[0], z_got[-1]]
    x_place, z_place = lax.axis_index("gx"), lax.axis_index("gz")
    even = x_place % 2 == 0
    rows = Rows()
    weights = z_weights(rows)
    corners = {}
    first_sums, second_sums = [], []
    for z in range(2):
        u = load(state, z)
        for f in range(4):
            whole[z, f] = local[z, f]
        sign = -1 if z == 0 else 1
        inside = (z_place > 0) if z == 0 else (z_place < nz - 1)
        outer = [z_from[z][pl.ds(8 * f, 8)].reshape(4, 2, 8, LANES) for f in range(4)]
        terms = z_terms(u, outer, float(sign), weights[sign] * jnp.where(inside, 1.0, 0.0), False)
        for f in range(4):
            whole[z, f] += terms[f]
        for side in range(2):
            sign = 1.0 if side else -1.0
            a = 3 * side
            end = (x_place == nx - 1) if side else (x_place == 0)
            mine = [u[f][a] for f in range(4)]
            theirs = [x_side(side, even, got_a, got_b, 4 * f + 2 * z) for f in range(4)]
            corners[side, z] = theirs
            flag = small[1, X_WALL + 2 * side + z : X_WALL + 2 * side + z + 1, :]
            inner = traces(mine, 0, -sign)
            image = (1.0 - 2.0 * flag) * (mine[0] + sign * mine[3])
            outer = [
                jnp.where(end, e, o)
                for e, o in zip(inner[:2] + [image], traces(theirs, 0, -sign))
            ]
            terms = face_terms(inner, outer, 0, sign, JUMP, False)
            for f in range(4):
                whole[z, f, a] += terms[f]
        first = sum(whole[z, k] * u[k] for k in range(3))
        second = sum(u[k] * u[k] for k in range(3))
        first_sums.append(jnp.sum(first, axis=(0, 1, 2))[None])
        second_sums.append(jnp.sum(second, axis=(0, 1, 2))[None])
    devices = send.shape[0]
    slots = small[0].astype(jnp.int32)
    total = jnp.zeros((devices, LANES), jnp.float32)
    place = lax.broadcasted_iota(jnp.int32, (LANES, LANES), 0)
    owner = lax.broadcasted_iota(jnp.int32, (devices, LANES), 0)
    for z in range(2):
        slot = slots[z : z + 1, :]
        chosen = jnp.where(owner == slot // length, 1.0, 0.0).astype(jnp.bfloat16)
        position = slot % length
        values = jnp.where(
            place == position + length,
            first_sums[z],
            jnp.where(place == position + 2 * length, second_sums[z], 0.0),
        )
        for _ in range(3):
            piece = values.astype(jnp.bfloat16)
            total += lax.dot_general(
                chosen, piece, (((1,), (1,)), ((), ())), preferred_element_type=jnp.float32
            )
            values = values - piece.astype(jnp.float32)
    send[...] = total
    logk = small[1, LOGK : LOGK + 1, 0:length]
    send[:, 0:length] = jnp.broadcast_to(logk, (devices, length))
    for direction in range(count):
        layer = 1 - z_place if nz == 2 else 1 - direction
        for f in range(4):
            z_pay[direction][pl.ds(8 * f, 8)] = whole[layer, f].reshape(8, 8, LANES)
            for side in range(2):
                if nz == 2:
                    value = jnp.where(layer == 0, corners[side, 0][f], corners[side, 1][f])
                else:
                    value = corners[side, layer][f]
                z_pay[direction][pl.ds(W_CORNERS + 8 * side + 2 * f, 2)] = value


def look_up(table, length, slots):
    devices = table.shape[0]
    fold = LANES // length
    table_rows = devices // fold
    chunk = min(8, table_rows)
    lane = lax.broadcasted_iota(jnp.int32, (chunk, LANES), 1)
    in_lane = slots & (LANES - 1)
    in_row = lax.shift_right_logical(slots, 7)

    def step(index, result):
        rows = jnp.zeros((chunk, LANES), jnp.float32)
        for j in range(fold):
            part = table[pl.ds(index * chunk * fold + j, chunk, stride=fold), :]
            rows += pltpu.roll(jnp.where(lane < length, part, 0.0), j * length, 1)
        for i in range(chunk):
            wide = jnp.broadcast_to(rows[i : i + 1, :], (8, LANES))
            taken = jnp.take_along_axis(wide, in_lane, axis=1)
            result = jnp.where(in_row == index * chunk + i, taken, result)
        return result

    result = jnp.zeros((8, LANES), jnp.float32)
    if table_rows == chunk:
        return step(0, result)
    return lax.fori_loop(0, table_rows // chunk, step, result)


def adjoint_kernel(sizes, length, state, small, whole, got_a, got_b, received, *refs):
    nx, nz = sizes
    count = 1 if nz == 2 else 2
    z_got, w_got, refs = refs[:count], refs[count : 2 * count], refs[2 * count :]
    adjoint_out, gradient_out, adjoint, gradient, done = refs
    z_from, w_from = [z_got[0], z_got[-1]], [w_got[0], w_got[-1]]
    x_place, z_place = lax.axis_index("gx"), lax.axis_index("gz")
    even = x_place % 2 == 0
    rows = Rows()
    weights = z_weights(rows)
    derivative = Derivative(rows, derivative_matrix().T)
    held = jnp.exp(-small[1, LOGK : LOGK + 1, 0:length])
    summed = jnp.sum(received[...], axis=0, keepdims=True)
    first, second = summed[:, length : 2 * length], summed[:, 2 * length : 3 * length]
    gradient[...] = -(SCALE / 64.0) * held * (first + SCALE * held * second)
    copies = [pltpu.make_async_copy(gradient, gradient_out, done.at[2])]
    copies[0].start()
    slot_a, slot_b = got_a[X_SLOTS], got_b[X_SLOTS]
    row = lax.broadcasted_iota(jnp.int32, (8, LANES), 0)
    slots = small[0]
    slots = jnp.where(row // 2 == 1, pltpu.roll(jnp.where(even, slot_b, slot_a), 2, 0), slots)
    slots = jnp.where(row // 2 == 2, pltpu.roll(jnp.where(even, slot_a, slot_b), 4, 0), slots)
    slots = jnp.where(row == 6, z_from[0][Z_SLOTS], slots)
    slots = jnp.where(row == 7, z_from[1][Z_SLOTS], slots)
    quarter = jnp.exp(-look_up(received, length, slots.astype(jnp.int32)))
    resistance = [quarter[i : i + 1, :] for i in range(8)]
    residual = []
    for z in range(2):
        scaled = SCALE * resistance[z]
        residual.append(
            [whole[z, k] + scaled * state[z, k] for k in range(3)] + [whole[z, 3]]
        )
    for z in range(2):
        w = residual[z]
        jumps = y_terms(w, rows, True)
        sign = 1 if z == 0 else -1
        across = z_terms(w, residual[1 - z], float(sign), weights[sign], True)
        sign = -sign
        end = (z_place == 0) if z == 0 else (z_place == nz - 1)
        scaled = SCALE * resistance[6 + z]
        theirs = [w_from[z][pl.ds(8 * f, 8)].reshape(4, 2, 8, LANES) for f in range(4)]
        for k in range(3):
            field = z_from[z][pl.ds(8 * k, 8)].reshape(4, 2, 8, LANES)
            theirs[k] = theirs[k] + scaled * field
        flag = small[1, Z_WALL + z : Z_WALL + z + 1, :]
        inner = traces(w, 2, -float(sign))
        outer = [
            pltpu.roll(t, 3 if sign > 0 else 5, 2) for t in traces(theirs, 2, float(sign))
        ]
        image = inner[:2] + [(1.0 - 2.0 * flag) * inner[2]]
        outer = [jnp.where(end, i, o) for i, o in zip(image, outer)]
        beyond = face_terms(inner, outer, 2, float(sign), weights[sign], True)
        grads = [derivative.along(k, w[3]) for k in range(3)]
        divergence = sum(derivative.along(k, w[k]) for k in range(3))
        volume = [SCALE * (resistance[z] * w[k] + grads[k]) for k in range(3)]
        volume.append(SCALE * divergence)
        for f in range(4):
            adjoint[z, f] = volume[f] + jumps[f] + across[f] + beyond[f]
        for side in range(2):
            a = 3 * side
            s = 1.0 if side else -1.0
            u_out = [x_side(side, even, got_a, got_b, 4 * f + 2 * z) for f in range(4)]
            trace = [
                x_side(side, even, got_a, got_b, X_TRACES + 4 * j + 2 * z) for j in range(3)
            ]
            normal, tangential = trace[0], trace[1:]
            mine = traces([state[z, f, a] for f in range(4)], 0, s)
            there = traces(u_out, 0, s)
            normal = normal - (2.0 * JUMP) * (mine[2] - there[2])
            tangential = [t - JUMP * (m - o) for t, m, o in zip(tangential, mine[:2], there[:2])]
            t = float(sign)
            weight = weights[sign] * jnp.where(end, 0.0, 1.0)
            corner = [
                w_from[z][pl.ds(W_CORNERS + 8 * side + 2 * f, 2)] for f in range(4)
            ]
            edge = z_terms(u_out, corner, t, weight, False)
            normal = normal + edge[0] + s * edge[3]
            tangential = [tangential[0] + edge[1], tangential[1] + edge[2]]
            scaled = SCALE * resistance[2 + 2 * side + z]
            normal = normal + scaled * u_out[0]
            tangential = [v + scaled * u_out[1 + j] for j, v in enumerate(tangential)]
            inner = traces([w[f][a] for f in range(4)], 0, -s)
            flag = small[1, X_WALL + 2 * side + z : X_WALL + 2 * side + z + 1, :]
            image = inner[:2] + [(1.0 - 2.0 * flag) * inner[2]]
            last = (x_place == nx - 1) if side else (x_place == 0)
            outer = [jnp.where(last, i, o) for i, o in zip(image, tangential + [normal])]
            terms = face_terms(inner, outer, 0, s, JUMP, True)
            for f in range(4):
                adjoint[z, f, a] += terms[f]
        copies.append(pltpu.make_async_copy(adjoint.at[z], adjoint_out.at[z], done.at[z]))
        copies[-1].start()
    for copy in copies:
        copy.wait()


def call(kernel, operands, in_spec, shapes, out_spec, scratch, room):
    return pl.pallas_call(
        kernel,
        out_shape=[jax.ShapeDtypeStruct(shape, jnp.float32) for shape in shapes],
        in_specs=[in_spec] * len(operands),
        out_specs=[out_spec] * len(shapes),
        scratch_shapes=scratch,
        compiler_params=pltpu.CompilerParams(vmem_limit_bytes=room * 1024),
        cost_estimate=pl.CostEstimate(flops=2000000, bytes_accessed=800000, transcendentals=0),
    )(*operands)


def both_ways(pairs):
    return pairs + [(second, first) for first, second in pairs]


def along_z(payloads, nz):
    if nz == 2:
        return [lax.ppermute(payloads[0], "gz", [(0, 1), (1, 0)])]
    up = [(i, i + 1) for i in range(nz - 1)]
    down = [(second, first) for first, second in up]
    return [lax.ppermute(payloads[0], "gz", up), lax.ppermute(payloads[1], "gz", down)]


def shards(nx, nz, state, target, coarse_logk, cell_slot, cell_of, wall_flags_xaxis, z_wall):
    sizes = (nx, nz)
    shape = (2, 4, 4, 2, 8, LANES)
    length = coarse_logk.shape[0]
    inputs = [
        state.reshape(shape),
        target.reshape(shape),
        cell_of.reshape(2, LANES),
        cell_slot.reshape(-1, LANES),
        wall_flags_xaxis,
        z_wall.reshape(2, LANES),
        coarse_logk.reshape(1, -1),
    ]
    count = 1 if nz == 2 else 2
    x_shape, z_shape, w_shape = ((n, 8, LANES) for n in (X_BLOCKS, Z_BLOCKS, W_BLOCKS))
    held, small, local, pay_a, pay_b, *z_pay = call(
        functools.partial(local_kernel, sizes),
        inputs,
        HBM,
        [shape, (2, 8, LANES), shape, x_shape, x_shape] + [z_shape] * count,
        VMEM,
        [pltpu.VMEM(i.shape, i.dtype) for i in inputs[1:]] + [pltpu.SemaphoreType.DMA((7,))],
        54200,
    )
    pairs_b = both_ways([(i, i + 1) for i in range(1, nx - 1, 2)])
    pairs_a = both_ways([(i, i + 1) for i in range(0, nx - 1, 2)])
    got_a = lax.ppermute(pay_a, "gx", pairs_a)
    got_b = lax.ppermute(pay_b, "gx", pairs_b)
    z_got = along_z(z_pay, nz)
    whole, send, *w_pay = call(
        functools.partial(sums_kernel, sizes, length),
        [held, small, local, got_a, got_b] + z_got,
        VMEM,
        [shape, (nx * nz, LANES)] + [w_shape] * count,
        VMEM,
        [],
        16 * 1024,
    )
    w_got = along_z(w_pay, nz)
    received = lax.all_to_all(send, ("gx", "gz"), 0, 0, tiled=True)
    adjoint, gradient = call(
        functools.partial(adjoint_kernel, sizes, length),
        [held, small, whole, got_a, got_b, received] + z_got + w_got,
        VMEM,
        [shape, (1, length)],
        HBM,
        [
            pltpu.VMEM(shape, jnp.float32),
            pltpu.VMEM((1, length), jnp.float32),
            pltpu.SemaphoreType.DMA((3,)),
        ],
        16 * 1024,
    )
    return adjoint.reshape(state.shape), gradient.reshape(-1)


def solution(mesh):
    placed = (
        P("gx", "gz", None, None, None),
        P("gx", "gz", None, None, None),
        P(("gx", "gz")),
        P(),
        P("gx", "gz", None),
        P(None, "gz", None),
        P(None, "gx", None),
    )
    return jax.shard_map(
        functools.partial(shards, mesh.shape["gx"], mesh.shape["gz"]),
        mesh=mesh,
        in_specs=placed,
        out_specs=(P("gx", "gz", None, None, None), P(("gx", "gz"))),
        check_vma=False,
    )
```

```python
import functools
import math

import jax
import jax.numpy as jnp
import numpy as np
from jax import lax
from jax.experimental import pallas as pl
from jax.experimental.pallas import tpu as pltpu
from jax.sharding import PartitionSpec as P

SCALE = 0.25
JUMP = 0.75
LANES = 128
VMEM = pl.BlockSpec(memory_space=pltpu.VMEM)
HBM = pl.BlockSpec(memory_space=pltpu.HBM)

X_FIELDS, X_TRACES, X_SLOTS, X_BLOCKS = 0, 16, 28, 29
Z_SLOTS, Z_BLOCKS = 8, 9
W_CORNERS, W_BLOCKS = 8, 12
X_WALL, Z_WALL, LOGK = 0, 4, 6


def derivative_matrix():
    points = np.array([-1.0, -math.sqrt(0.2), math.sqrt(0.2), 1.0])
    products = np.array(
        [
            np.prod([points[first] - points[other] for other in range(4) if other != first])
            for first in range(4)
        ]
    )
    matrix = np.zeros((4, 4))
    for first in range(4):
        for second in range(4):
            if first != second:
                matrix[first, second] = (
                    products[first] / products[second] / (points[first] - points[second])
                )
        matrix[first, first] = sum(
            (1.0 / (points[first] - points[other]) for other in range(4) if other != first)
        )
    return matrix


class Rows:
    def __init__(self):
        row = lax.broadcasted_iota(jnp.int32, (8, LANES), 0)
        self.upper = row >= 4
        self.c = row & 3

    def halves(self, low, high):
        return jnp.where(self.upper, jnp.float32(high), jnp.float32(low))

    def by_c(self, values):
        result = jnp.full((8, LANES), values[0], jnp.float32)
        for c in range(1, 4):
            result = jnp.where(self.c == c, jnp.float32(values[c]), result)
        return result


class Derivative:
    def __init__(self, rows, matrix):
        self.matrix = matrix
        self.same = [
            [rows.halves(matrix[2 * h, 2 * g], matrix[2 * h + 1, 2 * g + 1]) for g in range(2)]
            for h in range(2)
        ]
        self.cross = [
            [rows.halves(matrix[2 * h, 2 * g + 1], matrix[2 * h + 1, 2 * g]) for g in range(2)]
            for h in range(2)
        ]
        self.shift = {
            delta: rows.by_c(
                [matrix[c, c + delta] if 0 <= c + delta < 4 else 0.0 for c in range(4)]
            )
            for delta in range(-3, 4)
        }

    def across(self, a, u):
        return sum(float(self.matrix[a, j]) * u[j : j + 1] for j in range(4))

    def along(self, axis, u):
        if axis == 0:
            return jnp.concatenate([self.across(a, u) for a in range(4)])
        if axis == 1:
            swapped = pltpu.roll(u, 4, 2)
            return jnp.stack(
                [
                    sum(self.same[h][g] * u[:, g] + self.cross[h][g] * swapped[:, g] for g in range(2))
                    for h in range(2)
                ],
                axis=1,
            )
        return sum(
            coefficient * (u if delta == 0 else pltpu.roll(u, -delta % 8, 2))
            for delta, coefficient in self.shift.items()
        )


def traces(fields, axis, sign):
    others = [fields[f] for f in range(3) if f != axis]
    return others + [fields[axis] + sign * fields[3]]


def face_terms(inner, outer, axis, sign, weight, adjoint):
    tangential = [weight * (i - o) for i, o in zip(inner[:2], outer[:2])]
    normal = weight * (inner[2] - outer[2])
    if adjoint:
        pressure = (-sign) * (weight * (inner[2] + outer[2]))
    else:
        pressure = (-sign) * normal
    terms = tangential[:]
    terms.insert(axis, normal)
    return terms + [pressure]


def y_terms(fields, rows, adjoint):
    high_weight = rows.halves(0.0, JUMP)
    low_weight = rows.halves(JUMP, 0.0)
    first = [field[:, 0] for field in fields]
    second = [field[:, 1] for field in fields]
    moved = lambda value, step: pltpu.roll(pltpu.roll(value, 4, 1), step, 2)
    flip = 1.0 if adjoint else -1.0
    high_out = [moved(t, LANES - 1) for t in traces(first, 1, flip)]
    high = face_terms(traces(second, 1, -1.0), high_out, 1, 1.0, high_weight, adjoint)
    low_out = [moved(t, 1) for t in traces(second, 1, -flip)]
    low = face_terms(traces(first, 1, 1.0), low_out, 1, -1.0, low_weight, adjoint)
    return [jnp.stack([l, h], axis=1) for l, h in zip(low, high)]


def z_terms(inner, outer_fields, sign, weight, adjoint):
    flip = sign if adjoint else -sign
    outer = [pltpu.roll(t, 3 if sign > 0 else 5, t.ndim - 2) for t in traces(outer_fields, 2, flip)]
    return face_terms(traces(inner, 2, -sign), outer, 2, sign, weight, adjoint)


def packed_face(rows, fields, sign):
    c = 3 if sign > 0 else 0
    axis = fields[0].ndim - 2
    result = None
    for f, field in enumerate(fields):
        moved = field if f == c else pltpu.roll(field, (f - c) % 8, axis)
        result = moved if result is None else jnp.where(rows.c == f, moved, result)
    return result


def unpacked_face(packed, sign):
    c = 3 if sign > 0 else 0
    axis = packed.ndim - 2
    return [packed if f == c else pltpu.roll(packed, (c - f) % 8, axis) for f in range(4)]


def met_terms(inner, packed, sign, weight):
    outer = traces(unpacked_face(packed, sign), 2, -sign)
    return face_terms(traces(inner, 2, -sign), outer, 2, sign, weight, False)


def wall_terms(fields, axis, sign, weight, flag, adjoint):
    inner = traces(fields, axis, -sign)
    image = inner[2] if adjoint else fields[axis] + sign * fields[3]
    outer = inner[:2] + [(1.0 - 2.0 * flag) * image]
    return face_terms(inner, outer, axis, sign, weight, adjoint)


def z_weights(rows):
    return {-1: jnp.where(rows.c == 0, JUMP, 0.0), 1: jnp.where(rows.c == 3, JUMP, 0.0)}


def load(ref, z):
    return [ref[z, f] for f in range(4)]


def faces_kernel(state_in, target_in, state, pay_a, pay_b, target, arrived):
    copies = [pltpu.make_async_copy(state_in, state, arrived.at[0])]
    for side in range(2):
        copies.append(
            pltpu.make_async_copy(
                target_in.at[:, :, 3 * side], target.at[side], arrived.at[1 + side]
            )
        )
    for copy in copies:
        copy.start()
    even = lax.axis_index("gx") % 2 == 0
    rows = Rows()
    derivative = Derivative(rows, derivative_matrix())
    weights = z_weights(rows)
    for copy in copies:
        copy.wait()
    for z in range(2):
        sign = 1 if z == 0 else -1
        values = []
        for side in range(2):
            a = 3 * side
            u = [state[z, f, a : a + 1] for f in range(4)]
            other = [state[1 - z, f, a : a + 1] for f in range(4)]
            grads = [derivative.across(a, state[z, 3])]
            grads += [derivative.along(k, u[3]) for k in (1, 2)]
            divergence = derivative.across(a, state[z, 0])
            divergence += derivative.along(1, u[1]) + derivative.along(2, u[2])
            jumps = y_terms(u, rows, False)
            terms = z_terms(u, other, float(sign), weights[sign], False)
            result = [
                (SCALE * v + j + t)[0] - target[side, z, f]
                for f, (v, j, t) in enumerate(zip(grads + [divergence], jumps, terms))
            ]
            normal = result[0] - result[3] if side else result[0] + result[3]
            values.append([v[0] for v in u] + [normal, result[1], result[2]])
        low, high = values
        for j in range(7):
            pay_a[pl.ds(4 * j + 2 * z, 2)] = jnp.where(even, high[j], low[j])
            pay_b[pl.ds(4 * j + 2 * z, 2)] = jnp.where(even, low[j], high[j])


def wall_rows(sizes, rows, weights, z, flags):
    z_place = lax.axis_index("gz")
    end = (z_place == 0) if z == 0 else (z_place == sizes[1] - 1)
    weight = weights[-1 if z == 0 else 1] * jnp.where(end, 1.0, 0.0)
    return weight, flags[z : z + 1, :].astype(jnp.float32)


def edges_kernel(sizes, first_a, first_b, cell_of, cell_slot, z_wall, pay_a, pay_b, positions):
    nx, nz = sizes
    x_place, z_place = lax.axis_index("gx"), lax.axis_index("gz")
    rows = Rows()
    weights = z_weights(rows)
    cell_rows = cell_slot.shape[0]
    slots = []
    for z in range(2):
        row_of = lax.shift_right_logical(cell_of[z : z + 1, :], 7)
        slot = jnp.zeros((1, LANES), jnp.int32)
        for step in (-1, 0, 1):
            row = (x_place // 4 + step) * nz + z_place
            row = jnp.clip(row, 0, cell_rows - 1)
            slot = jnp.where(row_of == row, cell_slot[pl.ds(row, 1), :], slot)
        slots.append(slot.astype(jnp.float32))
    row = lax.broadcasted_iota(jnp.int32, (8, LANES), 0)
    block = jnp.where(row == 0, slots[0], jnp.where(row == 1, slots[1], 0.0))
    positions[...] = block
    flip = jnp.where(x_place % 2 == 0, -1.0, 1.0)
    for first, pay, factor in ((first_a, pay_a, flip), (first_b, pay_b, -flip)):
        pay[X_SLOTS] = block
        for z in range(2):
            weight, flag = wall_rows(sizes, rows, weights, z, z_wall)
            fields = [first[pl.ds(4 * f + 2 * z, 2)] for f in range(4)]
            terms = wall_terms(fields, 2, -1.0 if z == 0 else 1.0, weight, flag, False)
            normal, tangential = X_TRACES + 2 * z, X_TRACES + 8 + 2 * z
            pay[pl.ds(normal, 2)] = first[pl.ds(normal, 2)] + factor * terms[3]
            pay[pl.ds(tangential, 2)] = first[pl.ds(tangential, 2)] + terms[2]


def local_kernel(sizes, state, positions, target, x_wall, z_wall, logk, small, local, *z_pay):
    nx, nz = sizes
    z_place = lax.axis_index("gz")
    rows = Rows()
    derivative = Derivative(rows, derivative_matrix())
    weights = z_weights(rows)
    small[0] = positions[...]
    for side in range(2):
        small[1, X_WALL + 2 * side : X_WALL + 2 * side + 2, :] = x_wall[side].astype(jnp.float32)
    small[1, Z_WALL : Z_WALL + 2, :] = z_wall[...].astype(jnp.float32)
    small[1, LOGK : LOGK + 1, 0 : logk.shape[1]] = logk[...]
    for z in range(2):
        u = load(state, z)
        other = load(state, 1 - z)
        grads = [derivative.along(k, u[3]) for k in range(3)]
        divergence = sum(derivative.along(k, u[k]) for k in range(3))
        jumps = y_terms(u, rows, False)
        sign = 1 if z == 0 else -1
        across = z_terms(u, other, float(sign), weights[sign], False)
        weight, flag = wall_rows(sizes, rows, weights, z, z_wall)
        wall = wall_terms(u, 2, -float(sign), weight, flag, False)
        for f, (v, j, a, w) in enumerate(zip(grads + [divergence], jumps, across, wall)):
            local[z, f] = SCALE * v + j + a + w - target[z, f]
    faces = [packed_face(rows, load(state, z), 2 * z - 1) for z in range(2)]
    for direction in range(len(z_pay)):
        upper = z_place == 0 if nz == 2 else direction == 0
        z_pay[direction][0:8] = jnp.where(upper, faces[1], faces[0]).reshape(8, 8, LANES)
        slot = jnp.where(upper, positions[1:2, :], positions[0:1, :])
        z_pay[direction][Z_SLOTS] = jnp.broadcast_to(slot, (8, LANES))


def x_side(side, even, got_a, got_b, block):
    a, b = got_a[pl.ds(block, 2)], got_b[pl.ds(block, 2)]
    return jnp.where(even, b, a) if side == 0 else jnp.where(even, a, b)


def sums_kernel(sizes, length, state, small, local, got_a, got_b, *refs):
    nx, nz = sizes
    count = 1 if nz == 2 else 2
    z_got, (whole, send), z_pay = refs[:count], refs[count : count + 2], refs[count + 2 :]
    z_from = [z_got[0], z_got[-1]]
    x_place, z_place = lax.axis_index("gx"), lax.axis_index("gz")
    even = x_place % 2 == 0
    rows = Rows()
    weights = z_weights(rows)
    corners = {}
    first_sums, second_sums = [], []
    for z in range(2):
        u = load(state, z)
        for f in range(4):
            whole[z, f] = local[z, f]
        sign = -1 if z == 0 else 1
        inside = (z_place > 0) if z == 0 else (z_place < nz - 1)
        packed = z_from[z][0:8].reshape(4, 2, 8, LANES)
        terms = met_terms(u, packed, float(sign), weights[sign] * jnp.where(inside, 1.0, 0.0))
        for f in range(4):
            whole[z, f] += terms[f]
        for side in range(2):
            sign = 1.0 if side else -1.0
            a = 3 * side
            end = (x_place == nx - 1) if side else (x_place == 0)
            mine = [u[f][a] for f in range(4)]
            theirs = [x_side(side, even, got_a, got_b, 4 * f + 2 * z) for f in range(4)]
            corners[side, z] = theirs
            flag = small[1, X_WALL + 2 * side + z : X_WALL + 2 * side + z + 1, :]
            inner = traces(mine, 0, -sign)
            image = (1.0 - 2.0 * flag) * (mine[0] + sign * mine[3])
            outer = [
                jnp.where(end, e, o)
                for e, o in zip(inner[:2] + [image], traces(theirs, 0, -sign))
            ]
            terms = face_terms(inner, outer, 0, sign, JUMP, False)
            for f in range(4):
                whole[z, f, a] += terms[f]
        first = sum(whole[z, k] * u[k] for k in range(3))
        second = sum(u[k] * u[k] for k in range(3))
        first_sums.append(jnp.sum(first, axis=(0, 1, 2))[None])
        second_sums.append(jnp.sum(second, axis=(0, 1, 2))[None])
    devices = send.shape[0]
    slots = small[0].astype(jnp.int32)
    total = jnp.zeros((devices, LANES), jnp.float32)
    place = lax.broadcasted_iota(jnp.int32, (LANES, LANES), 0)
    owner = lax.broadcasted_iota(jnp.int32, (devices, LANES), 0)
    for z in range(2):
        slot = slots[z : z + 1, :]
        chosen = jnp.where(owner == slot // length, 1.0, 0.0).astype(jnp.bfloat16)
        position = slot % length
        values = jnp.where(
            place == position + length,
            first_sums[z],
            jnp.where(place == position + 2 * length, second_sums[z], 0.0),
        )
        for _ in range(3):
            piece = values.astype(jnp.bfloat16)
            total += lax.dot_general(
                chosen, piece, (((1,), (1,)), ((), ())), preferred_element_type=jnp.float32
            )
            values = values - piece.astype(jnp.float32)
    send[...] = total
    logk = small[1, LOGK : LOGK + 1, 0:length]
    send[:, 0:length] = jnp.broadcast_to(logk, (devices, length))
    faces = [packed_face(rows, load(whole, z), 2 * z - 1) for z in range(2)]
    edges = [[packed_face(rows, corners[side, z], 2 * z - 1) for z in range(2)] for side in range(2)]
    for direction in range(count):
        upper = z_place == 0 if nz == 2 else direction == 0
        z_pay[direction][0:8] = jnp.where(upper, faces[1], faces[0]).reshape(8, 8, LANES)
        for side in range(2):
            block = W_CORNERS + 2 * side
            z_pay[direction][block : block + 2] = jnp.where(upper, edges[side][1], edges[side][0])


def look_up(table, length, slots):
    devices = table.shape[0]
    fold = LANES // length
    table_rows = devices // fold
    chunk = min(8, table_rows)
    lane = lax.broadcasted_iota(jnp.int32, (chunk, LANES), 1)
    in_lane = slots & (LANES - 1)
    in_row = lax.shift_right_logical(slots, 7)

    def step(index, result):
        rows = jnp.zeros((chunk, LANES), jnp.float32)
        for j in range(fold):
            part = table[pl.ds(index * chunk * fold + j, chunk, stride=fold), :]
            rows += pltpu.roll(jnp.where(lane < length, part, 0.0), j * length, 1)
        for i in range(chunk):
            wide = jnp.broadcast_to(rows[i : i + 1, :], (8, LANES))
            taken = jnp.take_along_axis(wide, in_lane, axis=1)
            result = jnp.where(in_row == index * chunk + i, taken, result)
        return result

    result = jnp.zeros((8, LANES), jnp.float32)
    if table_rows == chunk:
        return step(0, result)
    return lax.fori_loop(0, table_rows // chunk, step, result)


def adjoint_kernel(sizes, length, state, small, whole, got_a, got_b, received, *refs):
    nx, nz = sizes
    count = 1 if nz == 2 else 2
    z_got, w_got, refs = refs[:count], refs[count : 2 * count], refs[2 * count :]
    adjoint_out, gradient_out, adjoint, gradient, done = refs
    z_from, w_from = [z_got[0], z_got[-1]], [w_got[0], w_got[-1]]
    x_place, z_place = lax.axis_index("gx"), lax.axis_index("gz")
    even = x_place % 2 == 0
    rows = Rows()
    weights = z_weights(rows)
    derivative = Derivative(rows, derivative_matrix().T)
    held = jnp.exp(-small[1, LOGK : LOGK + 1, 0:length])
    summed = jnp.sum(received[...], axis=0, keepdims=True)
    first, second = summed[:, length : 2 * length], summed[:, 2 * length : 3 * length]
    gradient[...] = -(SCALE / 64.0) * held * (first + SCALE * held * second)
    copies = [pltpu.make_async_copy(gradient, gradient_out, done.at[2])]
    copies[0].start()
    slot_a, slot_b = got_a[X_SLOTS], got_b[X_SLOTS]
    row = lax.broadcasted_iota(jnp.int32, (8, LANES), 0)
    slots = small[0]
    slots = jnp.where(row // 2 == 1, pltpu.roll(jnp.where(even, slot_b, slot_a), 2, 0), slots)
    slots = jnp.where(row // 2 == 2, pltpu.roll(jnp.where(even, slot_a, slot_b), 4, 0), slots)
    slots = jnp.where(row == 6, z_from[0][Z_SLOTS], slots)
    slots = jnp.where(row == 7, z_from[1][Z_SLOTS], slots)
    quarter = jnp.exp(-look_up(received, length, slots.astype(jnp.int32)))
    resistance = [quarter[i : i + 1, :] for i in range(8)]
    residual = []
    for z in range(2):
        scaled = SCALE * resistance[z]
        residual.append(
            [whole[z, k] + scaled * state[z, k] for k in range(3)] + [whole[z, 3]]
        )
    for z in range(2):
        w = residual[z]
        jumps = y_terms(w, rows, True)
        sign = 1 if z == 0 else -1
        across = z_terms(w, residual[1 - z], float(sign), weights[sign], True)
        sign = -sign
        end = (z_place == 0) if z == 0 else (z_place == nz - 1)
        scaled = SCALE * resistance[6 + z]
        theirs = unpacked_face(w_from[z][0:8].reshape(4, 2, 8, LANES), sign)
        fields = unpacked_face(z_from[z][0:8].reshape(4, 2, 8, LANES), sign)
        theirs = [theirs[k] + scaled * fields[k] for k in range(3)] + [theirs[3]]
        flag = small[1, Z_WALL + z : Z_WALL + z + 1, :]
        inner = traces(w, 2, -float(sign))
        outer = traces(theirs, 2, float(sign))
        image = inner[:2] + [(1.0 - 2.0 * flag) * inner[2]]
        outer = [jnp.where(end, i, o) for i, o in zip(image, outer)]
        beyond = face_terms(inner, outer, 2, float(sign), weights[sign], True)
        grads = [derivative.along(k, w[3]) for k in range(3)]
        divergence = sum(derivative.along(k, w[k]) for k in range(3))
        volume = [SCALE * (resistance[z] * w[k] + grads[k]) for k in range(3)]
        volume.append(SCALE * divergence)
        for f in range(4):
            adjoint[z, f] = volume[f] + jumps[f] + across[f] + beyond[f]
        for side in range(2):
            a = 3 * side
            s = 1.0 if side else -1.0
            u_out = [x_side(side, even, got_a, got_b, 4 * f + 2 * z) for f in range(4)]
            trace = [
                x_side(side, even, got_a, got_b, X_TRACES + 4 * j + 2 * z) for j in range(3)
            ]
            normal, tangential = trace[0], trace[1:]
            mine = traces([state[z, f, a] for f in range(4)], 0, s)
            there = traces(u_out, 0, s)
            normal = normal - (2.0 * JUMP) * (mine[2] - there[2])
            tangential = [t - JUMP * (m - o) for t, m, o in zip(tangential, mine[:2], there[:2])]
            t = float(sign)
            weight = weights[sign] * jnp.where(end, 0.0, 1.0)
            block = W_CORNERS + 2 * side
            edge = met_terms(u_out, w_from[z][block : block + 2], t, weight)
            normal = normal + edge[0] + s * edge[3]
            tangential = [tangential[0] + edge[1], tangential[1] + edge[2]]
            scaled = SCALE * resistance[2 + 2 * side + z]
            normal = normal + scaled * u_out[0]
            tangential = [v + scaled * u_out[1 + j] for j, v in enumerate(tangential)]
            inner = traces([w[f][a] for f in range(4)], 0, -s)
            flag = small[1, X_WALL + 2 * side + z : X_WALL + 2 * side + z + 1, :]
            image = inner[:2] + [(1.0 - 2.0 * flag) * inner[2]]
            last = (x_place == nx - 1) if side else (x_place == 0)
            outer = [jnp.where(last, i, o) for i, o in zip(image, tangential + [normal])]
            terms = face_terms(inner, outer, 0, s, JUMP, True)
            for f in range(4):
                adjoint[z, f, a] += terms[f]
        copies.append(pltpu.make_async_copy(adjoint.at[z], adjoint_out.at[z], done.at[z]))
        copies[-1].start()
    for copy in copies:
        copy.wait()


def call(kernel, operands, in_spec, shapes, out_spec, scratch, room, aliases={}):
    return pl.pallas_call(
        kernel,
        out_shape=[jax.ShapeDtypeStruct(shape, jnp.float32) for shape in shapes],
        in_specs=[in_spec] * len(operands),
        out_specs=[out_spec] * len(shapes),
        scratch_shapes=scratch,
        input_output_aliases=aliases,
        compiler_params=pltpu.CompilerParams(vmem_limit_bytes=room * 1024),
        cost_estimate=pl.CostEstimate(flops=2000000, bytes_accessed=800000, transcendentals=0),
    )(*operands)


def both_ways(pairs):
    return pairs + [(second, first) for first, second in pairs]


def along_z(payloads, nz):
    if nz == 2:
        return [lax.ppermute(payloads[0], "gz", [(0, 1), (1, 0)])]
    up = [(i, i + 1) for i in range(nz - 1)]
    down = [(second, first) for first, second in up]
    return [lax.ppermute(payloads[0], "gz", up), lax.ppermute(payloads[1], "gz", down)]


def shards(nx, nz, state, target, coarse_logk, cell_slot, cell_of, wall_flags_xaxis, z_wall):
    sizes = (nx, nz)
    shape = (2, 4, 4, 2, 8, LANES)
    length = coarse_logk.shape[0]
    state6, target6 = state.reshape(shape), target.reshape(shape)
    z_flags = z_wall.reshape(2, LANES)
    count = 1 if nz == 2 else 2
    x_shape, z_shape, w_shape = ((n, 8, LANES) for n in (X_BLOCKS, Z_BLOCKS, W_BLOCKS))
    held, first_a, first_b = call(
        faces_kernel,
        [state6, target6],
        HBM,
        [shape, x_shape, x_shape],
        VMEM,
        [pltpu.VMEM((2, 2, 4, 2, 8, LANES), jnp.float32), pltpu.SemaphoreType.DMA((3,))],
        54600,
    )
    pay_a, pay_b, positions = call(
        functools.partial(edges_kernel, sizes),
        [first_a, first_b, cell_of.reshape(2, LANES), cell_slot.reshape(-1, LANES), z_flags],
        VMEM,
        [x_shape, x_shape, (8, LANES)],
        VMEM,
        [],
        16 * 1024,
        {0: 0, 1: 1},
    )
    pairs_b = both_ways([(i, i + 1) for i in range(1, nx - 1, 2)])
    pairs_a = both_ways([(i, i + 1) for i in range(0, nx - 1, 2)])
    got_a = lax.ppermute(pay_a, "gx", pairs_a)
    got_b = lax.ppermute(pay_b, "gx", pairs_b)
    small, local, *z_pay = call(
        functools.partial(local_kernel, sizes),
        [held, positions, target6, wall_flags_xaxis, z_flags, coarse_logk.reshape(1, -1)],
        VMEM,
        [(2, 8, LANES), shape] + [z_shape] * count,
        VMEM,
        [],
        16 * 1024,
    )
    z_got = along_z(z_pay, nz)
    whole, send, *w_pay = call(
        functools.partial(sums_kernel, sizes, length),
        [held, small, local, got_a, got_b] + z_got,
        VMEM,
        [shape, (nx * nz, LANES)] + [w_shape] * count,
        VMEM,
        [],
        16 * 1024,
    )
    w_got = along_z(w_pay, nz)
    received = lax.all_to_all(send, ("gx", "gz"), 0, 0, tiled=True)
    adjoint, gradient = call(
        functools.partial(adjoint_kernel, sizes, length),
        [held, small, whole, got_a, got_b, received] + z_got + w_got,
        VMEM,
        [shape, (1, length)],
        HBM,
        [
            pltpu.VMEM(shape, jnp.float32),
            pltpu.VMEM((1, length), jnp.float32),
            pltpu.SemaphoreType.DMA((3,)),
        ],
        16 * 1024,
    )
    return adjoint.reshape(state.shape), gradient.reshape(-1)


def solution(mesh):
    placed = (
        P("gx", "gz", None, None, None),
        P("gx", "gz", None, None, None),
        P(("gx", "gz")),
        P(),
        P("gx", "gz", None),
        P(None, "gz", None),
        P(None, "gx", None),
    )
    return jax.shard_map(
        functools.partial(shards, mesh.shape["gx"], mesh.shape["gz"]),
        mesh=mesh,
        in_specs=placed,
        out_specs=(P("gx", "gz", None, None, None), P(("gx", "gz"))),
        check_vma=False,
    )
```

```python
import functools
import math

import jax
import jax.numpy as jnp
import numpy as np
from jax import lax
from jax.experimental import pallas as pl
from jax.experimental.pallas import tpu as pltpu
from jax.sharding import PartitionSpec as P

SCALE = 0.25
JUMP = 0.75
LANES = 128
VMEM = pl.BlockSpec(memory_space=pltpu.VMEM)
HBM = pl.BlockSpec(memory_space=pltpu.HBM)

X_FIELDS, X_TRACES, X_SLOTS, X_BLOCKS = 0, 16, 28, 29
Z_SLOTS, Z_BLOCKS = 8, 9
W_CORNERS, W_BLOCKS = 8, 12
X_WALL, Z_WALL, LOGK = 0, 4, 6
SUMS = 2


def derivative_matrix():
    points = np.array([-1.0, -math.sqrt(0.2), math.sqrt(0.2), 1.0])
    products = np.array(
        [
            np.prod([points[first] - points[other] for other in range(4) if other != first])
            for first in range(4)
        ]
    )
    matrix = np.zeros((4, 4))
    for first in range(4):
        for second in range(4):
            if first != second:
                matrix[first, second] = (
                    products[first] / products[second] / (points[first] - points[second])
                )
        matrix[first, first] = sum(
            (1.0 / (points[first] - points[other]) for other in range(4) if other != first)
        )
    return matrix


class Rows:
    def __init__(self):
        row = lax.broadcasted_iota(jnp.int32, (8, LANES), 0)
        self.upper = row >= 4
        self.c = row & 3

    def halves(self, low, high):
        return jnp.where(self.upper, jnp.float32(high), jnp.float32(low))

    def by_c(self, values):
        result = jnp.full((8, LANES), values[0], jnp.float32)
        for c in range(1, 4):
            result = jnp.where(self.c == c, jnp.float32(values[c]), result)
        return result


class Derivative:
    def __init__(self, rows, matrix):
        self.matrix = matrix
        self.same = [
            [rows.halves(matrix[2 * h, 2 * g], matrix[2 * h + 1, 2 * g + 1]) for g in range(2)]
            for h in range(2)
        ]
        self.cross = [
            [rows.halves(matrix[2 * h, 2 * g + 1], matrix[2 * h + 1, 2 * g]) for g in range(2)]
            for h in range(2)
        ]
        self.shift = {
            delta: rows.by_c(
                [matrix[c, c + delta] if 0 <= c + delta < 4 else 0.0 for c in range(4)]
            )
            for delta in range(-3, 4)
        }

    def across(self, a, u):
        return sum(float(self.matrix[a, j]) * u[j : j + 1] for j in range(4))

    def along(self, axis, u):
        if axis == 0:
            return jnp.concatenate([self.across(a, u) for a in range(4)])
        if axis == 1:
            swapped = pltpu.roll(u, 4, 2)
            return jnp.stack(
                [
                    sum(self.same[h][g] * u[:, g] + self.cross[h][g] * swapped[:, g] for g in range(2))
                    for h in range(2)
                ],
                axis=1,
            )
        return sum(
            coefficient * (u if delta == 0 else pltpu.roll(u, -delta % 8, 2))
            for delta, coefficient in self.shift.items()
        )


def traces(fields, axis, sign):
    others = [fields[f] for f in range(3) if f != axis]
    return others + [fields[axis] + sign * fields[3]]


def face_terms(inner, outer, axis, sign, weight, adjoint):
    tangential = [weight * (i - o) for i, o in zip(inner[:2], outer[:2])]
    normal = weight * (inner[2] - outer[2])
    if adjoint:
        pressure = (-sign) * (weight * (inner[2] + outer[2]))
    else:
        pressure = (-sign) * normal
    terms = tangential[:]
    terms.insert(axis, normal)
    return terms + [pressure]


def y_terms(fields, rows, adjoint):
    high_weight = rows.halves(0.0, JUMP)
    low_weight = rows.halves(JUMP, 0.0)
    first = [field[:, 0] for field in fields]
    second = [field[:, 1] for field in fields]
    moved = lambda value, step: pltpu.roll(pltpu.roll(value, 4, 1), step, 2)
    flip = 1.0 if adjoint else -1.0
    high_out = [moved(t, LANES - 1) for t in traces(first, 1, flip)]
    high = face_terms(traces(second, 1, -1.0), high_out, 1, 1.0, high_weight, adjoint)
    low_out = [moved(t, 1) for t in traces(second, 1, -flip)]
    low = face_terms(traces(first, 1, 1.0), low_out, 1, -1.0, low_weight, adjoint)
    return [jnp.stack([l, h], axis=1) for l, h in zip(low, high)]


def z_terms(inner, outer_fields, sign, weight, adjoint):
    flip = sign if adjoint else -sign
    outer = [pltpu.roll(t, 3 if sign > 0 else 5, t.ndim - 2) for t in traces(outer_fields, 2, flip)]
    return face_terms(traces(inner, 2, -sign), outer, 2, sign, weight, adjoint)


def packed_face(rows, fields, sign):
    c = 3 if sign > 0 else 0
    axis = fields[0].ndim - 2
    result = None
    for f, field in enumerate(fields):
        moved = field if f == c else pltpu.roll(field, (f - c) % 8, axis)
        result = moved if result is None else jnp.where(rows.c == f, moved, result)
    return result


def unpacked_face(packed, sign):
    c = 3 if sign > 0 else 0
    axis = packed.ndim - 2
    return [packed if f == c else pltpu.roll(packed, (c - f) % 8, axis) for f in range(4)]


def met_terms(inner, packed, sign, weight):
    outer = traces(unpacked_face(packed, sign), 2, -sign)
    return face_terms(traces(inner, 2, -sign), outer, 2, sign, weight, False)


def wall_terms(fields, axis, sign, weight, flag, adjoint):
    inner = traces(fields, axis, -sign)
    image = inner[2] if adjoint else fields[axis] + sign * fields[3]
    outer = inner[:2] + [(1.0 - 2.0 * flag) * image]
    return face_terms(inner, outer, axis, sign, weight, adjoint)


def z_weights(rows):
    return {-1: jnp.where(rows.c == 0, JUMP, 0.0), 1: jnp.where(rows.c == 3, JUMP, 0.0)}


def load(ref, z):
    return [ref[z, f] for f in range(4)]


def faces_kernel(state_in, target_in, state, pay_a, pay_b, target, arrived):
    copies = [pltpu.make_async_copy(state_in, state, arrived.at[0])]
    for side in range(2):
        copies.append(
            pltpu.make_async_copy(
                target_in.at[:, :, 3 * side], target.at[side], arrived.at[1 + side]
            )
        )
    for copy in copies:
        copy.start()
    even = lax.axis_index("gx") % 2 == 0
    rows = Rows()
    derivative = Derivative(rows, derivative_matrix())
    weights = z_weights(rows)
    for copy in copies:
        copy.wait()
    for z in range(2):
        sign = 1 if z == 0 else -1
        values = []
        for side in range(2):
            a = 3 * side
            u = [state[z, f, a : a + 1] for f in range(4)]
            other = [state[1 - z, f, a : a + 1] for f in range(4)]
            grads = [derivative.across(a, state[z, 3])]
            grads += [derivative.along(k, u[3]) for k in (1, 2)]
            divergence = derivative.across(a, state[z, 0])
            divergence += derivative.along(1, u[1]) + derivative.along(2, u[2])
            jumps = y_terms(u, rows, False)
            terms = z_terms(u, other, float(sign), weights[sign], False)
            result = [
                (SCALE * v + j + t)[0] - target[side, z, f]
                for f, (v, j, t) in enumerate(zip(grads + [divergence], jumps, terms))
            ]
            normal = result[0] - result[3] if side else result[0] + result[3]
            values.append([v[0] for v in u] + [normal, result[1], result[2]])
        low, high = values
        for j in range(7):
            pay_a[pl.ds(4 * j + 2 * z, 2)] = jnp.where(even, high[j], low[j])
            pay_b[pl.ds(4 * j + 2 * z, 2)] = jnp.where(even, low[j], high[j])


def wall_rows(sizes, rows, weights, z, flags):
    z_place = lax.axis_index("gz")
    end = (z_place == 0) if z == 0 else (z_place == sizes[1] - 1)
    weight = weights[-1 if z == 0 else 1] * jnp.where(end, 1.0, 0.0)
    return weight, flags[z : z + 1, :].astype(jnp.float32)


def edges_kernel(sizes, first_a, first_b, cell_of, cell_slot, z_wall, pay_a, pay_b, positions):
    nx, nz = sizes
    x_place, z_place = lax.axis_index("gx"), lax.axis_index("gz")
    rows = Rows()
    weights = z_weights(rows)
    cell_rows = cell_slot.shape[0]
    slots = []
    for z in range(2):
        row_of = lax.shift_right_logical(cell_of[z : z + 1, :], 7)
        slot = jnp.zeros((1, LANES), jnp.int32)
        for step in (-1, 0, 1):
            row = (x_place // 4 + step) * nz + z_place
            row = jnp.clip(row, 0, cell_rows - 1)
            slot = jnp.where(row_of == row, cell_slot[pl.ds(row, 1), :], slot)
        slots.append(slot.astype(jnp.float32))
    row = lax.broadcasted_iota(jnp.int32, (8, LANES), 0)
    block = jnp.where(row == 0, slots[0], jnp.where(row == 1, slots[1], 0.0))
    positions[...] = block
    flip = jnp.where(x_place % 2 == 0, -1.0, 1.0)
    for first, pay, factor in ((first_a, pay_a, flip), (first_b, pay_b, -flip)):
        for i in range(X_SLOTS):
            pay[i] = first[i]
        pay[X_SLOTS] = block
        for z in range(2):
            weight, flag = wall_rows(sizes, rows, weights, z, z_wall)
            fields = [first[pl.ds(4 * f + 2 * z, 2)] for f in range(4)]
            terms = wall_terms(fields, 2, -1.0 if z == 0 else 1.0, weight, flag, False)
            normal, tangential = X_TRACES + 2 * z, X_TRACES + 8 + 2 * z
            pay[pl.ds(normal, 2)] = first[pl.ds(normal, 2)] + factor * terms[3]
            pay[pl.ds(tangential, 2)] = first[pl.ds(tangential, 2)] + terms[2]


def local_kernel(sizes, state, positions, target, x_wall, z_wall, logk, small, local, *z_pay):
    nx, nz = sizes
    z_place = lax.axis_index("gz")
    rows = Rows()
    derivative = Derivative(rows, derivative_matrix())
    weights = z_weights(rows)
    small[0] = positions[...]
    for side in range(2):
        small[1, X_WALL + 2 * side : X_WALL + 2 * side + 2, :] = x_wall[side].astype(jnp.float32)
    small[1, Z_WALL : Z_WALL + 2, :] = z_wall[...].astype(jnp.float32)
    small[1, LOGK : LOGK + 1, 0 : logk.shape[1]] = logk[...]
    for z in range(2):
        u = load(state, z)
        other = load(state, 1 - z)
        grads = [derivative.along(k, u[3]) for k in range(3)]
        divergence = sum(derivative.along(k, u[k]) for k in range(3))
        jumps = y_terms(u, rows, False)
        sign = 1 if z == 0 else -1
        across = z_terms(u, other, float(sign), weights[sign], False)
        weight, flag = wall_rows(sizes, rows, weights, z, z_wall)
        wall = wall_terms(u, 2, -float(sign), weight, flag, False)
        for f, (v, j, a, w) in enumerate(zip(grads + [divergence], jumps, across, wall)):
            local[z, f] = SCALE * v + j + a + w - target[z, f]
        first = sum(local[z, k] * u[k] for k in range(3))
        second = sum(u[k] * u[k] for k in range(3))
        small[SUMS, z : z + 1, :] = jnp.sum(first, axis=(0, 1, 2))[None]
        small[SUMS, 2 + z : 3 + z, :] = jnp.sum(second, axis=(0, 1, 2))[None]
    faces = [packed_face(rows, load(state, z), 2 * z - 1) for z in range(2)]
    for direction in range(len(z_pay)):
        upper = z_place == 0 if nz == 2 else direction == 0
        z_pay[direction][0:8] = jnp.where(upper, faces[1], faces[0]).reshape(8, 8, LANES)
        slot = jnp.where(upper, positions[1:2, :], positions[0:1, :])
        z_pay[direction][Z_SLOTS] = jnp.broadcast_to(slot, (8, LANES))


def x_side(side, even, got_a, got_b, block):
    a, b = got_a[pl.ds(block, 2)], got_b[pl.ds(block, 2)]
    return jnp.where(even, b, a) if side == 0 else jnp.where(even, a, b)


def sums_kernel(sizes, length, state, small, local, got_a, got_b, *refs):
    nx, nz = sizes
    count = 1 if nz == 2 else 2
    z_got, (whole, send), z_pay = refs[:count], refs[count : count + 2], refs[count + 2 :]
    z_from = [z_got[0], z_got[-1]]
    x_place, z_place = lax.axis_index("gx"), lax.axis_index("gz")
    even = x_place % 2 == 0
    rows = Rows()
    weights = z_weights(rows)
    corners = {}
    sums = []
    for z in range(2):
        u = load(state, z)
        for f in range(4):
            whole[z, f] = local[z, f]
        sign = -1 if z == 0 else 1
        inside = (z_place > 0) if z == 0 else (z_place < nz - 1)
        packed = z_from[z][0:8].reshape(4, 2, 8, LANES)
        terms = met_terms(u, packed, float(sign), weights[sign] * jnp.where(inside, 1.0, 0.0))
        for f in range(4):
            whole[z, f] += terms[f]
        total = sum(jnp.sum(terms[k] * u[k], axis=(0, 1)) for k in range(3))
        for side in range(2):
            sign = 1.0 if side else -1.0
            a = 3 * side
            end = (x_place == nx - 1) if side else (x_place == 0)
            mine = [u[f][a] for f in range(4)]
            theirs = [x_side(side, even, got_a, got_b, 4 * f + 2 * z) for f in range(4)]
            corners[side, z] = theirs
            flag = small[1, X_WALL + 2 * side + z : X_WALL + 2 * side + z + 1, :]
            inner = traces(mine, 0, -sign)
            image = (1.0 - 2.0 * flag) * (mine[0] + sign * mine[3])
            outer = [
                jnp.where(end, e, o)
                for e, o in zip(inner[:2] + [image], traces(theirs, 0, -sign))
            ]
            terms = face_terms(inner, outer, 0, sign, JUMP, False)
            for f in range(4):
                whole[z, f, a] += terms[f]
            total += sum(jnp.sum(terms[k] * mine[k], axis=0) for k in range(3))
        local_sum = small[SUMS, z : z + 1, :]
        sums.append((local_sum + jnp.sum(total, axis=0)[None], small[SUMS, 2 + z : 3 + z, :]))
    devices = send.shape[0]
    slots = small[0].astype(jnp.int32)
    place = lax.broadcasted_iota(jnp.int32, (LANES, LANES), 0)
    owner = lax.broadcasted_iota(jnp.int32, (devices, LANES), 0)
    chosen, values = [], []
    for z, (first, second) in enumerate(sums):
        slot = slots[z : z + 1, :]
        chosen.append(jnp.where(owner == slot // length, 1.0, 0.0).astype(jnp.bfloat16))
        position = slot % length
        value = jnp.where(
            place == position + length, first, jnp.where(place == position + 2 * length, second, 0.0)
        )
        piece = value.astype(jnp.bfloat16)
        values += [piece, (value - piece.astype(jnp.float32)).astype(jnp.bfloat16)]
    send[...] = lax.dot_general(
        jnp.concatenate([chosen[0], chosen[0], chosen[1], chosen[1]], axis=1),
        jnp.concatenate(values, axis=1),
        (((1,), (1,)), ((), ())),
        preferred_element_type=jnp.float32,
    )
    logk = small[1, LOGK : LOGK + 1, 0:length]
    send[:, 0:length] = jnp.broadcast_to(logk, (devices, length))
    faces = [packed_face(rows, load(whole, z), 2 * z - 1) for z in range(2)]
    edges = [[packed_face(rows, corners[side, z], 2 * z - 1) for z in range(2)] for side in range(2)]
    for direction in range(count):
        upper = z_place == 0 if nz == 2 else direction == 0
        z_pay[direction][0:8] = jnp.where(upper, faces[1], faces[0]).reshape(8, 8, LANES)
        for side in range(2):
            block = W_CORNERS + 2 * side
            z_pay[direction][block : block + 2] = jnp.where(upper, edges[side][1], edges[side][0])


def look_up(table, length, slots):
    devices = table.shape[0]
    fold = LANES // length
    table_rows = devices // fold
    chunk = min(8, table_rows)
    lane = lax.broadcasted_iota(jnp.int32, (chunk, LANES), 1)
    in_lane = slots & (LANES - 1)
    in_row = lax.shift_right_logical(slots, 7)

    def step(index, result):
        rows = jnp.zeros((chunk, LANES), jnp.float32)
        for j in range(fold):
            part = table[pl.ds(index * chunk * fold + j, chunk, stride=fold), :]
            rows += pltpu.roll(jnp.where(lane < length, part, 0.0), j * length, 1)
        for i in range(chunk):
            wide = jnp.broadcast_to(rows[i : i + 1, :], (8, LANES))
            taken = jnp.take_along_axis(wide, in_lane, axis=1)
            result = jnp.where(in_row == index * chunk + i, taken, result)
        return result

    result = jnp.zeros((8, LANES), jnp.float32)
    if table_rows == chunk:
        return step(0, result)
    return lax.fori_loop(0, table_rows // chunk, step, result)


def adjoint_kernel(sizes, length, state, small, whole, got_a, got_b, received, *refs):
    nx, nz = sizes
    count = 1 if nz == 2 else 2
    z_got, w_got, refs = refs[:count], refs[count : 2 * count], refs[2 * count :]
    adjoint_out, gradient_out, adjoint, gradient, done = refs
    z_from, w_from = [z_got[0], z_got[-1]], [w_got[0], w_got[-1]]
    x_place, z_place = lax.axis_index("gx"), lax.axis_index("gz")
    even = x_place % 2 == 0
    rows = Rows()
    weights = z_weights(rows)
    derivative = Derivative(rows, derivative_matrix().T)
    held = jnp.exp(-small[1, LOGK : LOGK + 1, 0:length])
    summed = jnp.sum(received[...], axis=0, keepdims=True)
    first, second = summed[:, length : 2 * length], summed[:, 2 * length : 3 * length]
    gradient[...] = -(SCALE / 64.0) * held * (first + SCALE * held * second)
    copies = [pltpu.make_async_copy(gradient, gradient_out, done.at[2])]
    copies[0].start()
    slot_a, slot_b = got_a[X_SLOTS], got_b[X_SLOTS]
    row = lax.broadcasted_iota(jnp.int32, (8, LANES), 0)
    slots = small[0]
    slots = jnp.where(row // 2 == 1, pltpu.roll(jnp.where(even, slot_b, slot_a), 2, 0), slots)
    slots = jnp.where(row // 2 == 2, pltpu.roll(jnp.where(even, slot_a, slot_b), 4, 0), slots)
    slots = jnp.where(row == 6, z_from[0][Z_SLOTS], slots)
    slots = jnp.where(row == 7, z_from[1][Z_SLOTS], slots)
    quarter = jnp.exp(-look_up(received, length, slots.astype(jnp.int32)))
    resistance = [quarter[i : i + 1, :] for i in range(8)]
    residual = []
    for z in range(2):
        scaled = SCALE * resistance[z]
        residual.append(
            [whole[z, k] + scaled * state[z, k] for k in range(3)] + [whole[z, 3]]
        )
    for z in range(2):
        w = residual[z]
        jumps = y_terms(w, rows, True)
        sign = 1 if z == 0 else -1
        across = z_terms(w, residual[1 - z], float(sign), weights[sign], True)
        sign = -sign
        end = (z_place == 0) if z == 0 else (z_place == nz - 1)
        scaled = SCALE * resistance[6 + z]
        theirs = unpacked_face(w_from[z][0:8].reshape(4, 2, 8, LANES), sign)
        fields = unpacked_face(z_from[z][0:8].reshape(4, 2, 8, LANES), sign)
        theirs = [theirs[k] + scaled * fields[k] for k in range(3)] + [theirs[3]]
        flag = small[1, Z_WALL + z : Z_WALL + z + 1, :]
        inner = traces(w, 2, -float(sign))
        outer = traces(theirs, 2, float(sign))
        image = inner[:2] + [(1.0 - 2.0 * flag) * inner[2]]
        outer = [jnp.where(end, i, o) for i, o in zip(image, outer)]
        beyond = face_terms(inner, outer, 2, float(sign), weights[sign], True)
        grads = [derivative.along(k, w[3]) for k in range(3)]
        divergence = sum(derivative.along(k, w[k]) for k in range(3))
        volume = [SCALE * (resistance[z] * w[k] + grads[k]) for k in range(3)]
        volume.append(SCALE * divergence)
        for f in range(4):
            adjoint[z, f] = volume[f] + jumps[f] + across[f] + beyond[f]
        for side in range(2):
            a = 3 * side
            s = 1.0 if side else -1.0
            u_out = [x_side(side, even, got_a, got_b, 4 * f + 2 * z) for f in range(4)]
            trace = [
                x_side(side, even, got_a, got_b, X_TRACES + 4 * j + 2 * z) for j in range(3)
            ]
            normal, tangential = trace[0], trace[1:]
            mine = traces([state[z, f, a] for f in range(4)], 0, s)
            there = traces(u_out, 0, s)
            normal = normal - (2.0 * JUMP) * (mine[2] - there[2])
            tangential = [t - JUMP * (m - o) for t, m, o in zip(tangential, mine[:2], there[:2])]
            t = float(sign)
            weight = weights[sign] * jnp.where(end, 0.0, 1.0)
            block = W_CORNERS + 2 * side
            edge = met_terms(u_out, w_from[z][block : block + 2], t, weight)
            normal = normal + edge[0] + s * edge[3]
            tangential = [tangential[0] + edge[1], tangential[1] + edge[2]]
            scaled = SCALE * resistance[2 + 2 * side + z]
            normal = normal + scaled * u_out[0]
            tangential = [v + scaled * u_out[1 + j] for j, v in enumerate(tangential)]
            inner = traces([w[f][a] for f in range(4)], 0, -s)
            flag = small[1, X_WALL + 2 * side + z : X_WALL + 2 * side + z + 1, :]
            image = inner[:2] + [(1.0 - 2.0 * flag) * inner[2]]
            last = (x_place == nx - 1) if side else (x_place == 0)
            outer = [jnp.where(last, i, o) for i, o in zip(image, tangential + [normal])]
            terms = face_terms(inner, outer, 0, s, JUMP, True)
            for f in range(4):
                adjoint[z, f, a] += terms[f]
        copies.append(pltpu.make_async_copy(adjoint.at[z], adjoint_out.at[z], done.at[z]))
        copies[-1].start()
    for copy in copies:
        copy.wait()


def call(kernel, operands, in_spec, shapes, out_spec, scratch, room):
    return pl.pallas_call(
        kernel,
        out_shape=[jax.ShapeDtypeStruct(shape, jnp.float32) for shape in shapes],
        in_specs=[in_spec] * len(operands),
        out_specs=[out_spec] * len(shapes),
        scratch_shapes=scratch,
        compiler_params=pltpu.CompilerParams(vmem_limit_bytes=room * 1024),
        cost_estimate=pl.CostEstimate(flops=2000000, bytes_accessed=800000, transcendentals=0),
    )(*operands)


def both_ways(pairs):
    return pairs + [(second, first) for first, second in pairs]


def along_z(payloads, nz):
    if nz == 2:
        return [lax.ppermute(payloads[0], "gz", [(0, 1), (1, 0)])]
    up = [(i, i + 1) for i in range(nz - 1)]
    down = [(second, first) for first, second in up]
    return [lax.ppermute(payloads[0], "gz", up), lax.ppermute(payloads[1], "gz", down)]


def shards(nx, nz, state, target, coarse_logk, cell_slot, cell_of, wall_flags_xaxis, z_wall):
    sizes = (nx, nz)
    shape = (2, 4, 4, 2, 8, LANES)
    length = coarse_logk.shape[0]
    state6, target6 = state.reshape(shape), target.reshape(shape)
    z_flags = z_wall.reshape(2, LANES)
    count = 1 if nz == 2 else 2
    x_shape, z_shape, w_shape = ((n, 8, LANES) for n in (X_BLOCKS, Z_BLOCKS, W_BLOCKS))
    held, first_a, first_b = call(
        faces_kernel,
        [state6, target6],
        HBM,
        [shape, x_shape, x_shape],
        VMEM,
        [pltpu.VMEM((2, 2, 4, 2, 8, LANES), jnp.float32), pltpu.SemaphoreType.DMA((3,))],
        54600,
    )
    pay_a, pay_b, positions = call(
        functools.partial(edges_kernel, sizes),
        [first_a, first_b, cell_of.reshape(2, LANES), cell_slot.reshape(-1, LANES), z_flags],
        VMEM,
        [x_shape, x_shape, (8, LANES)],
        VMEM,
        [],
        16 * 1024,
    )
    pairs_b = both_ways([(i, i + 1) for i in range(1, nx - 1, 2)])
    pairs_a = both_ways([(i, i + 1) for i in range(0, nx - 1, 2)])
    got_a = lax.ppermute(pay_a, "gx", pairs_a)
    got_b = lax.ppermute(pay_b, "gx", pairs_b)
    small, local, *z_pay = call(
        functools.partial(local_kernel, sizes),
        [held, positions, target6, wall_flags_xaxis, z_flags, coarse_logk.reshape(1, -1)],
        VMEM,
        [(3, 8, LANES), shape] + [z_shape] * count,
        VMEM,
        [],
        16 * 1024,
    )
    z_got = along_z(z_pay, nz)
    whole, send, *w_pay = call(
        functools.partial(sums_kernel, sizes, length),
        [held, small, local, got_a, got_b] + z_got,
        VMEM,
        [shape, (nx * nz, LANES)] + [w_shape] * count,
        VMEM,
        [],
        16 * 1024,
    )
    w_got = along_z(w_pay, nz)
    received = lax.all_to_all(send, ("gx", "gz"), 0, 0, tiled=True)
    adjoint, gradient = call(
        functools.partial(adjoint_kernel, sizes, length),
        [held, small, whole, got_a, got_b, received] + z_got + w_got,
        VMEM,
        [shape, (1, length)],
        HBM,
        [
            pltpu.VMEM(shape, jnp.float32),
            pltpu.VMEM((1, length), jnp.float32),
            pltpu.SemaphoreType.DMA((3,)),
        ],
        16 * 1024,
    )
    return adjoint.reshape(state.shape), gradient.reshape(-1)


def solution(mesh):
    placed = (
        P("gx", "gz", None, None, None),
        P("gx", "gz", None, None, None),
        P(("gx", "gz")),
        P(),
        P("gx", "gz", None),
        P(None, "gz", None),
        P(None, "gx", None),
    )
    return jax.shard_map(
        functools.partial(shards, mesh.shape["gx"], mesh.shape["gz"]),
        mesh=mesh,
        in_specs=placed,
        out_specs=(P("gx", "gz", None, None, None), P(("gx", "gz"))),
        check_vma=False,
    )
```

```python
import functools
import math

import jax
import jax.numpy as jnp
import numpy as np
from jax import lax
from jax.experimental import pallas as pl
from jax.experimental.pallas import tpu as pltpu
from jax.sharding import PartitionSpec as P

SCALE = 0.25
JUMP = 0.75
LANES = 128
VMEM = pl.BlockSpec(memory_space=pltpu.VMEM)
HBM = pl.BlockSpec(memory_space=pltpu.HBM)

X_FIELDS, X_TRACES, X_SLOTS, X_BLOCKS = 0, 16, 28, 29
Z_SLOTS, Z_BLOCKS = 8, 9
W_CORNERS, W_BLOCKS = 8, 12
X_WALL, Z_WALL, LOGK = 0, 4, 6


def derivative_matrix():
    points = np.array([-1.0, -math.sqrt(0.2), math.sqrt(0.2), 1.0])
    products = np.array(
        [
            np.prod([points[first] - points[other] for other in range(4) if other != first])
            for first in range(4)
        ]
    )
    matrix = np.zeros((4, 4))
    for first in range(4):
        for second in range(4):
            if first != second:
                matrix[first, second] = (
                    products[first] / products[second] / (points[first] - points[second])
                )
        matrix[first, first] = sum(
            (1.0 / (points[first] - points[other]) for other in range(4) if other != first)
        )
    return matrix


class Rows:
    def __init__(self):
        row = lax.broadcasted_iota(jnp.int32, (8, LANES), 0)
        self.upper = row >= 4
        self.c = row & 3

    def halves(self, low, high):
        return jnp.where(self.upper, jnp.float32(high), jnp.float32(low))

    def by_c(self, values):
        result = jnp.full((8, LANES), values[0], jnp.float32)
        for c in range(1, 4):
            result = jnp.where(self.c == c, jnp.float32(values[c]), result)
        return result


class Derivative:
    def __init__(self, rows, matrix):
        self.matrix = matrix
        self.same = [
            [rows.halves(matrix[2 * h, 2 * g], matrix[2 * h + 1, 2 * g + 1]) for g in range(2)]
            for h in range(2)
        ]
        self.cross = [
            [rows.halves(matrix[2 * h, 2 * g + 1], matrix[2 * h + 1, 2 * g]) for g in range(2)]
            for h in range(2)
        ]
        self.shift = {
            delta: rows.by_c(
                [matrix[c, c + delta] if 0 <= c + delta < 4 else 0.0 for c in range(4)]
            )
            for delta in range(-3, 4)
        }

    def across(self, a, u):
        return sum(float(self.matrix[a, j]) * u[j : j + 1] for j in range(4))

    def along(self, axis, u):
        if axis == 0:
            return jnp.concatenate([self.across(a, u) for a in range(4)])
        if axis == 1:
            swapped = pltpu.roll(u, 4, 2)
            return jnp.stack(
                [
                    sum(self.same[h][g] * u[:, g] + self.cross[h][g] * swapped[:, g] for g in range(2))
                    for h in range(2)
                ],
                axis=1,
            )
        return sum(
            coefficient * (u if delta == 0 else pltpu.roll(u, -delta % 8, 2))
            for delta, coefficient in self.shift.items()
        )


def traces(fields, axis, sign):
    others = [fields[f] for f in range(3) if f != axis]
    return others + [fields[axis] + sign * fields[3]]


def face_terms(inner, outer, axis, sign, weight, adjoint):
    tangential = [weight * (i - o) for i, o in zip(inner[:2], outer[:2])]
    normal = weight * (inner[2] - outer[2])
    if adjoint:
        pressure = (-sign) * (weight * (inner[2] + outer[2]))
    else:
        pressure = (-sign) * normal
    terms = tangential[:]
    terms.insert(axis, normal)
    return terms + [pressure]


def y_terms(fields, rows, adjoint):
    high_weight = rows.halves(0.0, JUMP)
    low_weight = rows.halves(JUMP, 0.0)
    first = [field[:, 0] for field in fields]
    second = [field[:, 1] for field in fields]
    moved = lambda value, step: pltpu.roll(pltpu.roll(value, 4, 1), step, 2)
    flip = 1.0 if adjoint else -1.0
    high_out = [moved(t, LANES - 1) for t in traces(first, 1, flip)]
    high = face_terms(traces(second, 1, -1.0), high_out, 1, 1.0, high_weight, adjoint)
    low_out = [moved(t, 1) for t in traces(second, 1, -flip)]
    low = face_terms(traces(first, 1, 1.0), low_out, 1, -1.0, low_weight, adjoint)
    return [jnp.stack([l, h], axis=1) for l, h in zip(low, high)]


def z_terms(inner, outer_fields, sign, weight, adjoint):
    flip = sign if adjoint else -sign
    outer = [pltpu.roll(t, 3 if sign > 0 else 5, t.ndim - 2) for t in traces(outer_fields, 2, flip)]
    return face_terms(traces(inner, 2, -sign), outer, 2, sign, weight, adjoint)


def packed_face(rows, fields, sign):
    c = 3 if sign > 0 else 0
    axis = fields[0].ndim - 2
    result = None
    for f, field in enumerate(fields):
        moved = field if f == c else pltpu.roll(field, (f - c) % 8, axis)
        result = moved if result is None else jnp.where(rows.c == f, moved, result)
    return result


def unpacked_face(packed, sign):
    c = 3 if sign > 0 else 0
    axis = packed.ndim - 2
    return [packed if f == c else pltpu.roll(packed, (c - f) % 8, axis) for f in range(4)]


def met_terms(inner, packed, sign, weight):
    outer = traces(unpacked_face(packed, sign), 2, -sign)
    return face_terms(traces(inner, 2, -sign), outer, 2, sign, weight, False)


def wall_terms(fields, axis, sign, weight, flag, adjoint):
    inner = traces(fields, axis, -sign)
    image = inner[2] if adjoint else fields[axis] + sign * fields[3]
    outer = inner[:2] + [(1.0 - 2.0 * flag) * image]
    return face_terms(inner, outer, axis, sign, weight, adjoint)


def z_weights(rows):
    return {-1: jnp.where(rows.c == 0, JUMP, 0.0), 1: jnp.where(rows.c == 3, JUMP, 0.0)}


def load(ref, z):
    return [ref[z, f] for f in range(4)]


def faces_kernel(state_in, target_in, state, pay_a, pay_b, target, arrived):
    copies = [pltpu.make_async_copy(state_in, state, arrived.at[0])]
    for side in range(2):
        copies.append(
            pltpu.make_async_copy(
                target_in.at[:, :, 3 * side], target.at[side], arrived.at[1 + side]
            )
        )
    for copy in copies:
        copy.start()
    even = lax.axis_index("gx") % 2 == 0
    rows = Rows()
    derivative = Derivative(rows, derivative_matrix())
    weights = z_weights(rows)
    for copy in copies:
        copy.wait()
    for z in range(2):
        sign = 1 if z == 0 else -1
        values = []
        for side in range(2):
            a = 3 * side
            u = [state[z, f, a : a + 1] for f in range(4)]
            other = [state[1 - z, f, a : a + 1] for f in range(4)]
            grads = [derivative.across(a, state[z, 3])]
            grads += [derivative.along(k, u[3]) for k in (1, 2)]
            divergence = derivative.across(a, state[z, 0])
            divergence += derivative.along(1, u[1]) + derivative.along(2, u[2])
            jumps = y_terms(u, rows, False)
            terms = z_terms(u, other, float(sign), weights[sign], False)
            result = [
                (SCALE * v + j + t)[0] - target[side, z, f]
                for f, (v, j, t) in enumerate(zip(grads + [divergence], jumps, terms))
            ]
            normal = result[0] - result[3] if side else result[0] + result[3]
            values.append([v[0] for v in u] + [normal, result[1], result[2]])
        low, high = values
        for j in range(7):
            pay_a[pl.ds(4 * j + 2 * z, 2)] = jnp.where(even, high[j], low[j])
            pay_b[pl.ds(4 * j + 2 * z, 2)] = jnp.where(even, low[j], high[j])


def wall_rows(sizes, rows, weights, z, flags):
    z_place = lax.axis_index("gz")
    end = (z_place == 0) if z == 0 else (z_place == sizes[1] - 1)
    weight = weights[-1 if z == 0 else 1] * jnp.where(end, 1.0, 0.0)
    return weight, flags[z : z + 1, :].astype(jnp.float32)


def edges_kernel(
    sizes, first_a, first_b, cell_of, cell_slot, x_wall, z_wall, logk, pay_a, pay_b, small
):
    nx, nz = sizes
    x_place, z_place = lax.axis_index("gx"), lax.axis_index("gz")
    rows = Rows()
    weights = z_weights(rows)
    cell_rows = cell_slot.shape[0]
    slots = []
    for z in range(2):
        row_of = lax.shift_right_logical(cell_of[z : z + 1, :], 7)
        slot = jnp.zeros((1, LANES), jnp.int32)
        for step in (-1, 0, 1):
            row = (x_place // 4 + step) * nz + z_place
            row = jnp.clip(row, 0, cell_rows - 1)
            slot = jnp.where(row_of == row, cell_slot[pl.ds(row, 1), :], slot)
        slots.append(slot.astype(jnp.float32))
    row = lax.broadcasted_iota(jnp.int32, (8, LANES), 0)
    block = jnp.where(row == 0, slots[0], jnp.where(row == 1, slots[1], 0.0))
    small[0] = block
    for side in range(2):
        small[1, X_WALL + 2 * side : X_WALL + 2 * side + 2, :] = x_wall[side].astype(jnp.float32)
    small[1, Z_WALL : Z_WALL + 2, :] = z_wall[...].astype(jnp.float32)
    small[1, LOGK : LOGK + 1, 0 : logk.shape[1]] = logk[...]
    flip = jnp.where(x_place % 2 == 0, -1.0, 1.0)
    for first, pay, factor in ((first_a, pay_a, flip), (first_b, pay_b, -flip)):
        for i in range(X_SLOTS):
            pay[i] = first[i]
        pay[X_SLOTS] = block
        for z in range(2):
            weight, flag = wall_rows(sizes, rows, weights, z, z_wall)
            fields = [first[pl.ds(4 * f + 2 * z, 2)] for f in range(4)]
            terms = wall_terms(fields, 2, -1.0 if z == 0 else 1.0, weight, flag, False)
            normal, tangential = X_TRACES + 2 * z, X_TRACES + 8 + 2 * z
            pay[pl.ds(normal, 2)] = first[pl.ds(normal, 2)] + factor * terms[3]
            pay[pl.ds(tangential, 2)] = first[pl.ds(tangential, 2)] + terms[2]


def local_kernel(sizes, state, small, target, local, sums, *z_pay):
    nx, nz = sizes
    z_place = lax.axis_index("gz")
    rows = Rows()
    derivative = Derivative(rows, derivative_matrix())
    weights = z_weights(rows)
    for z in range(2):
        u = load(state, z)
        other = load(state, 1 - z)
        grads = [derivative.along(k, u[3]) for k in range(3)]
        divergence = sum(derivative.along(k, u[k]) for k in range(3))
        jumps = y_terms(u, rows, False)
        sign = 1 if z == 0 else -1
        across = z_terms(u, other, float(sign), weights[sign], False)
        weight, flag = wall_rows(sizes, rows, weights, z, small[1, Z_WALL : Z_WALL + 2, :])
        wall = wall_terms(u, 2, -float(sign), weight, flag, False)
        for f, (v, j, a, w) in enumerate(zip(grads + [divergence], jumps, across, wall)):
            local[z, f] = SCALE * v + j + a + w - target[z, f]
        first = sum(local[z, k] * u[k] for k in range(3))
        second = sum(u[k] * u[k] for k in range(3))
        sums[z : z + 1, :] = jnp.sum(first, axis=(0, 1, 2))[None]
        sums[2 + z : 3 + z, :] = jnp.sum(second, axis=(0, 1, 2))[None]
    faces = [packed_face(rows, load(state, z), 2 * z - 1) for z in range(2)]
    for direction in range(len(z_pay)):
        upper = z_place == 0 if nz == 2 else direction == 0
        z_pay[direction][0:8] = jnp.where(upper, faces[1], faces[0]).reshape(8, 8, LANES)
        slot = jnp.where(upper, small[0, 1:2, :], small[0, 0:1, :])
        z_pay[direction][Z_SLOTS] = jnp.broadcast_to(slot, (8, LANES))


def x_side(side, even, got_a, got_b, block):
    a, b = got_a[pl.ds(block, 2)], got_b[pl.ds(block, 2)]
    return jnp.where(even, b, a) if side == 0 else jnp.where(even, a, b)


def sums_kernel(sizes, length, state, small, local, local_sums, got_a, got_b, *refs):
    nx, nz = sizes
    count = 1 if nz == 2 else 2
    z_got, (whole, send), z_pay = refs[:count], refs[count : count + 2], refs[count + 2 :]
    z_from = [z_got[0], z_got[-1]]
    x_place, z_place = lax.axis_index("gx"), lax.axis_index("gz")
    even = x_place % 2 == 0
    rows = Rows()
    weights = z_weights(rows)
    corners = {}
    sums = []
    for z in range(2):
        u = load(state, z)
        for f in range(4):
            whole[z, f] = local[z, f]
        sign = -1 if z == 0 else 1
        inside = (z_place > 0) if z == 0 else (z_place < nz - 1)
        packed = z_from[z][0:8].reshape(4, 2, 8, LANES)
        terms = met_terms(u, packed, float(sign), weights[sign] * jnp.where(inside, 1.0, 0.0))
        for f in range(4):
            whole[z, f] += terms[f]
        total = sum(jnp.sum(terms[k] * u[k], axis=(0, 1)) for k in range(3))
        for side in range(2):
            sign = 1.0 if side else -1.0
            a = 3 * side
            end = (x_place == nx - 1) if side else (x_place == 0)
            mine = [u[f][a] for f in range(4)]
            theirs = [x_side(side, even, got_a, got_b, 4 * f + 2 * z) for f in range(4)]
            corners[side, z] = theirs
            flag = small[1, X_WALL + 2 * side + z : X_WALL + 2 * side + z + 1, :]
            inner = traces(mine, 0, -sign)
            image = (1.0 - 2.0 * flag) * (mine[0] + sign * mine[3])
            outer = [
                jnp.where(end, e, o)
                for e, o in zip(inner[:2] + [image], traces(theirs, 0, -sign))
            ]
            terms = face_terms(inner, outer, 0, sign, JUMP, False)
            for f in range(4):
                whole[z, f, a] += terms[f]
            total += sum(jnp.sum(terms[k] * mine[k], axis=0) for k in range(3))
        first = local_sums[z : z + 1, :] + jnp.sum(total, axis=0)[None]
        sums.append((first, local_sums[2 + z : 3 + z, :]))
    devices = send.shape[0]
    slots = small[0].astype(jnp.int32)
    place = lax.broadcasted_iota(jnp.int32, (LANES, LANES), 0)
    owner = lax.broadcasted_iota(jnp.int32, (devices, LANES), 0)
    chosen, values = [], []
    for z, (first, second) in enumerate(sums):
        slot = slots[z : z + 1, :]
        chosen.append(jnp.where(owner == slot // length, 1.0, 0.0).astype(jnp.bfloat16))
        position = slot % length
        value = jnp.where(
            place == position + length, first, jnp.where(place == position + 2 * length, second, 0.0)
        )
        for _ in range(3):
            piece = value.astype(jnp.bfloat16)
            values.append(piece)
            value = value - piece.astype(jnp.float32)
    send[...] = lax.dot_general(
        jnp.concatenate([chosen[0]] * 3 + [chosen[1]] * 3, axis=1),
        jnp.concatenate(values, axis=1),
        (((1,), (1,)), ((), ())),
        preferred_element_type=jnp.float32,
    )
    logk = small[1, LOGK : LOGK + 1, 0:length]
    send[:, 0:length] = jnp.broadcast_to(logk, (devices, length))
    faces = [packed_face(rows, load(whole, z), 2 * z - 1) for z in range(2)]
    edges = [[packed_face(rows, corners[side, z], 2 * z - 1) for z in range(2)] for side in range(2)]
    for direction in range(count):
        upper = z_place == 0 if nz == 2 else direction == 0
        z_pay[direction][0:8] = jnp.where(upper, faces[1], faces[0]).reshape(8, 8, LANES)
        for side in range(2):
            block = W_CORNERS + 2 * side
            z_pay[direction][block : block + 2] = jnp.where(upper, edges[side][1], edges[side][0])


def look_up(table, length, slots):
    devices = table.shape[0]
    fold = LANES // length
    table_rows = devices // fold
    chunk = min(8, table_rows)
    lane = lax.broadcasted_iota(jnp.int32, (chunk, LANES), 1)
    in_lane = slots & (LANES - 1)
    in_row = lax.shift_right_logical(slots, 7)

    def step(index, result):
        rows = jnp.zeros((chunk, LANES), jnp.float32)
        for j in range(fold):
            part = table[pl.ds(index * chunk * fold + j, chunk, stride=fold), :]
            rows += pltpu.roll(jnp.where(lane < length, part, 0.0), j * length, 1)
        for i in range(chunk):
            wide = jnp.broadcast_to(rows[i : i + 1, :], (8, LANES))
            taken = jnp.take_along_axis(wide, in_lane, axis=1)
            result = jnp.where(in_row == index * chunk + i, taken, result)
        return result

    result = jnp.zeros((8, LANES), jnp.float32)
    if table_rows == chunk:
        return step(0, result)
    return lax.fori_loop(0, table_rows // chunk, step, result)


def adjoint_kernel(sizes, length, state, small, whole, got_a, got_b, received, *refs):
    nx, nz = sizes
    count = 1 if nz == 2 else 2
    z_got, w_got, refs = refs[:count], refs[count : 2 * count], refs[2 * count :]
    adjoint_out, gradient_out, adjoint, gradient, done = refs
    z_from, w_from = [z_got[0], z_got[-1]], [w_got[0], w_got[-1]]
    x_place, z_place = lax.axis_index("gx"), lax.axis_index("gz")
    even = x_place % 2 == 0
    rows = Rows()
    weights = z_weights(rows)
    derivative = Derivative(rows, derivative_matrix().T)
    held = jnp.exp(-small[1, LOGK : LOGK + 1, 0:length])
    summed = jnp.sum(received[...], axis=0, keepdims=True)
    first, second = summed[:, length : 2 * length], summed[:, 2 * length : 3 * length]
    gradient[...] = -(SCALE / 64.0) * held * (first + SCALE * held * second)
    copies = [pltpu.make_async_copy(gradient, gradient_out, done.at[2])]
    copies[0].start()
    slot_a, slot_b = got_a[X_SLOTS], got_b[X_SLOTS]
    row = lax.broadcasted_iota(jnp.int32, (8, LANES), 0)
    slots = small[0]
    slots = jnp.where(row // 2 == 1, pltpu.roll(jnp.where(even, slot_b, slot_a), 2, 0), slots)
    slots = jnp.where(row // 2 == 2, pltpu.roll(jnp.where(even, slot_a, slot_b), 4, 0), slots)
    slots = jnp.where(row == 6, z_from[0][Z_SLOTS], slots)
    slots = jnp.where(row == 7, z_from[1][Z_SLOTS], slots)
    quarter = jnp.exp(-look_up(received, length, slots.astype(jnp.int32)))
    resistance = [quarter[i : i + 1, :] for i in range(8)]
    residual = []
    for z in range(2):
        scaled = SCALE * resistance[z]
        residual.append(
            [whole[z, k] + scaled * state[z, k] for k in range(3)] + [whole[z, 3]]
        )
    for z in range(2):
        w = residual[z]
        jumps = y_terms(w, rows, True)
        sign = 1 if z == 0 else -1
        across = z_terms(w, residual[1 - z], float(sign), weights[sign], True)
        sign = -sign
        end = (z_place == 0) if z == 0 else (z_place == nz - 1)
        scaled = SCALE * resistance[6 + z]
        theirs = unpacked_face(w_from[z][0:8].reshape(4, 2, 8, LANES), sign)
        fields = unpacked_face(z_from[z][0:8].reshape(4, 2, 8, LANES), sign)
        theirs = [theirs[k] + scaled * fields[k] for k in range(3)] + [theirs[3]]
        flag = small[1, Z_WALL + z : Z_WALL + z + 1, :]
        inner = traces(w, 2, -float(sign))
        outer = traces(theirs, 2, float(sign))
        image = inner[:2] + [(1.0 - 2.0 * flag) * inner[2]]
        outer = [jnp.where(end, i, o) for i, o in zip(image, outer)]
        beyond = face_terms(inner, outer, 2, float(sign), weights[sign], True)
        grads = [derivative.along(k, w[3]) for k in range(3)]
        divergence = sum(derivative.along(k, w[k]) for k in range(3))
        volume = [SCALE * (resistance[z] * w[k] + grads[k]) for k in range(3)]
        volume.append(SCALE * divergence)
        for f in range(4):
            adjoint[z, f] = volume[f] + jumps[f] + across[f] + beyond[f]
        for side in range(2):
            a = 3 * side
            s = 1.0 if side else -1.0
            u_out = [x_side(side, even, got_a, got_b, 4 * f + 2 * z) for f in range(4)]
            trace = [
                x_side(side, even, got_a, got_b, X_TRACES + 4 * j + 2 * z) for j in range(3)
            ]
            normal, tangential = trace[0], trace[1:]
            mine = traces([state[z, f, a] for f in range(4)], 0, s)
            there = traces(u_out, 0, s)
            normal = normal - (2.0 * JUMP) * (mine[2] - there[2])
            tangential = [t - JUMP * (m - o) for t, m, o in zip(tangential, mine[:2], there[:2])]
            t = float(sign)
            weight = weights[sign] * jnp.where(end, 0.0, 1.0)
            block = W_CORNERS + 2 * side
            edge = met_terms(u_out, w_from[z][block : block + 2], t, weight)
            normal = normal + edge[0] + s * edge[3]
            tangential = [tangential[0] + edge[1], tangential[1] + edge[2]]
            scaled = SCALE * resistance[2 + 2 * side + z]
            normal = normal + scaled * u_out[0]
            tangential = [v + scaled * u_out[1 + j] for j, v in enumerate(tangential)]
            inner = traces([w[f][a] for f in range(4)], 0, -s)
            flag = small[1, X_WALL + 2 * side + z : X_WALL + 2 * side + z + 1, :]
            image = inner[:2] + [(1.0 - 2.0 * flag) * inner[2]]
            last = (x_place == nx - 1) if side else (x_place == 0)
            outer = [jnp.where(last, i, o) for i, o in zip(image, tangential + [normal])]
            terms = face_terms(inner, outer, 0, s, JUMP, True)
            for f in range(4):
                adjoint[z, f, a] += terms[f]
        copies.append(pltpu.make_async_copy(adjoint.at[z], adjoint_out.at[z], done.at[z]))
        copies[-1].start()
    for copy in copies:
        copy.wait()


def call(kernel, operands, in_spec, shapes, out_spec, scratch, room):
    return pl.pallas_call(
        kernel,
        out_shape=[jax.ShapeDtypeStruct(shape, jnp.float32) for shape in shapes],
        in_specs=[in_spec] * len(operands),
        out_specs=[out_spec] * len(shapes),
        scratch_shapes=scratch,
        compiler_params=pltpu.CompilerParams(vmem_limit_bytes=room * 1024),
        cost_estimate=pl.CostEstimate(flops=2000000, bytes_accessed=800000, transcendentals=0),
    )(*operands)


def both_ways(pairs):
    return pairs + [(second, first) for first, second in pairs]


def along_z(payloads, nz):
    if nz == 2:
        return [lax.ppermute(payloads[0], "gz", [(0, 1), (1, 0)])]
    up = [(i, i + 1) for i in range(nz - 1)]
    down = [(second, first) for first, second in up]
    return [lax.ppermute(payloads[0], "gz", up), lax.ppermute(payloads[1], "gz", down)]


def shards(nx, nz, state, target, coarse_logk, cell_slot, cell_of, wall_flags_xaxis, z_wall):
    sizes = (nx, nz)
    shape = (2, 4, 4, 2, 8, LANES)
    length = coarse_logk.shape[0]
    state6, target6 = state.reshape(shape), target.reshape(shape)
    z_flags = z_wall.reshape(2, LANES)
    count = 1 if nz == 2 else 2
    x_shape, z_shape, w_shape = ((n, 8, LANES) for n in (X_BLOCKS, Z_BLOCKS, W_BLOCKS))
    held, first_a, first_b = call(
        faces_kernel,
        [state6, target6],
        HBM,
        [shape, x_shape, x_shape],
        VMEM,
        [pltpu.VMEM((2, 2, 4, 2, 8, LANES), jnp.float32), pltpu.SemaphoreType.DMA((3,))],
        54600,
    )
    pay_a, pay_b, small = call(
        functools.partial(edges_kernel, sizes),
        [
            first_a,
            first_b,
            cell_of.reshape(2, LANES),
            cell_slot.reshape(-1, LANES),
            wall_flags_xaxis,
            z_flags,
            coarse_logk.reshape(1, -1),
        ],
        VMEM,
        [x_shape, x_shape, (2, 8, LANES)],
        VMEM,
        [],
        16 * 1024,
    )
    pairs_b = both_ways([(i, i + 1) for i in range(1, nx - 1, 2)])
    pairs_a = both_ways([(i, i + 1) for i in range(0, nx - 1, 2)])
    got_a = lax.ppermute(pay_a, "gx", pairs_a)
    got_b = lax.ppermute(pay_b, "gx", pairs_b)
    local, sums, *z_pay = call(
        functools.partial(local_kernel, sizes),
        [held, small, target6],
        VMEM,
        [shape, (4, LANES)] + [z_shape] * count,
        VMEM,
        [],
        16 * 1024,
    )
    z_got = along_z(z_pay, nz)
    whole, send, *w_pay = call(
        functools.partial(sums_kernel, sizes, length),
        [held, small, local, sums, got_a, got_b] + z_got,
        VMEM,
        [shape, (nx * nz, LANES)] + [w_shape] * count,
        VMEM,
        [],
        16 * 1024,
    )
    w_got = along_z(w_pay, nz)
    received = lax.all_to_all(send, ("gx", "gz"), 0, 0, tiled=True)
    adjoint, gradient = call(
        functools.partial(adjoint_kernel, sizes, length),
        [held, small, whole, got_a, got_b, received] + z_got + w_got,
        VMEM,
        [shape, (1, length)],
        HBM,
        [
            pltpu.VMEM(shape, jnp.float32),
            pltpu.VMEM((1, length), jnp.float32),
            pltpu.SemaphoreType.DMA((3,)),
        ],
        16 * 1024,
    )
    return adjoint.reshape(state.shape), gradient.reshape(-1)


def solution(mesh):
    placed = (
        P("gx", "gz", None, None, None),
        P("gx", "gz", None, None, None),
        P(("gx", "gz")),
        P(),
        P("gx", "gz", None),
        P(None, "gz", None),
        P(None, "gx", None),
    )
    return jax.shard_map(
        functools.partial(shards, mesh.shape["gx"], mesh.shape["gz"]),
        mesh=mesh,
        in_specs=placed,
        out_specs=(P("gx", "gz", None, None, None), P(("gx", "gz"))),
        check_vma=False,
    )
```

```python
import functools
import math

import jax
import jax.numpy as jnp
import numpy as np
from jax import lax
from jax.experimental import pallas as pl
from jax.experimental.pallas import tpu as pltpu
from jax.sharding import PartitionSpec as P

SCALE = 0.25
JUMP = 0.75
LANES = 128
VMEM = pl.BlockSpec(memory_space=pltpu.VMEM)
HBM = pl.BlockSpec(memory_space=pltpu.HBM)

X_FIELDS, X_TRACES, X_SLOTS, X_BLOCKS = 0, 16, 28, 29
Z_SLOTS, Z_BLOCKS = 8, 9
W_CORNERS, W_BLOCKS = 8, 12
X_WALL, Z_WALL, LOGK = 0, 4, 6
SUMS = 2


def derivative_matrix():
    points = np.array([-1.0, -math.sqrt(0.2), math.sqrt(0.2), 1.0])
    products = np.array(
        [
            np.prod([points[first] - points[other] for other in range(4) if other != first])
            for first in range(4)
        ]
    )
    matrix = np.zeros((4, 4))
    for first in range(4):
        for second in range(4):
            if first != second:
                matrix[first, second] = (
                    products[first] / products[second] / (points[first] - points[second])
                )
        matrix[first, first] = sum(
            (1.0 / (points[first] - points[other]) for other in range(4) if other != first)
        )
    return matrix


class Rows:
    def __init__(self):
        row = lax.broadcasted_iota(jnp.int32, (8, LANES), 0)
        self.upper = row >= 4
        self.c = row & 3

    def halves(self, low, high):
        return jnp.where(self.upper, jnp.float32(high), jnp.float32(low))

    def by_c(self, values):
        result = jnp.full((8, LANES), values[0], jnp.float32)
        for c in range(1, 4):
            result = jnp.where(self.c == c, jnp.float32(values[c]), result)
        return result


class Derivative:
    def __init__(self, rows, matrix):
        self.matrix = matrix
        self.same = [
            [rows.halves(matrix[2 * h, 2 * g], matrix[2 * h + 1, 2 * g + 1]) for g in range(2)]
            for h in range(2)
        ]
        self.cross = [
            [rows.halves(matrix[2 * h, 2 * g + 1], matrix[2 * h + 1, 2 * g]) for g in range(2)]
            for h in range(2)
        ]
        self.shift = {
            delta: rows.by_c(
                [matrix[c, c + delta] if 0 <= c + delta < 4 else 0.0 for c in range(4)]
            )
            for delta in range(-3, 4)
        }

    def across(self, a, u):
        return sum(float(self.matrix[a, j]) * u[j : j + 1] for j in range(4))

    def along(self, axis, u):
        if axis == 0:
            return jnp.concatenate([self.across(a, u) for a in range(4)])
        if axis == 1:
            swapped = pltpu.roll(u, 4, 2)
            return jnp.stack(
                [
                    sum(self.same[h][g] * u[:, g] + self.cross[h][g] * swapped[:, g] for g in range(2))
                    for h in range(2)
                ],
                axis=1,
            )
        return sum(
            coefficient * (u if delta == 0 else pltpu.roll(u, -delta % 8, 2))
            for delta, coefficient in self.shift.items()
        )


def traces(fields, axis, sign):
    others = [fields[f] for f in range(3) if f != axis]
    return others + [fields[axis] + sign * fields[3]]


def face_terms(inner, outer, axis, sign, weight, adjoint):
    tangential = [weight * (i - o) for i, o in zip(inner[:2], outer[:2])]
    normal = weight * (inner[2] - outer[2])
    if adjoint:
        pressure = (-sign) * (weight * (inner[2] + outer[2]))
    else:
        pressure = (-sign) * normal
    terms = tangential[:]
    terms.insert(axis, normal)
    return terms + [pressure]


def y_terms(fields, rows, adjoint):
    high_weight = rows.halves(0.0, JUMP)
    low_weight = rows.halves(JUMP, 0.0)
    first = [field[:, 0] for field in fields]
    second = [field[:, 1] for field in fields]
    moved = lambda value, step: pltpu.roll(pltpu.roll(value, 4, 1), step, 2)
    flip = 1.0 if adjoint else -1.0
    high_out = [moved(t, LANES - 1) for t in traces(first, 1, flip)]
    high = face_terms(traces(second, 1, -1.0), high_out, 1, 1.0, high_weight, adjoint)
    low_out = [moved(t, 1) for t in traces(second, 1, -flip)]
    low = face_terms(traces(first, 1, 1.0), low_out, 1, -1.0, low_weight, adjoint)
    return [jnp.stack([l, h], axis=1) for l, h in zip(low, high)]


def z_terms(inner, outer_fields, sign, weight, adjoint):
    flip = sign if adjoint else -sign
    outer = [pltpu.roll(t, 3 if sign > 0 else 5, t.ndim - 2) for t in traces(outer_fields, 2, flip)]
    return face_terms(traces(inner, 2, -sign), outer, 2, sign, weight, adjoint)


def packed_face(rows, fields, sign):
    c = 3 if sign > 0 else 0
    axis = fields[0].ndim - 2
    result = None
    for f, field in enumerate(fields):
        moved = field if f == c else pltpu.roll(field, (f - c) % 8, axis)
        result = moved if result is None else jnp.where(rows.c == f, moved, result)
    return result


def unpacked_face(packed, sign):
    c = 3 if sign > 0 else 0
    axis = packed.ndim - 2
    return [packed if f == c else pltpu.roll(packed, (c - f) % 8, axis) for f in range(4)]


def met_terms(inner, packed, sign, weight):
    outer = traces(unpacked_face(packed, sign), 2, -sign)
    return face_terms(traces(inner, 2, -sign), outer, 2, sign, weight, False)


def wall_terms(fields, axis, sign, weight, flag, adjoint):
    inner = traces(fields, axis, -sign)
    image = inner[2] if adjoint else fields[axis] + sign * fields[3]
    outer = inner[:2] + [(1.0 - 2.0 * flag) * image]
    return face_terms(inner, outer, axis, sign, weight, adjoint)


def z_weights(rows):
    return {-1: jnp.where(rows.c == 0, JUMP, 0.0), 1: jnp.where(rows.c == 3, JUMP, 0.0)}


def load(ref, z):
    return [ref[z, f] for f in range(4)]


def faces_kernel(state_in, target_in, state, pay_a, pay_b, target, arrived):
    copies = [pltpu.make_async_copy(state_in, state, arrived.at[0])]
    for side in range(2):
        copies.append(
            pltpu.make_async_copy(
                target_in.at[:, :, 3 * side], target.at[side], arrived.at[1 + side]
            )
        )
    for copy in copies:
        copy.start()
    even = lax.axis_index("gx") % 2 == 0
    rows = Rows()
    derivative = Derivative(rows, derivative_matrix())
    weights = z_weights(rows)
    for copy in copies:
        copy.wait()
    for z in range(2):
        sign = 1 if z == 0 else -1
        values = []
        for side in range(2):
            a = 3 * side
            u = [state[z, f, a : a + 1] for f in range(4)]
            other = [state[1 - z, f, a : a + 1] for f in range(4)]
            grads = [derivative.across(a, state[z, 3])]
            grads += [derivative.along(k, u[3]) for k in (1, 2)]
            divergence = derivative.across(a, state[z, 0])
            divergence += derivative.along(1, u[1]) + derivative.along(2, u[2])
            jumps = y_terms(u, rows, False)
            terms = z_terms(u, other, float(sign), weights[sign], False)
            result = [
                (SCALE * v + j + t)[0] - target[side, z, f]
                for f, (v, j, t) in enumerate(zip(grads + [divergence], jumps, terms))
            ]
            normal = result[0] - result[3] if side else result[0] + result[3]
            values.append([v[0] for v in u] + [normal, result[1], result[2]])
        low, high = values
        for j in range(7):
            pay_a[pl.ds(4 * j + 2 * z, 2)] = jnp.where(even, high[j], low[j])
            pay_b[pl.ds(4 * j + 2 * z, 2)] = jnp.where(even, low[j], high[j])


def wall_rows(sizes, rows, weights, z, flags):
    z_place = lax.axis_index("gz")
    end = (z_place == 0) if z == 0 else (z_place == sizes[1] - 1)
    weight = weights[-1 if z == 0 else 1] * jnp.where(end, 1.0, 0.0)
    return weight, flags[z : z + 1, :].astype(jnp.float32)


def edges_kernel(sizes, first_a, first_b, cell_of, cell_slot, z_wall, pay_a, pay_b, positions):
    nx, nz = sizes
    x_place, z_place = lax.axis_index("gx"), lax.axis_index("gz")
    rows = Rows()
    weights = z_weights(rows)
    cell_rows = cell_slot.shape[0]
    slots = []
    for z in range(2):
        row_of = lax.shift_right_logical(cell_of[z : z + 1, :], 7)
        slot = jnp.zeros((1, LANES), jnp.int32)
        for step in (-1, 0, 1):
            row = (x_place // 4 + step) * nz + z_place
            row = jnp.clip(row, 0, cell_rows - 1)
            slot = jnp.where(row_of == row, cell_slot[pl.ds(row, 1), :], slot)
        slots.append(slot.astype(jnp.float32))
    row = lax.broadcasted_iota(jnp.int32, (8, LANES), 0)
    block = jnp.where(row == 0, slots[0], jnp.where(row == 1, slots[1], 0.0))
    positions[...] = block
    flip = jnp.where(x_place % 2 == 0, -1.0, 1.0)
    for first, pay, factor in ((first_a, pay_a, flip), (first_b, pay_b, -flip)):
        for i in range(X_SLOTS):
            pay[i] = first[i]
        pay[X_SLOTS] = block
        for z in range(2):
            weight, flag = wall_rows(sizes, rows, weights, z, z_wall)
            fields = [first[pl.ds(4 * f + 2 * z, 2)] for f in range(4)]
            terms = wall_terms(fields, 2, -1.0 if z == 0 else 1.0, weight, flag, False)
            normal, tangential = X_TRACES + 2 * z, X_TRACES + 8 + 2 * z
            pay[pl.ds(normal, 2)] = first[pl.ds(normal, 2)] + factor * terms[3]
            pay[pl.ds(tangential, 2)] = first[pl.ds(tangential, 2)] + terms[2]


def local_kernel(sizes, state, positions, target, x_wall, z_wall, logk, small, local, *z_pay):
    nx, nz = sizes
    z_place = lax.axis_index("gz")
    rows = Rows()
    derivative = Derivative(rows, derivative_matrix())
    weights = z_weights(rows)
    small[0] = positions[...]
    for side in range(2):
        small[1, X_WALL + 2 * side : X_WALL + 2 * side + 2, :] = x_wall[side].astype(jnp.float32)
    small[1, Z_WALL : Z_WALL + 2, :] = z_wall[...].astype(jnp.float32)
    small[1, LOGK : LOGK + 1, 0 : logk.shape[1]] = logk[...]
    for z in range(2):
        u = load(state, z)
        other = load(state, 1 - z)
        grads = [derivative.along(k, u[3]) for k in range(3)]
        divergence = sum(derivative.along(k, u[k]) for k in range(3))
        jumps = y_terms(u, rows, False)
        sign = 1 if z == 0 else -1
        across = z_terms(u, other, float(sign), weights[sign], False)
        weight, flag = wall_rows(sizes, rows, weights, z, z_wall)
        wall = wall_terms(u, 2, -float(sign), weight, flag, False)
        for f, (v, j, a, w) in enumerate(zip(grads + [divergence], jumps, across, wall)):
            local[z, f] = SCALE * v + j + a + w - target[z, f]
        first = sum(local[z, k] * u[k] for k in range(3))
        second = sum(u[k] * u[k] for k in range(3))
        small[SUMS, z : z + 1, :] = jnp.sum(first, axis=(0, 1, 2))[None]
        small[SUMS, 2 + z : 3 + z, :] = jnp.sum(second, axis=(0, 1, 2))[None]
    faces = [packed_face(rows, load(state, z), 2 * z - 1) for z in range(2)]
    for direction in range(len(z_pay)):
        upper = z_place == 0 if nz == 2 else direction == 0
        z_pay[direction][0:8] = jnp.where(upper, faces[1], faces[0]).reshape(8, 8, LANES)
        slot = jnp.where(upper, positions[1:2, :], positions[0:1, :])
        z_pay[direction][Z_SLOTS] = jnp.broadcast_to(slot, (8, LANES))


def x_side(side, even, got_a, got_b, block):
    a, b = got_a[pl.ds(block, 2)], got_b[pl.ds(block, 2)]
    return jnp.where(even, b, a) if side == 0 else jnp.where(even, a, b)


def sums_kernel(sizes, length, state, small, local, got_a, got_b, *refs):
    nx, nz = sizes
    count = 1 if nz == 2 else 2
    z_got, (whole, send), z_pay = refs[:count], refs[count : count + 2], refs[count + 2 :]
    z_from = [z_got[0], z_got[-1]]
    x_place, z_place = lax.axis_index("gx"), lax.axis_index("gz")
    even = x_place % 2 == 0
    rows = Rows()
    weights = z_weights(rows)
    corners = {}
    sums = []
    for z in range(2):
        u = load(state, z)
        for f in range(4):
            whole[z, f] = local[z, f]
        sign = -1 if z == 0 else 1
        inside = (z_place > 0) if z == 0 else (z_place < nz - 1)
        packed = z_from[z][0:8].reshape(4, 2, 8, LANES)
        terms = met_terms(u, packed, float(sign), weights[sign] * jnp.where(inside, 1.0, 0.0))
        for f in range(4):
            whole[z, f] += terms[f]
        total = sum(jnp.sum(terms[k] * u[k], axis=(0, 1)) for k in range(3))
        for side in range(2):
            sign = 1.0 if side else -1.0
            a = 3 * side
            end = (x_place == nx - 1) if side else (x_place == 0)
            mine = [u[f][a] for f in range(4)]
            theirs = [x_side(side, even, got_a, got_b, 4 * f + 2 * z) for f in range(4)]
            corners[side, z] = theirs
            flag = small[1, X_WALL + 2 * side + z : X_WALL + 2 * side + z + 1, :]
            inner = traces(mine, 0, -sign)
            image = (1.0 - 2.0 * flag) * (mine[0] + sign * mine[3])
            outer = [
                jnp.where(end, e, o)
                for e, o in zip(inner[:2] + [image], traces(theirs, 0, -sign))
            ]
            terms = face_terms(inner, outer, 0, sign, JUMP, False)
            for f in range(4):
                whole[z, f, a] += terms[f]
            total += sum(jnp.sum(terms[k] * mine[k], axis=0) for k in range(3))
        local_sum = small[SUMS, z : z + 1, :]
        sums.append((local_sum + jnp.sum(total, axis=0)[None], small[SUMS, 2 + z : 3 + z, :]))
    devices = send.shape[0]
    slots = small[0].astype(jnp.int32)
    place = lax.broadcasted_iota(jnp.int32, (LANES, LANES), 0)
    owner = lax.broadcasted_iota(jnp.int32, (devices, LANES), 0)
    chosen, values = [], []
    for z, (first, second) in enumerate(sums):
        slot = slots[z : z + 1, :]
        chosen.append(jnp.where(owner == slot // length, 1.0, 0.0).astype(jnp.bfloat16))
        position = slot % length
        value = jnp.where(
            place == position + length, first, jnp.where(place == position + 2 * length, second, 0.0)
        )
        for _ in range(3):
            piece = value.astype(jnp.bfloat16)
            values.append(piece)
            value = value - piece.astype(jnp.float32)
    send[...] = lax.dot_general(
        jnp.concatenate([chosen[0]] * 3 + [chosen[1]] * 3, axis=1),
        jnp.concatenate(values, axis=1),
        (((1,), (1,)), ((), ())),
        preferred_element_type=jnp.float32,
    )
    logk = small[1, LOGK : LOGK + 1, 0:length]
    send[:, 0:length] = jnp.broadcast_to(logk, (devices, length))
    faces = [packed_face(rows, load(whole, z), 2 * z - 1) for z in range(2)]
    edges = [[packed_face(rows, corners[side, z], 2 * z - 1) for z in range(2)] for side in range(2)]
    for direction in range(count):
        upper = z_place == 0 if nz == 2 else direction == 0
        z_pay[direction][0:8] = jnp.where(upper, faces[1], faces[0]).reshape(8, 8, LANES)
        for side in range(2):
            block = W_CORNERS + 2 * side
            z_pay[direction][block : block + 2] = jnp.where(upper, edges[side][1], edges[side][0])


def look_up(table, length, slots):
    devices = table.shape[0]
    fold = LANES // length
    table_rows = devices // fold
    chunk = min(8, table_rows)
    lane = lax.broadcasted_iota(jnp.int32, (chunk, LANES), 1)
    in_lane = slots & (LANES - 1)
    in_row = lax.shift_right_logical(slots, 7)

    def step(index, result):
        rows = jnp.zeros((chunk, LANES), jnp.float32)
        for j in range(fold):
            part = table[pl.ds(index * chunk * fold + j, chunk, stride=fold), :]
            rows += pltpu.roll(jnp.where(lane < length, part, 0.0), j * length, 1)
        for i in range(chunk):
            wide = jnp.broadcast_to(rows[i : i + 1, :], (8, LANES))
            taken = jnp.take_along_axis(wide, in_lane, axis=1)
            result = jnp.where(in_row == index * chunk + i, taken, result)
        return result

    result = jnp.zeros((8, LANES), jnp.float32)
    if table_rows == chunk:
        return step(0, result)
    return lax.fori_loop(0, table_rows // chunk, step, result)


def adjoint_kernel(sizes, length, state, small, whole, got_a, got_b, received, *refs):
    nx, nz = sizes
    count = 1 if nz == 2 else 2
    z_got, w_got, refs = refs[:count], refs[count : 2 * count], refs[2 * count :]
    adjoint_out, gradient_out, adjoint, gradient, done = refs
    z_from, w_from = [z_got[0], z_got[-1]], [w_got[0], w_got[-1]]
    x_place, z_place = lax.axis_index("gx"), lax.axis_index("gz")
    even = x_place % 2 == 0
    rows = Rows()
    weights = z_weights(rows)
    derivative = Derivative(rows, derivative_matrix().T)
    held = jnp.exp(-small[1, LOGK : LOGK + 1, 0:length])
    summed = jnp.sum(received[...], axis=0, keepdims=True)
    first, second = summed[:, length : 2 * length], summed[:, 2 * length : 3 * length]
    gradient[...] = -(SCALE / 64.0) * held * (first + SCALE * held * second)
    copies = [pltpu.make_async_copy(gradient, gradient_out, done.at[2])]
    copies[0].start()
    slot_a, slot_b = got_a[X_SLOTS], got_b[X_SLOTS]
    row = lax.broadcasted_iota(jnp.int32, (8, LANES), 0)
    slots = small[0]
    slots = jnp.where(row // 2 == 1, pltpu.roll(jnp.where(even, slot_b, slot_a), 2, 0), slots)
    slots = jnp.where(row // 2 == 2, pltpu.roll(jnp.where(even, slot_a, slot_b), 4, 0), slots)
    slots = jnp.where(row == 6, z_from[0][Z_SLOTS], slots)
    slots = jnp.where(row == 7, z_from[1][Z_SLOTS], slots)
    quarter = jnp.exp(-look_up(received, length, slots.astype(jnp.int32)))
    resistance = [quarter[i : i + 1, :] for i in range(8)]
    residual = []
    for z in range(2):
        scaled = SCALE * resistance[z]
        residual.append(
            [whole[z, k] + scaled * state[z, k] for k in range(3)] + [whole[z, 3]]
        )
    for z in range(2):
        w = residual[z]
        jumps = y_terms(w, rows, True)
        sign = 1 if z == 0 else -1
        across = z_terms(w, residual[1 - z], float(sign), weights[sign], True)
        sign = -sign
        end = (z_place == 0) if z == 0 else (z_place == nz - 1)
        scaled = SCALE * resistance[6 + z]
        theirs = unpacked_face(w_from[z][0:8].reshape(4, 2, 8, LANES), sign)
        fields = unpacked_face(z_from[z][0:8].reshape(4, 2, 8, LANES), sign)
        theirs = [theirs[k] + scaled * fields[k] for k in range(3)] + [theirs[3]]
        flag = small[1, Z_WALL + z : Z_WALL + z + 1, :]
        inner = traces(w, 2, -float(sign))
        outer = traces(theirs, 2, float(sign))
        image = inner[:2] + [(1.0 - 2.0 * flag) * inner[2]]
        outer = [jnp.where(end, i, o) for i, o in zip(image, outer)]
        beyond = face_terms(inner, outer, 2, float(sign), weights[sign], True)
        grads = [derivative.along(k, w[3]) for k in range(3)]
        divergence = sum(derivative.along(k, w[k]) for k in range(3))
        volume = [SCALE * (resistance[z] * w[k] + grads[k]) for k in range(3)]
        volume.append(SCALE * divergence)
        for f in range(4):
            adjoint[z, f] = volume[f] + jumps[f] + across[f] + beyond[f]
        for side in range(2):
            a = 3 * side
            s = 1.0 if side else -1.0
            u_out = [x_side(side, even, got_a, got_b, 4 * f + 2 * z) for f in range(4)]
            trace = [
                x_side(side, even, got_a, got_b, X_TRACES + 4 * j + 2 * z) for j in range(3)
            ]
            normal, tangential = trace[0], trace[1:]
            mine = traces([state[z, f, a] for f in range(4)], 0, s)
            there = traces(u_out, 0, s)
            normal = normal - (2.0 * JUMP) * (mine[2] - there[2])
            tangential = [t - JUMP * (m - o) for t, m, o in zip(tangential, mine[:2], there[:2])]
            t = float(sign)
            weight = weights[sign] * jnp.where(end, 0.0, 1.0)
            block = W_CORNERS + 2 * side
            edge = met_terms(u_out, w_from[z][block : block + 2], t, weight)
            normal = normal + edge[0] + s * edge[3]
            tangential = [tangential[0] + edge[1], tangential[1] + edge[2]]
            scaled = SCALE * resistance[2 + 2 * side + z]
            normal = normal + scaled * u_out[0]
            tangential = [v + scaled * u_out[1 + j] for j, v in enumerate(tangential)]
            inner = traces([w[f][a] for f in range(4)], 0, -s)
            flag = small[1, X_WALL + 2 * side + z : X_WALL + 2 * side + z + 1, :]
            image = inner[:2] + [(1.0 - 2.0 * flag) * inner[2]]
            last = (x_place == nx - 1) if side else (x_place == 0)
            outer = [jnp.where(last, i, o) for i, o in zip(image, tangential + [normal])]
            terms = face_terms(inner, outer, 0, s, JUMP, True)
            for f in range(4):
                adjoint[z, f, a] += terms[f]
        copies.append(pltpu.make_async_copy(adjoint.at[z], adjoint_out.at[z], done.at[z]))
        copies[-1].start()
    for copy in copies:
        copy.wait()


def call(kernel, operands, in_spec, shapes, out_spec, scratch, room):
    return pl.pallas_call(
        kernel,
        out_shape=[jax.ShapeDtypeStruct(shape, jnp.float32) for shape in shapes],
        in_specs=[in_spec] * len(operands),
        out_specs=[out_spec] * len(shapes),
        scratch_shapes=scratch,
        compiler_params=pltpu.CompilerParams(vmem_limit_bytes=room * 1024),
        cost_estimate=pl.CostEstimate(flops=2000000, bytes_accessed=800000, transcendentals=0),
    )(*operands)


def both_ways(pairs):
    return pairs + [(second, first) for first, second in pairs]


def along_z(payloads, nz):
    if nz == 2:
        return [lax.ppermute(payloads[0], "gz", [(0, 1), (1, 0)])]
    up = [(i, i + 1) for i in range(nz - 1)]
    down = [(second, first) for first, second in up]
    return [lax.ppermute(payloads[0], "gz", up), lax.ppermute(payloads[1], "gz", down)]


def shards(nx, nz, state, target, coarse_logk, cell_slot, cell_of, wall_flags_xaxis, z_wall):
    sizes = (nx, nz)
    shape = (2, 4, 4, 2, 8, LANES)
    length = coarse_logk.shape[0]
    state6, target6 = state.reshape(shape), target.reshape(shape)
    z_flags = z_wall.reshape(2, LANES)
    count = 1 if nz == 2 else 2
    x_shape, z_shape, w_shape = ((n, 8, LANES) for n in (X_BLOCKS, Z_BLOCKS, W_BLOCKS))
    held, first_a, first_b = call(
        faces_kernel,
        [state6, target6],
        HBM,
        [shape, x_shape, x_shape],
        VMEM,
        [pltpu.VMEM((2, 2, 4, 2, 8, LANES), jnp.float32), pltpu.SemaphoreType.DMA((3,))],
        54600,
    )
    pay_a, pay_b, positions = call(
        functools.partial(edges_kernel, sizes),
        [first_a, first_b, cell_of.reshape(2, LANES), cell_slot.reshape(-1, LANES), z_flags],
        VMEM,
        [x_shape, x_shape, (8, LANES)],
        VMEM,
        [],
        16 * 1024,
    )
    pairs_b = both_ways([(i, i + 1) for i in range(1, nx - 1, 2)])
    pairs_a = both_ways([(i, i + 1) for i in range(0, nx - 1, 2)])
    got_a = lax.ppermute(pay_a, "gx", pairs_a)
    got_b = lax.ppermute(pay_b, "gx", pairs_b)
    small, local, *z_pay = call(
        functools.partial(local_kernel, sizes),
        [held, positions, target6, wall_flags_xaxis, z_flags, coarse_logk.reshape(1, -1)],
        VMEM,
        [(3, 8, LANES), shape] + [z_shape] * count,
        VMEM,
        [],
        16 * 1024,
    )
    z_got = along_z(z_pay, nz)
    whole, send, *w_pay = call(
        functools.partial(sums_kernel, sizes, length),
        [held, small, local, got_a, got_b] + z_got,
        VMEM,
        [shape, (nx * nz, LANES)] + [w_shape] * count,
        VMEM,
        [],
        16 * 1024,
    )
    w_got = along_z(w_pay, nz)
    received = lax.all_to_all(send, ("gx", "gz"), 0, 0, tiled=True)
    adjoint, gradient = call(
        functools.partial(adjoint_kernel, sizes, length),
        [held, small, whole, got_a, got_b, received] + z_got + w_got,
        VMEM,
        [shape, (1, length)],
        HBM,
        [
            pltpu.VMEM(shape, jnp.float32),
            pltpu.VMEM((1, length), jnp.float32),
            pltpu.SemaphoreType.DMA((3,)),
        ],
        16 * 1024,
    )
    return adjoint.reshape(state.shape), gradient.reshape(-1)


def solution(mesh):
    placed = (
        P("gx", "gz", None, None, None),
        P("gx", "gz", None, None, None),
        P(("gx", "gz")),
        P(),
        P("gx", "gz", None),
        P(None, "gz", None),
        P(None, "gx", None),
    )
    return jax.shard_map(
        functools.partial(shards, mesh.shape["gx"], mesh.shape["gz"]),
        mesh=mesh,
        in_specs=placed,
        out_specs=(P("gx", "gz", None, None, None), P(("gx", "gz"))),
        check_vma=False,
    )
```

```python
import functools
import math

import jax
import jax.numpy as jnp
import numpy as np
from jax import lax
from jax.experimental import pallas as pl
from jax.experimental.pallas import tpu as pltpu
from jax.sharding import PartitionSpec as P

SCALE = 0.25
JUMP = 0.75
LANES = 128
VMEM = pl.BlockSpec(memory_space=pltpu.VMEM)
HBM = pl.BlockSpec(memory_space=pltpu.HBM)

X_FIELDS, X_TRACES, X_SLOTS, X_BLOCKS = 0, 16, 28, 29
Z_SLOTS, Z_BLOCKS = 8, 9
W_CORNERS, W_BLOCKS = 8, 12
X_WALL, Z_WALL, LOGK = 0, 4, 6
SUMS = 2


def derivative_matrix():
    points = np.array([-1.0, -math.sqrt(0.2), math.sqrt(0.2), 1.0])
    products = np.array(
        [
            np.prod([points[first] - points[other] for other in range(4) if other != first])
            for first in range(4)
        ]
    )
    matrix = np.zeros((4, 4))
    for first in range(4):
        for second in range(4):
            if first != second:
                matrix[first, second] = (
                    products[first] / products[second] / (points[first] - points[second])
                )
        matrix[first, first] = sum(
            (1.0 / (points[first] - points[other]) for other in range(4) if other != first)
        )
    return matrix


class Rows:
    def __init__(self):
        row = lax.broadcasted_iota(jnp.int32, (8, LANES), 0)
        self.upper = row >= 4
        self.c = row & 3

    def halves(self, low, high):
        return jnp.where(self.upper, jnp.float32(high), jnp.float32(low))

    def by_c(self, values):
        result = jnp.full((8, LANES), values[0], jnp.float32)
        for c in range(1, 4):
            result = jnp.where(self.c == c, jnp.float32(values[c]), result)
        return result


class Derivative:
    def __init__(self, rows, matrix):
        self.matrix = matrix
        self.same = [
            [rows.halves(matrix[2 * h, 2 * g], matrix[2 * h + 1, 2 * g + 1]) for g in range(2)]
            for h in range(2)
        ]
        self.cross = [
            [rows.halves(matrix[2 * h, 2 * g + 1], matrix[2 * h + 1, 2 * g]) for g in range(2)]
            for h in range(2)
        ]
        self.shift = {
            delta: rows.by_c(
                [matrix[c, c + delta] if 0 <= c + delta < 4 else 0.0 for c in range(4)]
            )
            for delta in range(-3, 4)
        }

    def across(self, a, u):
        return sum(float(self.matrix[a, j]) * u[j : j + 1] for j in range(4))

    def along(self, axis, u):
        if axis == 0:
            return jnp.concatenate([self.across(a, u) for a in range(4)])
        if axis == 1:
            swapped = pltpu.roll(u, 4, 2)
            return jnp.stack(
                [
                    sum(self.same[h][g] * u[:, g] + self.cross[h][g] * swapped[:, g] for g in range(2))
                    for h in range(2)
                ],
                axis=1,
            )
        return sum(
            coefficient * (u if delta == 0 else pltpu.roll(u, -delta % 8, 2))
            for delta, coefficient in self.shift.items()
        )


def traces(fields, axis, sign):
    others = [fields[f] for f in range(3) if f != axis]
    return others + [fields[axis] + sign * fields[3]]


def face_terms(inner, outer, axis, sign, weight, adjoint):
    tangential = [weight * (i - o) for i, o in zip(inner[:2], outer[:2])]
    normal = weight * (inner[2] - outer[2])
    if adjoint:
        pressure = (-sign) * (weight * (inner[2] + outer[2]))
    else:
        pressure = (-sign) * normal
    terms = tangential[:]
    terms.insert(axis, normal)
    return terms + [pressure]


def y_terms(fields, rows, adjoint):
    high_weight = rows.halves(0.0, JUMP)
    low_weight = rows.halves(JUMP, 0.0)
    first = [field[:, 0] for field in fields]
    second = [field[:, 1] for field in fields]
    moved = lambda value, step: pltpu.roll(pltpu.roll(value, 4, 1), step, 2)
    flip = 1.0 if adjoint else -1.0
    high_out = [moved(t, LANES - 1) for t in traces(first, 1, flip)]
    high = face_terms(traces(second, 1, -1.0), high_out, 1, 1.0, high_weight, adjoint)
    low_out = [moved(t, 1) for t in traces(second, 1, -flip)]
    low = face_terms(traces(first, 1, 1.0), low_out, 1, -1.0, low_weight, adjoint)
    return [jnp.stack([l, h], axis=1) for l, h in zip(low, high)]


def z_terms(inner, outer_fields, sign, weight, adjoint):
    flip = sign if adjoint else -sign
    outer = [pltpu.roll(t, 3 if sign > 0 else 5, t.ndim - 2) for t in traces(outer_fields, 2, flip)]
    return face_terms(traces(inner, 2, -sign), outer, 2, sign, weight, adjoint)


def packed_face(rows, fields, sign):
    c = 3 if sign > 0 else 0
    axis = fields[0].ndim - 2
    result = None
    for f, field in enumerate(fields):
        moved = field if f == c else pltpu.roll(field, (f - c) % 8, axis)
        result = moved if result is None else jnp.where(rows.c == f, moved, result)
    return result


def unpacked_face(packed, sign):
    c = 3 if sign > 0 else 0
    axis = packed.ndim - 2
    return [packed if f == c else pltpu.roll(packed, (c - f) % 8, axis) for f in range(4)]


def met_terms(inner, packed, sign, weight):
    outer = traces(unpacked_face(packed, sign), 2, -sign)
    return face_terms(traces(inner, 2, -sign), outer, 2, sign, weight, False)


def wall_terms(fields, axis, sign, weight, flag, adjoint):
    inner = traces(fields, axis, -sign)
    image = inner[2] if adjoint else fields[axis] + sign * fields[3]
    outer = inner[:2] + [(1.0 - 2.0 * flag) * image]
    return face_terms(inner, outer, axis, sign, weight, adjoint)


def z_weights(rows):
    return {-1: jnp.where(rows.c == 0, JUMP, 0.0), 1: jnp.where(rows.c == 3, JUMP, 0.0)}


def load(ref, z):
    return [ref[z, f] for f in range(4)]


def faces_kernel(state_in, target_in, state, pay_a, pay_b, target, arrived):
    copies = [pltpu.make_async_copy(state_in, state, arrived.at[0])]
    for side in range(2):
        copies.append(
            pltpu.make_async_copy(
                target_in.at[:, :, 3 * side], target.at[side], arrived.at[1 + side]
            )
        )
    for copy in copies:
        copy.start()
    even = lax.axis_index("gx") % 2 == 0
    rows = Rows()
    derivative = Derivative(rows, derivative_matrix())
    weights = z_weights(rows)
    for copy in copies:
        copy.wait()
    for z in range(2):
        sign = 1 if z == 0 else -1
        values = []
        for side in range(2):
            a = 3 * side
            u = [state[z, f, a : a + 1] for f in range(4)]
            other = [state[1 - z, f, a : a + 1] for f in range(4)]
            grads = [derivative.across(a, state[z, 3])]
            grads += [derivative.along(k, u[3]) for k in (1, 2)]
            divergence = derivative.across(a, state[z, 0])
            divergence += derivative.along(1, u[1]) + derivative.along(2, u[2])
            jumps = y_terms(u, rows, False)
            terms = z_terms(u, other, float(sign), weights[sign], False)
            result = [
                (SCALE * v + j + t)[0] - target[side, z, f]
                for f, (v, j, t) in enumerate(zip(grads + [divergence], jumps, terms))
            ]
            normal = result[0] - result[3] if side else result[0] + result[3]
            values.append([v[0] for v in u] + [normal, result[1], result[2]])
        low, high = values
        for j in range(7):
            pay_a[pl.ds(4 * j + 2 * z, 2)] = jnp.where(even, high[j], low[j])
            pay_b[pl.ds(4 * j + 2 * z, 2)] = jnp.where(even, low[j], high[j])


def wall_rows(sizes, rows, weights, z, flags):
    z_place = lax.axis_index("gz")
    end = (z_place == 0) if z == 0 else (z_place == sizes[1] - 1)
    weight = weights[-1 if z == 0 else 1] * jnp.where(end, 1.0, 0.0)
    return weight, flags[z : z + 1, :].astype(jnp.float32)


def edges_kernel(sizes, first_a, first_b, cell_of, cell_slot, z_wall, pay_a, pay_b, positions):
    nx, nz = sizes
    x_place, z_place = lax.axis_index("gx"), lax.axis_index("gz")
    rows = Rows()
    weights = z_weights(rows)
    cell_rows = cell_slot.shape[0]
    slots = []
    for z in range(2):
        row_of = lax.shift_right_logical(cell_of[z : z + 1, :], 7)
        slot = jnp.zeros((1, LANES), jnp.int32)
        for step in (-1, 0, 1):
            row = (x_place // 4 + step) * nz + z_place
            row = jnp.clip(row, 0, cell_rows - 1)
            slot = jnp.where(row_of == row, cell_slot[pl.ds(row, 1), :], slot)
        slots.append(slot.astype(jnp.float32))
    row = lax.broadcasted_iota(jnp.int32, (8, LANES), 0)
    block = jnp.where(row == 0, slots[0], jnp.where(row == 1, slots[1], 0.0))
    positions[...] = block
    flip = jnp.where(x_place % 2 == 0, -1.0, 1.0)
    for first, pay, factor in ((first_a, pay_a, flip), (first_b, pay_b, -flip)):
        for i in range(X_SLOTS):
            pay[i] = first[i]
        pay[X_SLOTS] = block
        for z in range(2):
            weight, flag = wall_rows(sizes, rows, weights, z, z_wall)
            fields = [first[pl.ds(4 * f + 2 * z, 2)] for f in range(4)]
            terms = wall_terms(fields, 2, -1.0 if z == 0 else 1.0, weight, flag, False)
            normal, tangential = X_TRACES + 2 * z, X_TRACES + 8 + 2 * z
            pay[pl.ds(normal, 2)] = first[pl.ds(normal, 2)] + factor * terms[3]
            pay[pl.ds(tangential, 2)] = first[pl.ds(tangential, 2)] + terms[2]


def local_kernel(sizes, state, positions, target, x_wall, z_wall, logk, small, local, *z_pay):
    nx, nz = sizes
    z_place = lax.axis_index("gz")
    rows = Rows()
    derivative = Derivative(rows, derivative_matrix())
    weights = z_weights(rows)
    small[0] = positions[...]
    for side in range(2):
        small[1, X_WALL + 2 * side : X_WALL + 2 * side + 2, :] = x_wall[side].astype(jnp.float32)
    small[1, Z_WALL : Z_WALL + 2, :] = z_wall[...].astype(jnp.float32)
    small[1, LOGK : LOGK + 1, 0 : logk.shape[1]] = logk[...]
    for z in range(2):
        u = load(state, z)
        other = load(state, 1 - z)
        grads = [derivative.along(k, u[3]) for k in range(3)]
        divergence = sum(derivative.along(k, u[k]) for k in range(3))
        jumps = y_terms(u, rows, False)
        sign = 1 if z == 0 else -1
        across = z_terms(u, other, float(sign), weights[sign], False)
        weight, flag = wall_rows(sizes, rows, weights, z, z_wall)
        wall = wall_terms(u, 2, -float(sign), weight, flag, False)
        for f, (v, j, a, w) in enumerate(zip(grads + [divergence], jumps, across, wall)):
            local[z, f] = SCALE * v + j + a + w - target[z, f]
        first = sum(local[z, k] * u[k] for k in range(3))
        second = sum(u[k] * u[k] for k in range(3))
        small[SUMS, z : z + 1, :] = jnp.sum(first, axis=(0, 1, 2))[None]
        small[SUMS, 2 + z : 3 + z, :] = jnp.sum(second, axis=(0, 1, 2))[None]
    faces = [packed_face(rows, load(state, z), 2 * z - 1) for z in range(2)]
    for direction in range(len(z_pay)):
        upper = z_place == 0 if nz == 2 else direction == 0
        z_pay[direction][0:8] = jnp.where(upper, faces[1], faces[0]).reshape(8, 8, LANES)
        slot = jnp.where(upper, positions[1:2, :], positions[0:1, :])
        z_pay[direction][Z_SLOTS] = jnp.broadcast_to(slot, (8, LANES))


def x_side(side, even, got_a, got_b, block):
    a, b = got_a[pl.ds(block, 2)], got_b[pl.ds(block, 2)]
    return jnp.where(even, b, a) if side == 0 else jnp.where(even, a, b)


def sums_kernel(sizes, length, state, small, local, got_a, got_b, *refs):
    nx, nz = sizes
    count = 1 if nz == 2 else 2
    z_got, (whole, send), z_pay = refs[:count], refs[count : count + 2], refs[count + 2 :]
    z_from = [z_got[0], z_got[-1]]
    x_place, z_place = lax.axis_index("gx"), lax.axis_index("gz")
    even = x_place % 2 == 0
    rows = Rows()
    weights = z_weights(rows)
    corners = {}
    sums = []
    for z in range(2):
        u = load(state, z)
        for f in range(4):
            whole[z, f] = local[z, f]
        sign = -1 if z == 0 else 1
        inside = (z_place > 0) if z == 0 else (z_place < nz - 1)
        packed = z_from[z][0:8].reshape(4, 2, 8, LANES)
        terms = met_terms(u, packed, float(sign), weights[sign] * jnp.where(inside, 1.0, 0.0))
        for f in range(4):
            whole[z, f] += terms[f]
        total = sum(jnp.sum(terms[k] * u[k], axis=(0, 1)) for k in range(3))
        for side in range(2):
            sign = 1.0 if side else -1.0
            a = 3 * side
            end = (x_place == nx - 1) if side else (x_place == 0)
            mine = [u[f][a] for f in range(4)]
            theirs = [x_side(side, even, got_a, got_b, 4 * f + 2 * z) for f in range(4)]
            corners[side, z] = theirs
            flag = small[1, X_WALL + 2 * side + z : X_WALL + 2 * side + z + 1, :]
            inner = traces(mine, 0, -sign)
            image = (1.0 - 2.0 * flag) * (mine[0] + sign * mine[3])
            outer = [
                jnp.where(end, e, o)
                for e, o in zip(inner[:2] + [image], traces(theirs, 0, -sign))
            ]
            terms = face_terms(inner, outer, 0, sign, JUMP, False)
            for f in range(4):
                whole[z, f, a] += terms[f]
            total += sum(jnp.sum(terms[k] * mine[k], axis=0) for k in range(3))
        local_sum = small[SUMS, z : z + 1, :]
        sums.append((local_sum + jnp.sum(total, axis=0)[None], small[SUMS, 2 + z : 3 + z, :]))
    devices = send.shape[0]
    slots = small[0].astype(jnp.int32)
    elements = 2 * LANES
    slot = jnp.concatenate([slots[0:1, :], slots[1:2, :]], axis=1)
    owner = lax.broadcasted_iota(jnp.int32, (devices, elements), 0)
    place = lax.broadcasted_iota(jnp.int32, (LANES, elements), 0) % length
    chosen = owner == slot // length
    position = jnp.where(place == slot % length, 1.0, 0.0).astype(jnp.bfloat16)
    pieces = []
    for parts in zip(*sums):
        value = jnp.where(chosen, jnp.concatenate(parts, axis=1), 0.0)
        for _ in range(3):
            piece = value.astype(jnp.bfloat16)
            pieces.append(piece)
            value = value - piece.astype(jnp.float32)
    placed = lax.dot_general(
        jnp.concatenate(pieces, axis=0),
        position,
        (((1,), (1,)), ((), ())),
        preferred_element_type=jnp.float32,
    )
    parts = [placed[i * devices : (i + 1) * devices] for i in range(6)]
    lane = lax.broadcasted_iota(jnp.int32, (devices, LANES), 1)
    first, second = parts[0] + parts[1] + parts[2], parts[3] + parts[4] + parts[5]
    send[...] = jnp.where(lane < 2 * length, first, second)
    logk = small[1, LOGK : LOGK + 1, 0:length]
    send[:, 0:length] = jnp.broadcast_to(logk, (devices, length))
    faces = [packed_face(rows, load(whole, z), 2 * z - 1) for z in range(2)]
    edges = [[packed_face(rows, corners[side, z], 2 * z - 1) for z in range(2)] for side in range(2)]
    for direction in range(count):
        upper = z_place == 0 if nz == 2 else direction == 0
        z_pay[direction][0:8] = jnp.where(upper, faces[1], faces[0]).reshape(8, 8, LANES)
        for side in range(2):
            block = W_CORNERS + 2 * side
            z_pay[direction][block : block + 2] = jnp.where(upper, edges[side][1], edges[side][0])


def look_up(table, length, slots):
    devices = table.shape[0]
    fold = LANES // length
    table_rows = devices // fold
    chunk = min(8, table_rows)
    lane = lax.broadcasted_iota(jnp.int32, (chunk, LANES), 1)
    in_lane = slots & (LANES - 1)
    in_row = lax.shift_right_logical(slots, 7)

    def step(index, result):
        rows = jnp.zeros((chunk, LANES), jnp.float32)
        for j in range(fold):
            part = table[pl.ds(index * chunk * fold + j, chunk, stride=fold), :]
            rows += pltpu.roll(jnp.where(lane < length, part, 0.0), j * length, 1)
        for i in range(chunk):
            wide = jnp.broadcast_to(rows[i : i + 1, :], (8, LANES))
            taken = jnp.take_along_axis(wide, in_lane, axis=1)
            result = jnp.where(in_row == index * chunk + i, taken, result)
        return result

    result = jnp.zeros((8, LANES), jnp.float32)
    if table_rows == chunk:
        return step(0, result)
    return lax.fori_loop(0, table_rows // chunk, step, result)


def adjoint_kernel(sizes, length, state, small, whole, got_a, got_b, received, *refs):
    nx, nz = sizes
    count = 1 if nz == 2 else 2
    z_got, w_got, refs = refs[:count], refs[count : 2 * count], refs[2 * count :]
    adjoint_out, gradient_out, adjoint, gradient, done = refs
    z_from, w_from = [z_got[0], z_got[-1]], [w_got[0], w_got[-1]]
    x_place, z_place = lax.axis_index("gx"), lax.axis_index("gz")
    even = x_place % 2 == 0
    rows = Rows()
    weights = z_weights(rows)
    derivative = Derivative(rows, derivative_matrix().T)
    held = jnp.exp(-small[1, LOGK : LOGK + 1, 0:length])
    summed = jnp.sum(received[...], axis=0, keepdims=True)
    first, second = summed[:, length : 2 * length], summed[:, 2 * length : 3 * length]
    gradient[...] = -(SCALE / 64.0) * held * (first + SCALE * held * second)
    copies = [pltpu.make_async_copy(gradient, gradient_out, done.at[2])]
    copies[0].start()
    slot_a, slot_b = got_a[X_SLOTS], got_b[X_SLOTS]
    row = lax.broadcasted_iota(jnp.int32, (8, LANES), 0)
    slots = small[0]
    slots = jnp.where(row // 2 == 1, pltpu.roll(jnp.where(even, slot_b, slot_a), 2, 0), slots)
    slots = jnp.where(row // 2 == 2, pltpu.roll(jnp.where(even, slot_a, slot_b), 4, 0), slots)
    slots = jnp.where(row == 6, z_from[0][Z_SLOTS], slots)
    slots = jnp.where(row == 7, z_from[1][Z_SLOTS], slots)
    quarter = jnp.exp(-look_up(received, length, slots.astype(jnp.int32)))
    resistance = [quarter[i : i + 1, :] for i in range(8)]
    residual = []
    for z in range(2):
        scaled = SCALE * resistance[z]
        residual.append(
            [whole[z, k] + scaled * state[z, k] for k in range(3)] + [whole[z, 3]]
        )
    for z in range(2):
        w = residual[z]
        jumps = y_terms(w, rows, True)
        sign = 1 if z == 0 else -1
        across = z_terms(w, residual[1 - z], float(sign), weights[sign], True)
        sign = -sign
        end = (z_place == 0) if z == 0 else (z_place == nz - 1)
        scaled = SCALE * resistance[6 + z]
        theirs = unpacked_face(w_from[z][0:8].reshape(4, 2, 8, LANES), sign)
        fields = unpacked_face(z_from[z][0:8].reshape(4, 2, 8, LANES), sign)
        theirs = [theirs[k] + scaled * fields[k] for k in range(3)] + [theirs[3]]
        flag = small[1, Z_WALL + z : Z_WALL + z + 1, :]
        inner = traces(w, 2, -float(sign))
        outer = traces(theirs, 2, float(sign))
        image = inner[:2] + [(1.0 - 2.0 * flag) * inner[2]]
        outer = [jnp.where(end, i, o) for i, o in zip(image, outer)]
        beyond = face_terms(inner, outer, 2, float(sign), weights[sign], True)
        grads = [derivative.along(k, w[3]) for k in range(3)]
        divergence = sum(derivative.along(k, w[k]) for k in range(3))
        volume = [SCALE * (resistance[z] * w[k] + grads[k]) for k in range(3)]
        volume.append(SCALE * divergence)
        for f in range(4):
            adjoint[z, f] = volume[f] + jumps[f] + across[f] + beyond[f]
        for side in range(2):
            a = 3 * side
            s = 1.0 if side else -1.0
            u_out = [x_side(side, even, got_a, got_b, 4 * f + 2 * z) for f in range(4)]
            trace = [
                x_side(side, even, got_a, got_b, X_TRACES + 4 * j + 2 * z) for j in range(3)
            ]
            normal, tangential = trace[0], trace[1:]
            mine = traces([state[z, f, a] for f in range(4)], 0, s)
            there = traces(u_out, 0, s)
            normal = normal - (2.0 * JUMP) * (mine[2] - there[2])
            tangential = [t - JUMP * (m - o) for t, m, o in zip(tangential, mine[:2], there[:2])]
            t = float(sign)
            weight = weights[sign] * jnp.where(end, 0.0, 1.0)
            block = W_CORNERS + 2 * side
            edge = met_terms(u_out, w_from[z][block : block + 2], t, weight)
            normal = normal + edge[0] + s * edge[3]
            tangential = [tangential[0] + edge[1], tangential[1] + edge[2]]
            scaled = SCALE * resistance[2 + 2 * side + z]
            normal = normal + scaled * u_out[0]
            tangential = [v + scaled * u_out[1 + j] for j, v in enumerate(tangential)]
            inner = traces([w[f][a] for f in range(4)], 0, -s)
            flag = small[1, X_WALL + 2 * side + z : X_WALL + 2 * side + z + 1, :]
            image = inner[:2] + [(1.0 - 2.0 * flag) * inner[2]]
            last = (x_place == nx - 1) if side else (x_place == 0)
            outer = [jnp.where(last, i, o) for i, o in zip(image, tangential + [normal])]
            terms = face_terms(inner, outer, 0, s, JUMP, True)
            for f in range(4):
                adjoint[z, f, a] += terms[f]
        copies.append(pltpu.make_async_copy(adjoint.at[z], adjoint_out.at[z], done.at[z]))
        copies[-1].start()
    for copy in copies:
        copy.wait()


def call(kernel, operands, in_spec, shapes, out_spec, scratch, room):
    return pl.pallas_call(
        kernel,
        out_shape=[jax.ShapeDtypeStruct(shape, jnp.float32) for shape in shapes],
        in_specs=[in_spec] * len(operands),
        out_specs=[out_spec] * len(shapes),
        scratch_shapes=scratch,
        compiler_params=pltpu.CompilerParams(vmem_limit_bytes=room * 1024),
        cost_estimate=pl.CostEstimate(flops=2000000, bytes_accessed=800000, transcendentals=0),
    )(*operands)


def both_ways(pairs):
    return pairs + [(second, first) for first, second in pairs]


def along_z(payloads, nz):
    if nz == 2:
        return [lax.ppermute(payloads[0], "gz", [(0, 1), (1, 0)])]
    up = [(i, i + 1) for i in range(nz - 1)]
    down = [(second, first) for first, second in up]
    return [lax.ppermute(payloads[0], "gz", up), lax.ppermute(payloads[1], "gz", down)]


def shards(nx, nz, state, target, coarse_logk, cell_slot, cell_of, wall_flags_xaxis, z_wall):
    sizes = (nx, nz)
    shape = (2, 4, 4, 2, 8, LANES)
    length = coarse_logk.shape[0]
    state6, target6 = state.reshape(shape), target.reshape(shape)
    z_flags = z_wall.reshape(2, LANES)
    count = 1 if nz == 2 else 2
    x_shape, z_shape, w_shape = ((n, 8, LANES) for n in (X_BLOCKS, Z_BLOCKS, W_BLOCKS))
    held, first_a, first_b = call(
        faces_kernel,
        [state6, target6],
        HBM,
        [shape, x_shape, x_shape],
        VMEM,
        [pltpu.VMEM((2, 2, 4, 2, 8, LANES), jnp.float32), pltpu.SemaphoreType.DMA((3,))],
        54600,
    )
    pay_a, pay_b, positions = call(
        functools.partial(edges_kernel, sizes),
        [first_a, first_b, cell_of.reshape(2, LANES), cell_slot.reshape(-1, LANES), z_flags],
        VMEM,
        [x_shape, x_shape, (8, LANES)],
        VMEM,
        [],
        16 * 1024,
    )
    pairs_b = both_ways([(i, i + 1) for i in range(1, nx - 1, 2)])
    pairs_a = both_ways([(i, i + 1) for i in range(0, nx - 1, 2)])
    got_a = lax.ppermute(pay_a, "gx", pairs_a)
    got_b = lax.ppermute(pay_b, "gx", pairs_b)
    small, local, *z_pay = call(
        functools.partial(local_kernel, sizes),
        [held, positions, target6, wall_flags_xaxis, z_flags, coarse_logk.reshape(1, -1)],
        VMEM,
        [(3, 8, LANES), shape] + [z_shape] * count,
        VMEM,
        [],
        16 * 1024,
    )
    z_got = along_z(z_pay, nz)
    whole, send, *w_pay = call(
        functools.partial(sums_kernel, sizes, length),
        [held, small, local, got_a, got_b] + z_got,
        VMEM,
        [shape, (nx * nz, LANES)] + [w_shape] * count,
        VMEM,
        [],
        16 * 1024,
    )
    w_got = along_z(w_pay, nz)
    received = lax.all_to_all(send, ("gx", "gz"), 0, 0, tiled=True)
    adjoint, gradient = call(
        functools.partial(adjoint_kernel, sizes, length),
        [held, small, whole, got_a, got_b, received] + z_got + w_got,
        VMEM,
        [shape, (1, length)],
        HBM,
        [
            pltpu.VMEM(shape, jnp.float32),
            pltpu.VMEM((1, length), jnp.float32),
            pltpu.SemaphoreType.DMA((3,)),
        ],
        16 * 1024,
    )
    return adjoint.reshape(state.shape), gradient.reshape(-1)


def solution(mesh):
    placed = (
        P("gx", "gz", None, None, None),
        P("gx", "gz", None, None, None),
        P(("gx", "gz")),
        P(),
        P("gx", "gz", None),
        P(None, "gz", None),
        P(None, "gx", None),
    )
    return jax.shard_map(
        functools.partial(shards, mesh.shape["gx"], mesh.shape["gz"]),
        mesh=mesh,
        in_specs=placed,
        out_specs=(P("gx", "gz", None, None, None), P(("gx", "gz"))),
        check_vma=False,
    )
```

```python
import functools
import math

import jax
import jax.numpy as jnp
import numpy as np
from jax import lax
from jax.experimental import pallas as pl
from jax.experimental.pallas import tpu as pltpu
from jax.sharding import PartitionSpec as P

SCALE = 0.25
JUMP = 0.75
LANES = 128
VMEM = pl.BlockSpec(memory_space=pltpu.VMEM)
HBM = pl.BlockSpec(memory_space=pltpu.HBM)

X_FIELDS, X_TRACES, X_SLOTS, X_BLOCKS = 0, 16, 28, 29
Z_SLOTS, Z_BLOCKS = 8, 9
W_CORNERS, W_BLOCKS = 8, 12
X_WALL, Z_WALL, LOGK = 0, 4, 6
SUMS = 2


def derivative_matrix():
    points = np.array([-1.0, -math.sqrt(0.2), math.sqrt(0.2), 1.0])
    products = np.array(
        [
            np.prod([points[first] - points[other] for other in range(4) if other != first])
            for first in range(4)
        ]
    )
    matrix = np.zeros((4, 4))
    for first in range(4):
        for second in range(4):
            if first != second:
                matrix[first, second] = (
                    products[first] / products[second] / (points[first] - points[second])
                )
        matrix[first, first] = sum(
            (1.0 / (points[first] - points[other]) for other in range(4) if other != first)
        )
    return matrix


class Rows:
    def __init__(self):
        row = lax.broadcasted_iota(jnp.int32, (8, LANES), 0)
        self.upper = row >= 4
        self.c = row & 3

    def halves(self, low, high):
        return jnp.where(self.upper, jnp.float32(high), jnp.float32(low))

    def by_c(self, values):
        result = jnp.full((8, LANES), values[0], jnp.float32)
        for c in range(1, 4):
            result = jnp.where(self.c == c, jnp.float32(values[c]), result)
        return result


class Derivative:
    def __init__(self, rows, matrix):
        self.matrix = matrix
        self.same = [
            [rows.halves(matrix[2 * h, 2 * g], matrix[2 * h + 1, 2 * g + 1]) for g in range(2)]
            for h in range(2)
        ]
        self.cross = [
            [rows.halves(matrix[2 * h, 2 * g + 1], matrix[2 * h + 1, 2 * g]) for g in range(2)]
            for h in range(2)
        ]
        self.shift = {
            delta: rows.by_c(
                [matrix[c, c + delta] if 0 <= c + delta < 4 else 0.0 for c in range(4)]
            )
            for delta in range(-3, 4)
        }

    def across(self, a, u):
        return sum(float(self.matrix[a, j]) * u[j : j + 1] for j in range(4))

    def along(self, axis, u):
        if axis == 0:
            return jnp.concatenate([self.across(a, u) for a in range(4)])
        if axis == 1:
            swapped = pltpu.roll(u, 4, 2)
            return jnp.stack(
                [
                    sum(self.same[h][g] * u[:, g] + self.cross[h][g] * swapped[:, g] for g in range(2))
                    for h in range(2)
                ],
                axis=1,
            )
        return sum(
            coefficient * (u if delta == 0 else pltpu.roll(u, -delta % 8, 2))
            for delta, coefficient in self.shift.items()
        )


def traces(fields, axis, sign):
    others = [fields[f] for f in range(3) if f != axis]
    return others + [fields[axis] + sign * fields[3]]


def face_terms(inner, outer, axis, sign, weight, adjoint):
    tangential = [weight * (i - o) for i, o in zip(inner[:2], outer[:2])]
    normal = weight * (inner[2] - outer[2])
    if adjoint:
        pressure = (-sign) * (weight * (inner[2] + outer[2]))
    else:
        pressure = (-sign) * normal
    terms = tangential[:]
    terms.insert(axis, normal)
    return terms + [pressure]


def y_terms(fields, rows, adjoint):
    high_weight = rows.halves(0.0, JUMP)
    low_weight = rows.halves(JUMP, 0.0)
    first = [field[:, 0] for field in fields]
    second = [field[:, 1] for field in fields]
    moved = lambda value, step: pltpu.roll(pltpu.roll(value, 4, 1), step, 2)
    flip = 1.0 if adjoint else -1.0
    high_out = [moved(t, LANES - 1) for t in traces(first, 1, flip)]
    high = face_terms(traces(second, 1, -1.0), high_out, 1, 1.0, high_weight, adjoint)
    low_out = [moved(t, 1) for t in traces(second, 1, -flip)]
    low = face_terms(traces(first, 1, 1.0), low_out, 1, -1.0, low_weight, adjoint)
    return [jnp.stack([l, h], axis=1) for l, h in zip(low, high)]


def z_terms(inner, outer_fields, sign, weight, adjoint):
    flip = sign if adjoint else -sign
    outer = [pltpu.roll(t, 3 if sign > 0 else 5, t.ndim - 2) for t in traces(outer_fields, 2, flip)]
    return face_terms(traces(inner, 2, -sign), outer, 2, sign, weight, adjoint)


def packed_face(rows, fields, sign):
    c = 3 if sign > 0 else 0
    axis = fields[0].ndim - 2
    result = None
    for f, field in enumerate(fields):
        moved = field if f == c else pltpu.roll(field, (f - c) % 8, axis)
        result = moved if result is None else jnp.where(rows.c == f, moved, result)
    return result


def unpacked_face(packed, sign):
    c = 3 if sign > 0 else 0
    axis = packed.ndim - 2
    return [packed if f == c else pltpu.roll(packed, (c - f) % 8, axis) for f in range(4)]


def met_terms(inner, packed, sign, weight):
    outer = traces(unpacked_face(packed, sign), 2, -sign)
    return face_terms(traces(inner, 2, -sign), outer, 2, sign, weight, False)


def wall_terms(fields, axis, sign, weight, flag, adjoint):
    inner = traces(fields, axis, -sign)
    image = inner[2] if adjoint else fields[axis] + sign * fields[3]
    outer = inner[:2] + [(1.0 - 2.0 * flag) * image]
    return face_terms(inner, outer, axis, sign, weight, adjoint)


def z_weights(rows):
    return {-1: jnp.where(rows.c == 0, JUMP, 0.0), 1: jnp.where(rows.c == 3, JUMP, 0.0)}


def load(ref, z):
    return [ref[z, f] for f in range(4)]


def faces_kernel(state_in, target_in, state, pay_a, pay_b, target, arrived):
    copies = [pltpu.make_async_copy(state_in, state, arrived.at[0])]
    for side in range(2):
        copies.append(
            pltpu.make_async_copy(
                target_in.at[:, :, 3 * side], target.at[side], arrived.at[1 + side]
            )
        )
    for copy in copies:
        copy.start()
    even = lax.axis_index("gx") % 2 == 0
    rows = Rows()
    derivative = Derivative(rows, derivative_matrix())
    weights = z_weights(rows)
    for copy in copies:
        copy.wait()
    for z in range(2):
        sign = 1 if z == 0 else -1
        values = []
        for side in range(2):
            a = 3 * side
            u = [state[z, f, a : a + 1] for f in range(4)]
            other = [state[1 - z, f, a : a + 1] for f in range(4)]
            grads = [derivative.across(a, state[z, 3])]
            grads += [derivative.along(k, u[3]) for k in (1, 2)]
            divergence = derivative.across(a, state[z, 0])
            divergence += derivative.along(1, u[1]) + derivative.along(2, u[2])
            jumps = y_terms(u, rows, False)
            terms = z_terms(u, other, float(sign), weights[sign], False)
            result = [
                (SCALE * v + j + t)[0] - target[side, z, f]
                for f, (v, j, t) in enumerate(zip(grads + [divergence], jumps, terms))
            ]
            normal = result[0] - result[3] if side else result[0] + result[3]
            values.append([v[0] for v in u] + [normal, result[1], result[2]])
        low, high = values
        for j in range(7):
            pay_a[pl.ds(4 * j + 2 * z, 2)] = jnp.where(even, high[j], low[j])
            pay_b[pl.ds(4 * j + 2 * z, 2)] = jnp.where(even, low[j], high[j])


def wall_rows(sizes, rows, weights, z, flags):
    z_place = lax.axis_index("gz")
    end = (z_place == 0) if z == 0 else (z_place == sizes[1] - 1)
    weight = weights[-1 if z == 0 else 1] * jnp.where(end, 1.0, 0.0)
    return weight, flags[z : z + 1, :].astype(jnp.float32)


def edges_kernel(sizes, first_a, first_b, cell_of, cell_slot, z_wall, pay_a, pay_b, positions):
    nx, nz = sizes
    x_place, z_place = lax.axis_index("gx"), lax.axis_index("gz")
    rows = Rows()
    weights = z_weights(rows)
    cell_rows = cell_slot.shape[0]
    slots = []
    for z in range(2):
        row_of = lax.shift_right_logical(cell_of[z : z + 1, :], 7)
        slot = jnp.zeros((1, LANES), jnp.int32)
        for step in (-1, 0, 1):
            row = (x_place // 4 + step) * nz + z_place
            row = jnp.clip(row, 0, cell_rows - 1)
            slot = jnp.where(row_of == row, cell_slot[pl.ds(row, 1), :], slot)
        slots.append(slot.astype(jnp.float32))
    row = lax.broadcasted_iota(jnp.int32, (8, LANES), 0)
    block = jnp.where(row == 0, slots[0], jnp.where(row == 1, slots[1], 0.0))
    positions[...] = block
    flip = jnp.where(x_place % 2 == 0, -1.0, 1.0)
    for first, pay, factor in ((first_a, pay_a, flip), (first_b, pay_b, -flip)):
        for i in range(X_SLOTS):
            pay[i] = first[i]
        pay[X_SLOTS] = block
        for z in range(2):
            weight, flag = wall_rows(sizes, rows, weights, z, z_wall)
            fields = [first[pl.ds(4 * f + 2 * z, 2)] for f in range(4)]
            terms = wall_terms(fields, 2, -1.0 if z == 0 else 1.0, weight, flag, False)
            normal, tangential = X_TRACES + 2 * z, X_TRACES + 8 + 2 * z
            pay[pl.ds(normal, 2)] = first[pl.ds(normal, 2)] + factor * terms[3]
            pay[pl.ds(tangential, 2)] = first[pl.ds(tangential, 2)] + terms[2]


def local_kernel(sizes, state, positions, target, x_wall, z_wall, logk, small, local, *z_pay):
    nx, nz = sizes
    z_place = lax.axis_index("gz")
    rows = Rows()
    derivative = Derivative(rows, derivative_matrix())
    weights = z_weights(rows)
    small[0] = positions[...]
    for side in range(2):
        small[1, X_WALL + 2 * side : X_WALL + 2 * side + 2, :] = x_wall[side].astype(jnp.float32)
    small[1, Z_WALL : Z_WALL + 2, :] = z_wall[...].astype(jnp.float32)
    small[1, LOGK : LOGK + 1, 0 : logk.shape[1]] = logk[...]
    for z in range(2):
        u = load(state, z)
        other = load(state, 1 - z)
        grads = [derivative.along(k, u[3]) for k in range(3)]
        divergence = sum(derivative.along(k, u[k]) for k in range(3))
        jumps = y_terms(u, rows, False)
        sign = 1 if z == 0 else -1
        across = z_terms(u, other, float(sign), weights[sign], False)
        weight, flag = wall_rows(sizes, rows, weights, z, z_wall)
        wall = wall_terms(u, 2, -float(sign), weight, flag, False)
        for f, (v, j, a, w) in enumerate(zip(grads + [divergence], jumps, across, wall)):
            local[z, f] = SCALE * v + j + a + w - target[z, f]
        first = sum(local[z, k] * u[k] for k in range(3))
        second = sum(u[k] * u[k] for k in range(3))
        small[SUMS, z : z + 1, :] = jnp.sum(first, axis=(0, 1, 2))[None]
        small[SUMS, 2 + z : 3 + z, :] = jnp.sum(second, axis=(0, 1, 2))[None]
    faces = [packed_face(rows, load(state, z), 2 * z - 1) for z in range(2)]
    for direction in range(len(z_pay)):
        upper = z_place == 0 if nz == 2 else direction == 0
        z_pay[direction][0:8] = jnp.where(upper, faces[1], faces[0]).reshape(8, 8, LANES)
        slot = jnp.where(upper, positions[1:2, :], positions[0:1, :])
        z_pay[direction][Z_SLOTS] = jnp.broadcast_to(slot, (8, LANES))


def x_side(side, even, got_a, got_b, block):
    a, b = got_a[pl.ds(block, 2)], got_b[pl.ds(block, 2)]
    return jnp.where(even, b, a) if side == 0 else jnp.where(even, a, b)


def sums_kernel(sizes, length, state, small, local, got_a, got_b, *refs):
    nx, nz = sizes
    count = 1 if nz == 2 else 2
    z_got, (whole, send), z_pay = refs[:count], refs[count : count + 2], refs[count + 2 :]
    z_from = [z_got[0], z_got[-1]]
    x_place, z_place = lax.axis_index("gx"), lax.axis_index("gz")
    even = x_place % 2 == 0
    rows = Rows()
    weights = z_weights(rows)
    corners = {}
    sums = []
    for z in range(2):
        u = load(state, z)
        for f in range(4):
            whole[z, f] = local[z, f]
        sign = -1 if z == 0 else 1
        inside = (z_place > 0) if z == 0 else (z_place < nz - 1)
        packed = z_from[z][0:8].reshape(4, 2, 8, LANES)
        terms = met_terms(u, packed, float(sign), weights[sign] * jnp.where(inside, 1.0, 0.0))
        for f in range(4):
            whole[z, f] += terms[f]
        total = sum(jnp.sum(terms[k] * u[k], axis=(0, 1)) for k in range(3))
        for side in range(2):
            sign = 1.0 if side else -1.0
            a = 3 * side
            end = (x_place == nx - 1) if side else (x_place == 0)
            mine = [u[f][a] for f in range(4)]
            theirs = [x_side(side, even, got_a, got_b, 4 * f + 2 * z) for f in range(4)]
            corners[side, z] = theirs
            flag = small[1, X_WALL + 2 * side + z : X_WALL + 2 * side + z + 1, :]
            inner = traces(mine, 0, -sign)
            image = (1.0 - 2.0 * flag) * (mine[0] + sign * mine[3])
            outer = [
                jnp.where(end, e, o)
                for e, o in zip(inner[:2] + [image], traces(theirs, 0, -sign))
            ]
            terms = face_terms(inner, outer, 0, sign, JUMP, False)
            for f in range(4):
                whole[z, f, a] += terms[f]
            total += sum(jnp.sum(terms[k] * mine[k], axis=0) for k in range(3))
        local_sum = small[SUMS, z : z + 1, :]
        sums.append((local_sum + jnp.sum(total, axis=0)[None], small[SUMS, 2 + z : 3 + z, :]))
    devices = send.shape[0]
    slots = small[0].astype(jnp.int32)
    elements = 2 * LANES
    slot = jnp.concatenate([slots[0:1, :], slots[1:2, :]], axis=1)
    owner = lax.broadcasted_iota(jnp.int32, (devices, elements), 0)
    place = lax.broadcasted_iota(jnp.int32, (LANES, elements), 0) % length
    chosen = owner == slot // length
    position = jnp.where(place == slot % length, 1.0, 0.0).astype(jnp.bfloat16)
    pieces = []
    for parts in zip(*sums):
        value = jnp.where(chosen, jnp.concatenate(parts, axis=1), 0.0)
        for _ in range(3):
            piece = value.astype(jnp.bfloat16)
            pieces.append(piece)
            value = value - piece.astype(jnp.float32)
    placed = lax.dot_general(
        jnp.concatenate(pieces, axis=0),
        position,
        (((1,), (1,)), ((), ())),
        preferred_element_type=jnp.float32,
    )
    parts = [placed[i * devices : (i + 1) * devices] for i in range(6)]
    lane = lax.broadcasted_iota(jnp.int32, (devices, LANES), 1)
    first, second = parts[0] + parts[1] + parts[2], parts[3] + parts[4] + parts[5]
    send[...] = jnp.where(lane < 2 * length, first, second)
    logk = small[1, LOGK : LOGK + 1, 0:length]
    send[:, 0:length] = jnp.broadcast_to(logk, (devices, length))
    faces = [packed_face(rows, load(whole, z), 2 * z - 1) for z in range(2)]
    edges = [[packed_face(rows, corners[side, z], 2 * z - 1) for z in range(2)] for side in range(2)]
    for direction in range(count):
        upper = z_place == 0 if nz == 2 else direction == 0
        z_pay[direction][0:8] = jnp.where(upper, faces[1], faces[0]).reshape(8, 8, LANES)
        for side in range(2):
            block = W_CORNERS + 2 * side
            z_pay[direction][block : block + 2] = jnp.where(upper, edges[side][1], edges[side][0])


def look_up(table, length, slots):
    devices = table.shape[0]
    fold = LANES // length
    table_rows = devices // fold
    chunk = min(8, table_rows)
    lane = lax.broadcasted_iota(jnp.int32, (chunk, LANES), 1)
    in_lane = slots & (LANES - 1)
    in_row = lax.shift_right_logical(slots, 7)

    def step(index, result):
        rows = jnp.zeros((chunk, LANES), jnp.float32)
        for j in range(fold):
            part = table[pl.ds(index * chunk * fold + j, chunk, stride=fold), :]
            rows += pltpu.roll(jnp.where(lane < length, part, 0.0), j * length, 1)
        for i in range(chunk):
            wide = jnp.broadcast_to(rows[i : i + 1, :], (8, LANES))
            taken = jnp.take_along_axis(wide, in_lane, axis=1)
            result = jnp.where(in_row == index * chunk + i, taken, result)
        return result

    result = jnp.zeros((8, LANES), jnp.float32)
    if table_rows == chunk:
        return step(0, result)
    return lax.fori_loop(0, table_rows // chunk, step, result)


def adjoint_kernel(sizes, length, state, small, whole, got_a, got_b, received, *refs):
    nx, nz = sizes
    count = 1 if nz == 2 else 2
    z_got, w_got, refs = refs[:count], refs[count : 2 * count], refs[2 * count :]
    adjoint_out, gradient_out, adjoint, gradient, done = refs
    z_from, w_from = [z_got[0], z_got[-1]], [w_got[0], w_got[-1]]
    x_place, z_place = lax.axis_index("gx"), lax.axis_index("gz")
    even = x_place % 2 == 0
    rows = Rows()
    weights = z_weights(rows)
    derivative = Derivative(rows, derivative_matrix().T)
    copies = []
    slot_a, slot_b = got_a[X_SLOTS], got_b[X_SLOTS]
    row = lax.broadcasted_iota(jnp.int32, (8, LANES), 0)
    slots = small[0]
    slots = jnp.where(row // 2 == 1, pltpu.roll(jnp.where(even, slot_b, slot_a), 2, 0), slots)
    slots = jnp.where(row // 2 == 2, pltpu.roll(jnp.where(even, slot_a, slot_b), 4, 0), slots)
    slots = jnp.where(row == 6, z_from[0][Z_SLOTS], slots)
    slots = jnp.where(row == 7, z_from[1][Z_SLOTS], slots)
    quarter = jnp.exp(-look_up(received, length, slots.astype(jnp.int32)))
    resistance = [quarter[i : i + 1, :] for i in range(8)]
    residual = []
    for z in range(2):
        scaled = SCALE * resistance[z]
        residual.append(
            [whole[z, k] + scaled * state[z, k] for k in range(3)] + [whole[z, 3]]
        )
    for z in range(2):
        w = residual[z]
        jumps = y_terms(w, rows, True)
        sign = 1 if z == 0 else -1
        across = z_terms(w, residual[1 - z], float(sign), weights[sign], True)
        sign = -sign
        end = (z_place == 0) if z == 0 else (z_place == nz - 1)
        scaled = SCALE * resistance[6 + z]
        theirs = unpacked_face(w_from[z][0:8].reshape(4, 2, 8, LANES), sign)
        fields = unpacked_face(z_from[z][0:8].reshape(4, 2, 8, LANES), sign)
        theirs = [theirs[k] + scaled * fields[k] for k in range(3)] + [theirs[3]]
        flag = small[1, Z_WALL + z : Z_WALL + z + 1, :]
        inner = traces(w, 2, -float(sign))
        outer = traces(theirs, 2, float(sign))
        image = inner[:2] + [(1.0 - 2.0 * flag) * inner[2]]
        outer = [jnp.where(end, i, o) for i, o in zip(image, outer)]
        beyond = face_terms(inner, outer, 2, float(sign), weights[sign], True)
        grads = [derivative.along(k, w[3]) for k in range(3)]
        divergence = sum(derivative.along(k, w[k]) for k in range(3))
        volume = [SCALE * (resistance[z] * w[k] + grads[k]) for k in range(3)]
        volume.append(SCALE * divergence)
        for f in range(4):
            adjoint[z, f] = volume[f] + jumps[f] + across[f] + beyond[f]
        for side in range(2):
            a = 3 * side
            s = 1.0 if side else -1.0
            u_out = [x_side(side, even, got_a, got_b, 4 * f + 2 * z) for f in range(4)]
            trace = [
                x_side(side, even, got_a, got_b, X_TRACES + 4 * j + 2 * z) for j in range(3)
            ]
            normal, tangential = trace[0], trace[1:]
            mine = traces([state[z, f, a] for f in range(4)], 0, s)
            there = traces(u_out, 0, s)
            normal = normal - (2.0 * JUMP) * (mine[2] - there[2])
            tangential = [t - JUMP * (m - o) for t, m, o in zip(tangential, mine[:2], there[:2])]
            t = float(sign)
            weight = weights[sign] * jnp.where(end, 0.0, 1.0)
            block = W_CORNERS + 2 * side
            edge = met_terms(u_out, w_from[z][block : block + 2], t, weight)
            normal = normal + edge[0] + s * edge[3]
            tangential = [tangential[0] + edge[1], tangential[1] + edge[2]]
            scaled = SCALE * resistance[2 + 2 * side + z]
            normal = normal + scaled * u_out[0]
            tangential = [v + scaled * u_out[1 + j] for j, v in enumerate(tangential)]
            inner = traces([w[f][a] for f in range(4)], 0, -s)
            flag = small[1, X_WALL + 2 * side + z : X_WALL + 2 * side + z + 1, :]
            image = inner[:2] + [(1.0 - 2.0 * flag) * inner[2]]
            last = (x_place == nx - 1) if side else (x_place == 0)
            outer = [jnp.where(last, i, o) for i, o in zip(image, tangential + [normal])]
            terms = face_terms(inner, outer, 0, s, JUMP, True)
            for f in range(4):
                adjoint[z, f, a] += terms[f]
        copies.append(pltpu.make_async_copy(adjoint.at[z], adjoint_out.at[z], done.at[z]))
        copies[-1].start()
        if z == 0:
            held = jnp.exp(-small[1, LOGK : LOGK + 1, 0:length])
            summed = jnp.sum(received[...], axis=0, keepdims=True)
            first, second = summed[:, length : 2 * length], summed[:, 2 * length : 3 * length]
            gradient[...] = -(SCALE / 64.0) * held * (first + SCALE * held * second)
            copies.append(pltpu.make_async_copy(gradient, gradient_out, done.at[2]))
            copies[-1].start()
    for copy in copies:
        copy.wait()


def call(kernel, operands, in_spec, shapes, out_spec, scratch, room):
    return pl.pallas_call(
        kernel,
        out_shape=[jax.ShapeDtypeStruct(shape, jnp.float32) for shape in shapes],
        in_specs=[in_spec] * len(operands),
        out_specs=[out_spec] * len(shapes),
        scratch_shapes=scratch,
        compiler_params=pltpu.CompilerParams(vmem_limit_bytes=room * 1024),
        cost_estimate=pl.CostEstimate(flops=2000000, bytes_accessed=800000, transcendentals=0),
    )(*operands)


def both_ways(pairs):
    return pairs + [(second, first) for first, second in pairs]


def along_z(payloads, nz):
    if nz == 2:
        return [lax.ppermute(payloads[0], "gz", [(0, 1), (1, 0)])]
    up = [(i, i + 1) for i in range(nz - 1)]
    down = [(second, first) for first, second in up]
    return [lax.ppermute(payloads[0], "gz", up), lax.ppermute(payloads[1], "gz", down)]


def shards(nx, nz, state, target, coarse_logk, cell_slot, cell_of, wall_flags_xaxis, z_wall):
    sizes = (nx, nz)
    shape = (2, 4, 4, 2, 8, LANES)
    length = coarse_logk.shape[0]
    state6, target6 = state.reshape(shape), target.reshape(shape)
    z_flags = z_wall.reshape(2, LANES)
    count = 1 if nz == 2 else 2
    x_shape, z_shape, w_shape = ((n, 8, LANES) for n in (X_BLOCKS, Z_BLOCKS, W_BLOCKS))
    held, first_a, first_b = call(
        faces_kernel,
        [state6, target6],
        HBM,
        [shape, x_shape, x_shape],
        VMEM,
        [pltpu.VMEM((2, 2, 4, 2, 8, LANES), jnp.float32), pltpu.SemaphoreType.DMA((3,))],
        54600,
    )
    pay_a, pay_b, positions = call(
        functools.partial(edges_kernel, sizes),
        [first_a, first_b, cell_of.reshape(2, LANES), cell_slot.reshape(-1, LANES), z_flags],
        VMEM,
        [x_shape, x_shape, (8, LANES)],
        VMEM,
        [],
        16 * 1024,
    )
    pairs_b = both_ways([(i, i + 1) for i in range(1, nx - 1, 2)])
    pairs_a = both_ways([(i, i + 1) for i in range(0, nx - 1, 2)])
    got_a = lax.ppermute(pay_a, "gx", pairs_a)
    got_b = lax.ppermute(pay_b, "gx", pairs_b)
    small, local, *z_pay = call(
        functools.partial(local_kernel, sizes),
        [held, positions, target6, wall_flags_xaxis, z_flags, coarse_logk.reshape(1, -1)],
        VMEM,
        [(3, 8, LANES), shape] + [z_shape] * count,
        VMEM,
        [],
        16 * 1024,
    )
    z_got = along_z(z_pay, nz)
    whole, send, *w_pay = call(
        functools.partial(sums_kernel, sizes, length),
        [held, small, local, got_a, got_b] + z_got,
        VMEM,
        [shape, (nx * nz, LANES)] + [w_shape] * count,
        VMEM,
        [],
        16 * 1024,
    )
    w_got = along_z(w_pay, nz)
    received = lax.all_to_all(send, ("gx", "gz"), 0, 0, tiled=True)
    adjoint, gradient = call(
        functools.partial(adjoint_kernel, sizes, length),
        [held, small, whole, got_a, got_b, received] + z_got + w_got,
        VMEM,
        [shape, (1, length)],
        HBM,
        [
            pltpu.VMEM(shape, jnp.float32),
            pltpu.VMEM((1, length), jnp.float32),
            pltpu.SemaphoreType.DMA((3,)),
        ],
        16 * 1024,
    )
    return adjoint.reshape(state.shape), gradient.reshape(-1)


def solution(mesh):
    placed = (
        P("gx", "gz", None, None, None),
        P("gx", "gz", None, None, None),
        P(("gx", "gz")),
        P(),
        P("gx", "gz", None),
        P(None, "gz", None),
        P(None, "gx", None),
    )
    return jax.shard_map(
        functools.partial(shards, mesh.shape["gx"], mesh.shape["gz"]),
        mesh=mesh,
        in_specs=placed,
        out_specs=(P("gx", "gz", None, None, None), P(("gx", "gz"))),
        check_vma=False,
    )
```

```python
import functools
import math

import jax
import jax.numpy as jnp
import numpy as np
from jax import lax
from jax.experimental import pallas as pl
from jax.experimental.pallas import tpu as pltpu
from jax.sharding import PartitionSpec as P

SCALE = 0.25
JUMP = 0.75
LANES = 128
VMEM = pl.BlockSpec(memory_space=pltpu.VMEM)
HBM = pl.BlockSpec(memory_space=pltpu.HBM)

X_FIELDS, X_TRACES, X_SLOTS, X_BLOCKS = 0, 16, 28, 29
Z_SLOTS, Z_BLOCKS = 8, 9
W_CORNERS, W_BLOCKS = 8, 12
X_WALL, Z_WALL, LOGK = 0, 4, 6
SUMS = 2


def derivative_matrix():
    points = np.array([-1.0, -math.sqrt(0.2), math.sqrt(0.2), 1.0])
    products = np.array(
        [
            np.prod([points[first] - points[other] for other in range(4) if other != first])
            for first in range(4)
        ]
    )
    matrix = np.zeros((4, 4))
    for first in range(4):
        for second in range(4):
            if first != second:
                matrix[first, second] = (
                    products[first] / products[second] / (points[first] - points[second])
                )
        matrix[first, first] = sum(
            (1.0 / (points[first] - points[other]) for other in range(4) if other != first)
        )
    return matrix


class Rows:
    def __init__(self):
        row = lax.broadcasted_iota(jnp.int32, (8, LANES), 0)
        self.upper = row >= 4
        self.c = row & 3

    def halves(self, low, high):
        return jnp.where(self.upper, jnp.float32(high), jnp.float32(low))

    def by_c(self, values):
        result = jnp.full((8, LANES), values[0], jnp.float32)
        for c in range(1, 4):
            result = jnp.where(self.c == c, jnp.float32(values[c]), result)
        return result


class Derivative:
    def __init__(self, rows, matrix):
        self.matrix = matrix
        self.same = [
            [rows.halves(matrix[2 * h, 2 * g], matrix[2 * h + 1, 2 * g + 1]) for g in range(2)]
            for h in range(2)
        ]
        self.cross = [
            [rows.halves(matrix[2 * h, 2 * g + 1], matrix[2 * h + 1, 2 * g]) for g in range(2)]
            for h in range(2)
        ]
        self.shift = {
            delta: rows.by_c(
                [matrix[c, c + delta] if 0 <= c + delta < 4 else 0.0 for c in range(4)]
            )
            for delta in range(-3, 4)
        }

    def across(self, a, u):
        return sum(float(self.matrix[a, j]) * u[j : j + 1] for j in range(4))

    def along(self, axis, u):
        if axis == 0:
            return jnp.concatenate([self.across(a, u) for a in range(4)])
        if axis == 1:
            swapped = pltpu.roll(u, 4, 2)
            return jnp.stack(
                [
                    sum(self.same[h][g] * u[:, g] + self.cross[h][g] * swapped[:, g] for g in range(2))
                    for h in range(2)
                ],
                axis=1,
            )
        return sum(
            coefficient * (u if delta == 0 else pltpu.roll(u, -delta % 8, 2))
            for delta, coefficient in self.shift.items()
        )


def traces(fields, axis, sign):
    others = [fields[f] for f in range(3) if f != axis]
    return others + [fields[axis] + sign * fields[3]]


def face_terms(inner, outer, axis, sign, weight, adjoint):
    tangential = [weight * (i - o) for i, o in zip(inner[:2], outer[:2])]
    normal = weight * (inner[2] - outer[2])
    if adjoint:
        pressure = (-sign) * (weight * (inner[2] + outer[2]))
    else:
        pressure = (-sign) * normal
    terms = tangential[:]
    terms.insert(axis, normal)
    return terms + [pressure]


def y_terms(fields, rows, adjoint):
    high_weight = rows.halves(0.0, JUMP)
    low_weight = rows.halves(JUMP, 0.0)
    first = [field[:, 0] for field in fields]
    second = [field[:, 1] for field in fields]
    moved = lambda value, step: pltpu.roll(pltpu.roll(value, 4, 1), step, 2)
    flip = 1.0 if adjoint else -1.0
    high_out = [moved(t, LANES - 1) for t in traces(first, 1, flip)]
    high = face_terms(traces(second, 1, -1.0), high_out, 1, 1.0, high_weight, adjoint)
    low_out = [moved(t, 1) for t in traces(second, 1, -flip)]
    low = face_terms(traces(first, 1, 1.0), low_out, 1, -1.0, low_weight, adjoint)
    return [jnp.stack([l, h], axis=1) for l, h in zip(low, high)]


def z_terms(inner, outer_fields, sign, weight, adjoint):
    flip = sign if adjoint else -sign
    outer = [pltpu.roll(t, 3 if sign > 0 else 5, t.ndim - 2) for t in traces(outer_fields, 2, flip)]
    return face_terms(traces(inner, 2, -sign), outer, 2, sign, weight, adjoint)


def packed_face(rows, fields, sign):
    c = 3 if sign > 0 else 0
    axis = fields[0].ndim - 2
    result = None
    for f, field in enumerate(fields):
        moved = field if f == c else pltpu.roll(field, (f - c) % 8, axis)
        result = moved if result is None else jnp.where(rows.c == f, moved, result)
    return result


def unpacked_face(packed, sign):
    c = 3 if sign > 0 else 0
    axis = packed.ndim - 2
    return [packed if f == c else pltpu.roll(packed, (c - f) % 8, axis) for f in range(4)]


def met_terms(inner, packed, sign, weight):
    outer = traces(unpacked_face(packed, sign), 2, -sign)
    return face_terms(traces(inner, 2, -sign), outer, 2, sign, weight, False)


def wall_terms(fields, axis, sign, weight, flag, adjoint):
    inner = traces(fields, axis, -sign)
    image = inner[2] if adjoint else fields[axis] + sign * fields[3]
    outer = inner[:2] + [(1.0 - 2.0 * flag) * image]
    return face_terms(inner, outer, axis, sign, weight, adjoint)


def z_weights(rows):
    return {-1: jnp.where(rows.c == 0, JUMP, 0.0), 1: jnp.where(rows.c == 3, JUMP, 0.0)}


def load(ref, z):
    return [ref[z, f] for f in range(4)]


def faces_kernel(state_in, target_in, state, pay_a, pay_b, target, arrived):
    copies = [pltpu.make_async_copy(state_in, state, arrived.at[0])]
    for side in range(2):
        copies.append(
            pltpu.make_async_copy(
                target_in.at[:, :, 3 * side], target.at[side], arrived.at[1 + side]
            )
        )
    for copy in copies:
        copy.start()
    even = lax.axis_index("gx") % 2 == 0
    rows = Rows()
    derivative = Derivative(rows, derivative_matrix())
    weights = z_weights(rows)
    for copy in copies:
        copy.wait()
    for z in range(2):
        sign = 1 if z == 0 else -1
        values = []
        for side in range(2):
            a = 3 * side
            u = [state[z, f, a : a + 1] for f in range(4)]
            other = [state[1 - z, f, a : a + 1] for f in range(4)]
            grads = [derivative.across(a, state[z, 3])]
            grads += [derivative.along(k, u[3]) for k in (1, 2)]
            divergence = derivative.across(a, state[z, 0])
            divergence += derivative.along(1, u[1]) + derivative.along(2, u[2])
            jumps = y_terms(u, rows, False)
            terms = z_terms(u, other, float(sign), weights[sign], False)
            result = [
                (SCALE * v + j + t)[0] - target[side, z, f]
                for f, (v, j, t) in enumerate(zip(grads + [divergence], jumps, terms))
            ]
            normal = result[0] - result[3] if side else result[0] + result[3]
            values.append([v[0] for v in u] + [normal, result[1], result[2]])
        low, high = values
        for j in range(7):
            pay_a[pl.ds(4 * j + 2 * z, 2)] = jnp.where(even, high[j], low[j])
            pay_b[pl.ds(4 * j + 2 * z, 2)] = jnp.where(even, low[j], high[j])


def wall_rows(sizes, rows, weights, z, flags):
    z_place = lax.axis_index("gz")
    end = (z_place == 0) if z == 0 else (z_place == sizes[1] - 1)
    weight = weights[-1 if z == 0 else 1] * jnp.where(end, 1.0, 0.0)
    return weight, flags[z : z + 1, :].astype(jnp.float32)


def edges_kernel(sizes, first_a, first_b, cell_of, cell_slot, z_wall, pay_a, pay_b, positions):
    nx, nz = sizes
    x_place, z_place = lax.axis_index("gx"), lax.axis_index("gz")
    rows = Rows()
    weights = z_weights(rows)
    cell_rows = cell_slot.shape[0]
    slots = []
    for z in range(2):
        row_of = lax.shift_right_logical(cell_of[z : z + 1, :], 7)
        slot = jnp.zeros((1, LANES), jnp.int32)
        for step in (-1, 0, 1):
            row = (x_place // 4 + step) * nz + z_place
            row = jnp.clip(row, 0, cell_rows - 1)
            slot = jnp.where(row_of == row, cell_slot[pl.ds(row, 1), :], slot)
        slots.append(slot.astype(jnp.float32))
    row = lax.broadcasted_iota(jnp.int32, (8, LANES), 0)
    block = jnp.where(row == 0, slots[0], jnp.where(row == 1, slots[1], 0.0))
    positions[...] = block
    flip = jnp.where(x_place % 2 == 0, -1.0, 1.0)
    for first, pay, factor in ((first_a, pay_a, flip), (first_b, pay_b, -flip)):
        for i in range(X_SLOTS):
            pay[i] = first[i]
        pay[X_SLOTS] = block
        for z in range(2):
            weight, flag = wall_rows(sizes, rows, weights, z, z_wall)
            fields = [first[pl.ds(4 * f + 2 * z, 2)] for f in range(4)]
            terms = wall_terms(fields, 2, -1.0 if z == 0 else 1.0, weight, flag, False)
            normal, tangential = X_TRACES + 2 * z, X_TRACES + 8 + 2 * z
            pay[pl.ds(normal, 2)] = first[pl.ds(normal, 2)] + factor * terms[3]
            pay[pl.ds(tangential, 2)] = first[pl.ds(tangential, 2)] + terms[2]


def local_kernel(sizes, state, positions, target, x_wall, z_wall, logk, small, local, *z_pay):
    nx, nz = sizes
    z_place = lax.axis_index("gz")
    rows = Rows()
    derivative = Derivative(rows, derivative_matrix())
    weights = z_weights(rows)
    small[0] = positions[...]
    for side in range(2):
        small[1, X_WALL + 2 * side : X_WALL + 2 * side + 2, :] = x_wall[side].astype(jnp.float32)
    small[1, Z_WALL : Z_WALL + 2, :] = z_wall[...].astype(jnp.float32)
    small[1, LOGK : LOGK + 1, 0 : logk.shape[1]] = logk[...]
    for z in range(2):
        u = load(state, z)
        other = load(state, 1 - z)
        grads = [derivative.along(k, u[3]) for k in range(3)]
        divergence = sum(derivative.along(k, u[k]) for k in range(3))
        jumps = y_terms(u, rows, False)
        sign = 1 if z == 0 else -1
        across = z_terms(u, other, float(sign), weights[sign], False)
        weight, flag = wall_rows(sizes, rows, weights, z, z_wall)
        wall = wall_terms(u, 2, -float(sign), weight, flag, False)
        for f, (v, j, a, w) in enumerate(zip(grads + [divergence], jumps, across, wall)):
            local[z, f] = SCALE * v + j + a + w - target[z, f]
        first = sum(local[z, k] * u[k] for k in range(3))
        second = sum(u[k] * u[k] for k in range(3))
        small[SUMS, z : z + 1, :] = jnp.sum(first, axis=(0, 1, 2))[None]
        small[SUMS, 2 + z : 3 + z, :] = jnp.sum(second, axis=(0, 1, 2))[None]
    faces = [packed_face(rows, load(state, z), 2 * z - 1) for z in range(2)]
    for direction in range(len(z_pay)):
        upper = z_place == 0 if nz == 2 else direction == 0
        z_pay[direction][0:8] = jnp.where(upper, faces[1], faces[0]).reshape(8, 8, LANES)
        slot = jnp.where(upper, positions[1:2, :], positions[0:1, :])
        z_pay[direction][Z_SLOTS] = jnp.broadcast_to(slot, (8, LANES))


def x_side(side, even, got_a, got_b, block):
    a, b = got_a[pl.ds(block, 2)], got_b[pl.ds(block, 2)]
    return jnp.where(even, b, a) if side == 0 else jnp.where(even, a, b)


def sums_kernel(sizes, length, state, small, local, got_a, got_b, *refs):
    nx, nz = sizes
    count = 1 if nz == 2 else 2
    z_got, (whole, send), z_pay = refs[:count], refs[count : count + 2], refs[count + 2 :]
    z_from = [z_got[0], z_got[-1]]
    x_place, z_place = lax.axis_index("gx"), lax.axis_index("gz")
    even = x_place % 2 == 0
    rows = Rows()
    weights = z_weights(rows)
    corners = {}
    sums = []
    for z in range(2):
        u = load(state, z)
        for f in range(4):
            whole[z, f] = local[z, f]
        sign = -1 if z == 0 else 1
        inside = (z_place > 0) if z == 0 else (z_place < nz - 1)
        packed = z_from[z][0:8].reshape(4, 2, 8, LANES)
        terms = met_terms(u, packed, float(sign), weights[sign] * jnp.where(inside, 1.0, 0.0))
        for f in range(4):
            whole[z, f] += terms[f]
        total = sum(jnp.sum(terms[k] * u[k], axis=(0, 1)) for k in range(3))
        for side in range(2):
            sign = 1.0 if side else -1.0
            a = 3 * side
            end = (x_place == nx - 1) if side else (x_place == 0)
            mine = [u[f][a] for f in range(4)]
            theirs = [x_side(side, even, got_a, got_b, 4 * f + 2 * z) for f in range(4)]
            corners[side, z] = theirs
            flag = small[1, X_WALL + 2 * side + z : X_WALL + 2 * side + z + 1, :]
            inner = traces(mine, 0, -sign)
            image = (1.0 - 2.0 * flag) * (mine[0] + sign * mine[3])
            outer = [
                jnp.where(end, e, o)
                for e, o in zip(inner[:2] + [image], traces(theirs, 0, -sign))
            ]
            terms = face_terms(inner, outer, 0, sign, JUMP, False)
            for f in range(4):
                whole[z, f, a] += terms[f]
            total += sum(jnp.sum(terms[k] * mine[k], axis=0) for k in range(3))
        local_sum = small[SUMS, z : z + 1, :]
        sums.append((local_sum + jnp.sum(total, axis=0)[None], small[SUMS, 2 + z : 3 + z, :]))
    devices = send.shape[0]
    slots = small[0].astype(jnp.int32)
    elements = 2 * LANES
    slot = jnp.concatenate([slots[0:1, :], slots[1:2, :]], axis=1)
    owner = lax.broadcasted_iota(jnp.int32, (devices, elements), 0)
    place = lax.broadcasted_iota(jnp.int32, (LANES, elements), 0) % length
    chosen = owner == slot // length
    position = jnp.where(place == slot % length, 1.0, 0.0).astype(jnp.bfloat16)
    pieces = []
    for parts in zip(*sums):
        value = jnp.where(chosen, jnp.concatenate(parts, axis=1), 0.0)
        for _ in range(3):
            piece = value.astype(jnp.bfloat16)
            pieces.append(piece)
            value = value - piece.astype(jnp.float32)
    placed = lax.dot_general(
        jnp.concatenate(pieces, axis=0),
        position,
        (((1,), (1,)), ((), ())),
        preferred_element_type=jnp.float32,
    )
    parts = [placed[i * devices : (i + 1) * devices] for i in range(6)]
    lane = lax.broadcasted_iota(jnp.int32, (devices, LANES), 1)
    first, second = parts[0] + parts[1] + parts[2], parts[3] + parts[4] + parts[5]
    send[...] = jnp.where(lane < 2 * length, first, second)
    logk = small[1, LOGK : LOGK + 1, 0:length]
    send[:, 0:length] = jnp.broadcast_to(logk, (devices, length))
    faces = [packed_face(rows, load(whole, z), 2 * z - 1) for z in range(2)]
    edges = [[packed_face(rows, corners[side, z], 2 * z - 1) for z in range(2)] for side in range(2)]
    for direction in range(count):
        upper = z_place == 0 if nz == 2 else direction == 0
        z_pay[direction][0:8] = jnp.where(upper, faces[1], faces[0]).reshape(8, 8, LANES)
        for side in range(2):
            block = W_CORNERS + 2 * side
            z_pay[direction][block : block + 2] = jnp.where(upper, edges[side][1], edges[side][0])


def look_up(table, length, slots):
    devices = table.shape[0]
    fold = LANES // length
    table_rows = devices // fold
    chunk = min(8, table_rows)
    lane = lax.broadcasted_iota(jnp.int32, (chunk, LANES), 1)
    in_lane = slots & (LANES - 1)
    in_row = lax.shift_right_logical(slots, 7)

    def step(index, result):
        rows = jnp.zeros((chunk, LANES), jnp.float32)
        for j in range(fold):
            part = table[pl.ds(index * chunk * fold + j, chunk, stride=fold), :]
            rows += pltpu.roll(jnp.where(lane < length, part, 0.0), j * length, 1)
        for i in range(chunk):
            wide = jnp.broadcast_to(rows[i : i + 1, :], (8, LANES))
            taken = jnp.take_along_axis(wide, in_lane, axis=1)
            result = jnp.where(in_row == index * chunk + i, taken, result)
        return result

    result = jnp.zeros((8, LANES), jnp.float32)
    if table_rows == chunk:
        return step(0, result)
    return lax.fori_loop(0, table_rows // chunk, step, result)


def adjoint_kernel(sizes, length, state, small, whole, got_a, got_b, received, *refs):
    nx, nz = sizes
    count = 1 if nz == 2 else 2
    z_got, w_got, refs = refs[:count], refs[count : 2 * count], refs[2 * count :]
    adjoint_out, gradient_out, adjoint, gradient, done = refs
    z_from, w_from = [z_got[0], z_got[-1]], [w_got[0], w_got[-1]]
    x_place, z_place = lax.axis_index("gx"), lax.axis_index("gz")
    even = x_place % 2 == 0
    rows = Rows()
    weights = z_weights(rows)
    derivative = Derivative(rows, derivative_matrix().T)
    copies = []
    slot_a, slot_b = got_a[X_SLOTS], got_b[X_SLOTS]
    row = lax.broadcasted_iota(jnp.int32, (8, LANES), 0)
    slots = small[0]
    slots = jnp.where(row // 2 == 1, pltpu.roll(jnp.where(even, slot_b, slot_a), 2, 0), slots)
    slots = jnp.where(row // 2 == 2, pltpu.roll(jnp.where(even, slot_a, slot_b), 4, 0), slots)
    slots = jnp.where(row == 6, z_from[0][Z_SLOTS], slots)
    slots = jnp.where(row == 7, z_from[1][Z_SLOTS], slots)
    quarter = jnp.exp(-look_up(received, length, slots.astype(jnp.int32)))
    resistance = [quarter[i : i + 1, :] for i in range(8)]
    residual = []
    for z in range(2):
        scaled = SCALE * resistance[z]
        residual.append(
            [whole[z, k] + scaled * state[z, k] for k in range(3)] + [whole[z, 3]]
        )
    for z in range(2):
        w = residual[z]
        jumps = y_terms(w, rows, True)
        sign = 1 if z == 0 else -1
        across = z_terms(w, residual[1 - z], float(sign), weights[sign], True)
        sign = -sign
        end = (z_place == 0) if z == 0 else (z_place == nz - 1)
        scaled = SCALE * resistance[6 + z]
        theirs = unpacked_face(w_from[z][0:8].reshape(4, 2, 8, LANES), sign)
        fields = unpacked_face(z_from[z][0:8].reshape(4, 2, 8, LANES), sign)
        theirs = [theirs[k] + scaled * fields[k] for k in range(3)] + [theirs[3]]
        flag = small[1, Z_WALL + z : Z_WALL + z + 1, :]
        inner = traces(w, 2, -float(sign))
        outer = traces(theirs, 2, float(sign))
        image = inner[:2] + [(1.0 - 2.0 * flag) * inner[2]]
        outer = [jnp.where(end, i, o) for i, o in zip(image, outer)]
        beyond = face_terms(inner, outer, 2, float(sign), weights[sign], True)
        grads = [derivative.along(k, w[3]) for k in range(3)]
        divergence = sum(derivative.along(k, w[k]) for k in range(3))
        volume = [SCALE * (resistance[z] * w[k] + grads[k]) for k in range(3)]
        volume.append(SCALE * divergence)
        for f in range(4):
            adjoint[z, f] = volume[f] + jumps[f] + across[f] + beyond[f]
        for side in range(2):
            a = 3 * side
            s = 1.0 if side else -1.0
            u_out = [x_side(side, even, got_a, got_b, 4 * f + 2 * z) for f in range(4)]
            trace = [
                x_side(side, even, got_a, got_b, X_TRACES + 4 * j + 2 * z) for j in range(3)
            ]
            normal, tangential = trace[0], trace[1:]
            mine = traces([state[z, f, a] for f in range(4)], 0, s)
            there = traces(u_out, 0, s)
            normal = normal - (2.0 * JUMP) * (mine[2] - there[2])
            tangential = [t - JUMP * (m - o) for t, m, o in zip(tangential, mine[:2], there[:2])]
            t = float(sign)
            weight = weights[sign] * jnp.where(end, 0.0, 1.0)
            block = W_CORNERS + 2 * side
            edge = met_terms(u_out, w_from[z][block : block + 2], t, weight)
            normal = normal + edge[0] + s * edge[3]
            tangential = [tangential[0] + edge[1], tangential[1] + edge[2]]
            scaled = SCALE * resistance[2 + 2 * side + z]
            normal = normal + scaled * u_out[0]
            tangential = [v + scaled * u_out[1 + j] for j, v in enumerate(tangential)]
            inner = traces([w[f][a] for f in range(4)], 0, -s)
            flag = small[1, X_WALL + 2 * side + z : X_WALL + 2 * side + z + 1, :]
            image = inner[:2] + [(1.0 - 2.0 * flag) * inner[2]]
            last = (x_place == nx - 1) if side else (x_place == 0)
            outer = [jnp.where(last, i, o) for i, o in zip(image, tangential + [normal])]
            terms = face_terms(inner, outer, 0, s, JUMP, True)
            for f in range(4):
                adjoint[z, f, a] += terms[f]
        copies.append(pltpu.make_async_copy(adjoint.at[z], adjoint_out.at[z], done.at[z]))
        copies[-1].start()
        if z == 0:
            held = jnp.exp(-small[1, LOGK : LOGK + 1, 0:length])
            summed = jnp.sum(received[...], axis=0, keepdims=True)
            first, second = summed[:, length : 2 * length], summed[:, 2 * length : 3 * length]
            gradient[...] = -(SCALE / 64.0) * held * (first + SCALE * held * second)
            copies.append(pltpu.make_async_copy(gradient, gradient_out, done.at[2]))
            copies[-1].start()
    for copy in copies:
        copy.wait()


def call(kernel, operands, in_spec, shapes, out_spec, scratch, room):
    return pl.pallas_call(
        kernel,
        out_shape=[jax.ShapeDtypeStruct(shape, jnp.float32) for shape in shapes],
        in_specs=[in_spec] * len(operands),
        out_specs=[out_spec] * len(shapes),
        scratch_shapes=scratch,
        compiler_params=pltpu.CompilerParams(vmem_limit_bytes=room * 1024),
        cost_estimate=pl.CostEstimate(flops=2000000, bytes_accessed=800000, transcendentals=0),
    )(*operands)


def both_ways(pairs):
    return pairs + [(second, first) for first, second in pairs]


def along_z(payloads, nz):
    if nz == 2:
        return [lax.ppermute(payloads[0], "gz", [(0, 1), (1, 0)])]
    up = [(i, i + 1) for i in range(nz - 1)]
    down = [(second, first) for first, second in up]
    return [lax.ppermute(payloads[0], "gz", up), lax.ppermute(payloads[1], "gz", down)]


def shards(nx, nz, state, target, coarse_logk, cell_slot, cell_of, wall_flags_xaxis, z_wall):
    sizes = (nx, nz)
    shape = (2, 4, 4, 2, 8, LANES)
    length = coarse_logk.shape[0]
    state6, target6 = state.reshape(shape), target.reshape(shape)
    z_flags = z_wall.reshape(2, LANES)
    count = 1 if nz == 2 else 2
    x_shape, z_shape, w_shape = ((n, 8, LANES) for n in (X_BLOCKS, Z_BLOCKS, W_BLOCKS))
    held, first_a, first_b = call(
        faces_kernel,
        [state6, target6],
        HBM,
        [shape, x_shape, x_shape],
        VMEM,
        [pltpu.VMEM((2, 2, 4, 2, 8, LANES), jnp.float32), pltpu.SemaphoreType.DMA((3,))],
        54600,
    )
    pay_a, pay_b, positions = call(
        functools.partial(edges_kernel, sizes),
        [first_a, first_b, cell_of.reshape(2, LANES), cell_slot.reshape(-1, LANES), z_flags],
        VMEM,
        [x_shape, x_shape, (8, LANES)],
        VMEM,
        [],
        16 * 1024,
    )
    pairs_b = both_ways([(i, i + 1) for i in range(1, nx - 1, 2)])
    pairs_b += [(i, i) for i in range(nx) if i not in dict(pairs_b)]
    pairs_a = both_ways([(i, i + 1) for i in range(0, nx - 1, 2)])
    got_a = lax.ppermute(pay_a, "gx", pairs_a)
    got_b = lax.ppermute(pay_b, "gx", pairs_b)
    small, local, *z_pay = call(
        functools.partial(local_kernel, sizes),
        [held, positions, target6, wall_flags_xaxis, z_flags, coarse_logk.reshape(1, -1)],
        VMEM,
        [(3, 8, LANES), shape] + [z_shape] * count,
        VMEM,
        [],
        16 * 1024,
    )
    z_got = along_z(z_pay, nz)
    whole, send, *w_pay = call(
        functools.partial(sums_kernel, sizes, length),
        [held, small, local, got_a, got_b] + z_got,
        VMEM,
        [shape, (nx * nz, LANES)] + [w_shape] * count,
        VMEM,
        [],
        16 * 1024,
    )
    w_got = along_z(w_pay, nz)
    received = lax.all_to_all(send, ("gx", "gz"), 0, 0, tiled=True)
    adjoint, gradient = call(
        functools.partial(adjoint_kernel, sizes, length),
        [held, small, whole, got_a, got_b, received] + z_got + w_got,
        VMEM,
        [shape, (1, length)],
        HBM,
        [
            pltpu.VMEM(shape, jnp.float32),
            pltpu.VMEM((1, length), jnp.float32),
            pltpu.SemaphoreType.DMA((3,)),
        ],
        16 * 1024,
    )
    return adjoint.reshape(state.shape), gradient.reshape(-1)


def solution(mesh):
    placed = (
        P("gx", "gz", None, None, None),
        P("gx", "gz", None, None, None),
        P(("gx", "gz")),
        P(),
        P("gx", "gz", None),
        P(None, "gz", None),
        P(None, "gx", None),
    )
    return jax.shard_map(
        functools.partial(shards, mesh.shape["gx"], mesh.shape["gz"]),
        mesh=mesh,
        in_specs=placed,
        out_specs=(P("gx", "gz", None, None, None), P(("gx", "gz"))),
        check_vma=False,
    )
```

```python
import functools
import math

import jax
import jax.numpy as jnp
import numpy as np
from jax import lax
from jax.experimental import pallas as pl
from jax.experimental.pallas import tpu as pltpu
from jax.sharding import PartitionSpec as P

SCALE = 0.25
JUMP = 0.75
LANES = 128
VMEM = pl.BlockSpec(memory_space=pltpu.VMEM)
HBM = pl.BlockSpec(memory_space=pltpu.HBM)

X_FIELDS, X_TRACES, X_SLOTS, X_BLOCKS = 0, 16, 28, 29
Z_SLOTS, Z_BLOCKS = 8, 9
W_CORNERS, W_BLOCKS = 8, 12
X_WALL, Z_WALL, LOGK = 0, 4, 6
SUMS = 2


def derivative_matrix():
    points = np.array([-1.0, -math.sqrt(0.2), math.sqrt(0.2), 1.0])
    products = np.array(
        [
            np.prod([points[first] - points[other] for other in range(4) if other != first])
            for first in range(4)
        ]
    )
    matrix = np.zeros((4, 4))
    for first in range(4):
        for second in range(4):
            if first != second:
                matrix[first, second] = (
                    products[first] / products[second] / (points[first] - points[second])
                )
        matrix[first, first] = sum(
            (1.0 / (points[first] - points[other]) for other in range(4) if other != first)
        )
    return matrix


class Rows:
    def __init__(self):
        row = lax.broadcasted_iota(jnp.int32, (8, LANES), 0)
        self.upper = row >= 4
        self.c = row & 3

    def halves(self, low, high):
        return jnp.where(self.upper, jnp.float32(high), jnp.float32(low))

    def by_c(self, values):
        result = jnp.full((8, LANES), values[0], jnp.float32)
        for c in range(1, 4):
            result = jnp.where(self.c == c, jnp.float32(values[c]), result)
        return result


class Derivative:
    def __init__(self, rows, matrix):
        self.matrix = matrix
        self.same = [
            [rows.halves(matrix[2 * h, 2 * g], matrix[2 * h + 1, 2 * g + 1]) for g in range(2)]
            for h in range(2)
        ]
        self.cross = [
            [rows.halves(matrix[2 * h, 2 * g + 1], matrix[2 * h + 1, 2 * g]) for g in range(2)]
            for h in range(2)
        ]
        self.shift = {
            delta: rows.by_c(
                [matrix[c, c + delta] if 0 <= c + delta < 4 else 0.0 for c in range(4)]
            )
            for delta in range(-3, 4)
        }

    def across(self, a, u):
        return sum(float(self.matrix[a, j]) * u[j : j + 1] for j in range(4))

    def along(self, axis, u):
        if axis == 0:
            return jnp.concatenate([self.across(a, u) for a in range(4)])
        if axis == 1:
            swapped = pltpu.roll(u, 4, 2)
            return jnp.stack(
                [
                    sum(self.same[h][g] * u[:, g] + self.cross[h][g] * swapped[:, g] for g in range(2))
                    for h in range(2)
                ],
                axis=1,
            )
        return sum(
            coefficient * (u if delta == 0 else pltpu.roll(u, -delta % 8, 2))
            for delta, coefficient in self.shift.items()
        )


def traces(fields, axis, sign):
    others = [fields[f] for f in range(3) if f != axis]
    return others + [fields[axis] + sign * fields[3]]


def face_terms(inner, outer, axis, sign, weight, adjoint):
    tangential = [weight * (i - o) for i, o in zip(inner[:2], outer[:2])]
    normal = weight * (inner[2] - outer[2])
    if adjoint:
        pressure = (-sign) * (weight * (inner[2] + outer[2]))
    else:
        pressure = (-sign) * normal
    terms = tangential[:]
    terms.insert(axis, normal)
    return terms + [pressure]


def y_terms(fields, rows, adjoint):
    high_weight = rows.halves(0.0, JUMP)
    low_weight = rows.halves(JUMP, 0.0)
    first = [field[:, 0] for field in fields]
    second = [field[:, 1] for field in fields]
    moved = lambda value, step: pltpu.roll(pltpu.roll(value, 4, 1), step, 2)
    flip = 1.0 if adjoint else -1.0
    high_out = [moved(t, LANES - 1) for t in traces(first, 1, flip)]
    high = face_terms(traces(second, 1, -1.0), high_out, 1, 1.0, high_weight, adjoint)
    low_out = [moved(t, 1) for t in traces(second, 1, -flip)]
    low = face_terms(traces(first, 1, 1.0), low_out, 1, -1.0, low_weight, adjoint)
    return [jnp.stack([l, h], axis=1) for l, h in zip(low, high)]


def z_terms(inner, outer_fields, sign, weight, adjoint):
    flip = sign if adjoint else -sign
    outer = [pltpu.roll(t, 3 if sign > 0 else 5, t.ndim - 2) for t in traces(outer_fields, 2, flip)]
    return face_terms(traces(inner, 2, -sign), outer, 2, sign, weight, adjoint)


def packed_face(rows, fields, sign):
    c = 3 if sign > 0 else 0
    axis = fields[0].ndim - 2
    result = None
    for f, field in enumerate(fields):
        moved = field if f == c else pltpu.roll(field, (f - c) % 8, axis)
        result = moved if result is None else jnp.where(rows.c == f, moved, result)
    return result


def unpacked_face(packed, sign):
    c = 3 if sign > 0 else 0
    axis = packed.ndim - 2
    return [packed if f == c else pltpu.roll(packed, (c - f) % 8, axis) for f in range(4)]


def met_terms(inner, packed, sign, weight):
    outer = traces(unpacked_face(packed, sign), 2, -sign)
    return face_terms(traces(inner, 2, -sign), outer, 2, sign, weight, False)


def wall_terms(fields, axis, sign, weight, flag, adjoint):
    inner = traces(fields, axis, -sign)
    image = inner[2] if adjoint else fields[axis] + sign * fields[3]
    outer = inner[:2] + [(1.0 - 2.0 * flag) * image]
    return face_terms(inner, outer, axis, sign, weight, adjoint)


def z_weights(rows):
    return {-1: jnp.where(rows.c == 0, JUMP, 0.0), 1: jnp.where(rows.c == 3, JUMP, 0.0)}


def load(ref, z):
    return [ref[z, f] for f in range(4)]


def faces_kernel(state_in, target_in, state, pay_a, pay_b, target, arrived):
    copies = [pltpu.make_async_copy(state_in, state, arrived.at[0])]
    for side in range(2):
        copies.append(
            pltpu.make_async_copy(
                target_in.at[:, :, 3 * side], target.at[side], arrived.at[1 + side]
            )
        )
    for copy in copies:
        copy.start()
    even = lax.axis_index("gx") % 2 == 0
    rows = Rows()
    derivative = Derivative(rows, derivative_matrix())
    weights = z_weights(rows)
    for copy in copies:
        copy.wait()
    for z in range(2):
        sign = 1 if z == 0 else -1
        values = []
        for side in range(2):
            a = 3 * side
            u = [state[z, f, a : a + 1] for f in range(4)]
            other = [state[1 - z, f, a : a + 1] for f in range(4)]
            grads = [derivative.across(a, state[z, 3])]
            grads += [derivative.along(k, u[3]) for k in (1, 2)]
            divergence = derivative.across(a, state[z, 0])
            divergence += derivative.along(1, u[1]) + derivative.along(2, u[2])
            jumps = y_terms(u, rows, False)
            terms = z_terms(u, other, float(sign), weights[sign], False)
            result = [
                (SCALE * v + j + t)[0] - target[side, z, f]
                for f, (v, j, t) in enumerate(zip(grads + [divergence], jumps, terms))
            ]
            normal = result[0] - result[3] if side else result[0] + result[3]
            values.append([v[0] for v in u] + [normal, result[1], result[2]])
        low, high = values
        for j in range(7):
            pay_a[pl.ds(4 * j + 2 * z, 2)] = jnp.where(even, high[j], low[j])
            pay_b[pl.ds(4 * j + 2 * z, 2)] = jnp.where(even, low[j], high[j])


def wall_rows(sizes, rows, weights, z, flags):
    z_place = lax.axis_index("gz")
    end = (z_place == 0) if z == 0 else (z_place == sizes[1] - 1)
    weight = weights[-1 if z == 0 else 1] * jnp.where(end, 1.0, 0.0)
    return weight, flags[z : z + 1, :].astype(jnp.float32)


def edges_kernel(sizes, first_a, first_b, cell_of, cell_slot, z_wall, pay_a, pay_b, positions):
    nx, nz = sizes
    x_place, z_place = lax.axis_index("gx"), lax.axis_index("gz")
    rows = Rows()
    weights = z_weights(rows)
    cell_rows = cell_slot.shape[0]
    slots = []
    for z in range(2):
        row_of = lax.shift_right_logical(cell_of[z : z + 1, :], 7)
        slot = jnp.zeros((1, LANES), jnp.int32)
        for step in (-1, 0, 1):
            row = (x_place // 4 + step) * nz + z_place
            row = jnp.clip(row, 0, cell_rows - 1)
            slot = jnp.where(row_of == row, cell_slot[pl.ds(row, 1), :], slot)
        slots.append(slot.astype(jnp.float32))
    row = lax.broadcasted_iota(jnp.int32, (8, LANES), 0)
    block = jnp.where(row == 0, slots[0], jnp.where(row == 1, slots[1], 0.0))
    positions[...] = block
    flip = jnp.where(x_place % 2 == 0, -1.0, 1.0)
    for first, pay, factor in ((first_a, pay_a, flip), (first_b, pay_b, -flip)):
        for i in range(X_SLOTS):
            pay[i] = first[i]
        pay[X_SLOTS] = block
        for z in range(2):
            weight, flag = wall_rows(sizes, rows, weights, z, z_wall)
            fields = [first[pl.ds(4 * f + 2 * z, 2)] for f in range(4)]
            terms = wall_terms(fields, 2, -1.0 if z == 0 else 1.0, weight, flag, False)
            normal, tangential = X_TRACES + 2 * z, X_TRACES + 8 + 2 * z
            pay[pl.ds(normal, 2)] = first[pl.ds(normal, 2)] + factor * terms[3]
            pay[pl.ds(tangential, 2)] = first[pl.ds(tangential, 2)] + terms[2]


def local_kernel(sizes, state, positions, target, x_wall, z_wall, logk, small, local, *z_pay):
    nx, nz = sizes
    z_place = lax.axis_index("gz")
    rows = Rows()
    derivative = Derivative(rows, derivative_matrix())
    weights = z_weights(rows)
    small[0] = positions[...]
    for side in range(2):
        small[1, X_WALL + 2 * side : X_WALL + 2 * side + 2, :] = x_wall[side].astype(jnp.float32)
    small[1, Z_WALL : Z_WALL + 2, :] = z_wall[...].astype(jnp.float32)
    small[1, LOGK : LOGK + 1, 0 : logk.shape[1]] = logk[...]
    for z in range(2):
        u = load(state, z)
        other = load(state, 1 - z)
        grads = [derivative.along(k, u[3]) for k in range(3)]
        divergence = sum(derivative.along(k, u[k]) for k in range(3))
        jumps = y_terms(u, rows, False)
        sign = 1 if z == 0 else -1
        across = z_terms(u, other, float(sign), weights[sign], False)
        weight, flag = wall_rows(sizes, rows, weights, z, z_wall)
        wall = wall_terms(u, 2, -float(sign), weight, flag, False)
        for f, (v, j, a, w) in enumerate(zip(grads + [divergence], jumps, across, wall)):
            local[z, f] = SCALE * v + j + a + w - target[z, f]
        first = sum(local[z, k] * u[k] for k in range(3))
        second = sum(u[k] * u[k] for k in range(3))
        small[SUMS, z : z + 1, :] = jnp.sum(first, axis=(0, 1, 2))[None]
        small[SUMS, 2 + z : 3 + z, :] = jnp.sum(second, axis=(0, 1, 2))[None]
    faces = [packed_face(rows, load(state, z), 2 * z - 1) for z in range(2)]
    for direction in range(len(z_pay)):
        upper = z_place == 0 if nz == 2 else direction == 0
        z_pay[direction][0:8] = jnp.where(upper, faces[1], faces[0]).reshape(8, 8, LANES)
        slot = jnp.where(upper, positions[1:2, :], positions[0:1, :])
        z_pay[direction][Z_SLOTS] = jnp.broadcast_to(slot, (8, LANES))


def x_side(side, even, got_a, got_b, block):
    a, b = got_a[pl.ds(block, 2)], got_b[pl.ds(block, 2)]
    return jnp.where(even, b, a) if side == 0 else jnp.where(even, a, b)


def sums_kernel(sizes, length, state, small, local, got_a, got_b, *refs):
    nx, nz = sizes
    count = 1 if nz == 2 else 2
    z_got, (whole, send), z_pay = refs[:count], refs[count : count + 2], refs[count + 2 :]
    z_from = [z_got[0], z_got[-1]]
    x_place, z_place = lax.axis_index("gx"), lax.axis_index("gz")
    even = x_place % 2 == 0
    rows = Rows()
    weights = z_weights(rows)
    corners = {}
    sums = []
    for z in range(2):
        u = load(state, z)
        for f in range(4):
            whole[z, f] = local[z, f]
        sign = -1 if z == 0 else 1
        inside = (z_place > 0) if z == 0 else (z_place < nz - 1)
        packed = z_from[z][0:8].reshape(4, 2, 8, LANES)
        terms = met_terms(u, packed, float(sign), weights[sign] * jnp.where(inside, 1.0, 0.0))
        for f in range(4):
            whole[z, f] += terms[f]
        total = sum(jnp.sum(terms[k] * u[k], axis=(0, 1)) for k in range(3))
        for side in range(2):
            sign = 1.0 if side else -1.0
            a = 3 * side
            end = (x_place == nx - 1) if side else (x_place == 0)
            mine = [u[f][a] for f in range(4)]
            theirs = [x_side(side, even, got_a, got_b, 4 * f + 2 * z) for f in range(4)]
            corners[side, z] = theirs
            flag = small[1, X_WALL + 2 * side + z : X_WALL + 2 * side + z + 1, :]
            inner = traces(mine, 0, -sign)
            image = (1.0 - 2.0 * flag) * (mine[0] + sign * mine[3])
            outer = [
                jnp.where(end, e, o)
                for e, o in zip(inner[:2] + [image], traces(theirs, 0, -sign))
            ]
            terms = face_terms(inner, outer, 0, sign, JUMP, False)
            for f in range(4):
                whole[z, f, a] += terms[f]
            total += sum(jnp.sum(terms[k] * mine[k], axis=0) for k in range(3))
        local_sum = small[SUMS, z : z + 1, :]
        sums.append((local_sum + jnp.sum(total, axis=0)[None], small[SUMS, 2 + z : 3 + z, :]))
    devices = send.shape[0]
    slots = small[0].astype(jnp.int32)
    elements = 2 * LANES
    slot = jnp.concatenate([slots[0:1, :], slots[1:2, :]], axis=1)
    owner = lax.broadcasted_iota(jnp.int32, (devices, elements), 0)
    place = lax.broadcasted_iota(jnp.int32, (LANES, elements), 0) % length
    chosen = owner == slot // length
    position = jnp.where(place == slot % length, 1.0, 0.0).astype(jnp.bfloat16)
    pieces = []
    for parts in zip(*sums):
        value = jnp.where(chosen, jnp.concatenate(parts, axis=1), 0.0)
        for _ in range(3):
            piece = value.astype(jnp.bfloat16)
            pieces.append(piece)
            value = value - piece.astype(jnp.float32)
    placed = lax.dot_general(
        jnp.concatenate(pieces, axis=0),
        position,
        (((1,), (1,)), ((), ())),
        preferred_element_type=jnp.float32,
    )
    parts = [placed[i * devices : (i + 1) * devices] for i in range(6)]
    lane = lax.broadcasted_iota(jnp.int32, (devices, LANES), 1)
    first, second = parts[0] + parts[1] + parts[2], parts[3] + parts[4] + parts[5]
    send[...] = jnp.where(lane < 2 * length, first, second)
    logk = small[1, LOGK : LOGK + 1, 0:length]
    send[:, 0:length] = jnp.broadcast_to(logk, (devices, length))
    faces = [packed_face(rows, load(whole, z), 2 * z - 1) for z in range(2)]
    edges = [[packed_face(rows, corners[side, z], 2 * z - 1) for z in range(2)] for side in range(2)]
    for direction in range(count):
        upper = z_place == 0 if nz == 2 else direction == 0
        z_pay[direction][0:8] = jnp.where(upper, faces[1], faces[0]).reshape(8, 8, LANES)
        for side in range(2):
            block = W_CORNERS + 2 * side
            z_pay[direction][block : block + 2] = jnp.where(upper, edges[side][1], edges[side][0])


def look_up(table, length, slots):
    devices = table.shape[0]
    fold = LANES // length
    table_rows = devices // fold
    chunk = min(8, table_rows)
    lane = lax.broadcasted_iota(jnp.int32, (chunk, LANES), 1)
    in_lane = slots & (LANES - 1)
    in_row = lax.shift_right_logical(slots, 7)

    def step(index, result):
        rows = jnp.zeros((chunk, LANES), jnp.float32)
        for j in range(fold):
            part = table[pl.ds(index * chunk * fold + j, chunk, stride=fold), :]
            rows += pltpu.roll(jnp.where(lane < length, part, 0.0), j * length, 1)
        for i in range(chunk):
            wide = jnp.broadcast_to(rows[i : i + 1, :], (8, LANES))
            taken = jnp.take_along_axis(wide, in_lane, axis=1)
            result = jnp.where(in_row == index * chunk + i, taken, result)
        return result

    result = jnp.zeros((8, LANES), jnp.float32)
    if table_rows == chunk:
        return step(0, result)
    return lax.fori_loop(0, table_rows // chunk, step, result)


def adjoint_kernel(sizes, length, state, small, whole, got_a, got_b, received, *refs):
    nx, nz = sizes
    count = 1 if nz == 2 else 2
    z_got, w_got, refs = refs[:count], refs[count : 2 * count], refs[2 * count :]
    adjoint_out, gradient_out, adjoint, gradient, done = refs
    z_from, w_from = [z_got[0], z_got[-1]], [w_got[0], w_got[-1]]
    x_place, z_place = lax.axis_index("gx"), lax.axis_index("gz")
    even = x_place % 2 == 0
    rows = Rows()
    weights = z_weights(rows)
    derivative = Derivative(rows, derivative_matrix().T)
    copies = []
    slot_a, slot_b = got_a[X_SLOTS], got_b[X_SLOTS]
    row = lax.broadcasted_iota(jnp.int32, (8, LANES), 0)
    slots = small[0]
    slots = jnp.where(row // 2 == 1, pltpu.roll(jnp.where(even, slot_b, slot_a), 2, 0), slots)
    slots = jnp.where(row // 2 == 2, pltpu.roll(jnp.where(even, slot_a, slot_b), 4, 0), slots)
    slots = jnp.where(row == 6, z_from[0][Z_SLOTS], slots)
    slots = jnp.where(row == 7, z_from[1][Z_SLOTS], slots)
    quarter = jnp.exp(-look_up(received, length, slots.astype(jnp.int32)))
    resistance = [quarter[i : i + 1, :] for i in range(8)]
    residual = []
    for z in range(2):
        scaled = SCALE * resistance[z]
        residual.append(
            [whole[z, k] + scaled * state[z, k] for k in range(3)] + [whole[z, 3]]
        )
    for z in range(2):
        w = residual[z]
        jumps = y_terms(w, rows, True)
        sign = 1 if z == 0 else -1
        across = z_terms(w, residual[1 - z], float(sign), weights[sign], True)
        sign = -sign
        end = (z_place == 0) if z == 0 else (z_place == nz - 1)
        scaled = SCALE * resistance[6 + z]
        theirs = unpacked_face(w_from[z][0:8].reshape(4, 2, 8, LANES), sign)
        fields = unpacked_face(z_from[z][0:8].reshape(4, 2, 8, LANES), sign)
        theirs = [theirs[k] + scaled * fields[k] for k in range(3)] + [theirs[3]]
        flag = small[1, Z_WALL + z : Z_WALL + z + 1, :]
        inner = traces(w, 2, -float(sign))
        outer = traces(theirs, 2, float(sign))
        image = inner[:2] + [(1.0 - 2.0 * flag) * inner[2]]
        outer = [jnp.where(end, i, o) for i, o in zip(image, outer)]
        beyond = face_terms(inner, outer, 2, float(sign), weights[sign], True)
        grads = [derivative.along(k, w[3]) for k in range(3)]
        divergence = sum(derivative.along(k, w[k]) for k in range(3))
        volume = [SCALE * (resistance[z] * w[k] + grads[k]) for k in range(3)]
        volume.append(SCALE * divergence)
        for f in range(4):
            adjoint[z, f] = volume[f] + jumps[f] + across[f] + beyond[f]
        for side in range(2):
            a = 3 * side
            s = 1.0 if side else -1.0
            u_out = [x_side(side, even, got_a, got_b, 4 * f + 2 * z) for f in range(4)]
            trace = [
                x_side(side, even, got_a, got_b, X_TRACES + 4 * j + 2 * z) for j in range(3)
            ]
            normal, tangential = trace[0], trace[1:]
            mine = traces([state[z, f, a] for f in range(4)], 0, s)
            there = traces(u_out, 0, s)
            normal = normal - (2.0 * JUMP) * (mine[2] - there[2])
            tangential = [t - JUMP * (m - o) for t, m, o in zip(tangential, mine[:2], there[:2])]
            t = float(sign)
            weight = weights[sign] * jnp.where(end, 0.0, 1.0)
            block = W_CORNERS + 2 * side
            edge = met_terms(u_out, w_from[z][block : block + 2], t, weight)
            normal = normal + edge[0] + s * edge[3]
            tangential = [tangential[0] + edge[1], tangential[1] + edge[2]]
            scaled = SCALE * resistance[2 + 2 * side + z]
            normal = normal + scaled * u_out[0]
            tangential = [v + scaled * u_out[1 + j] for j, v in enumerate(tangential)]
            inner = traces([w[f][a] for f in range(4)], 0, -s)
            flag = small[1, X_WALL + 2 * side + z : X_WALL + 2 * side + z + 1, :]
            image = inner[:2] + [(1.0 - 2.0 * flag) * inner[2]]
            last = (x_place == nx - 1) if side else (x_place == 0)
            outer = [jnp.where(last, i, o) for i, o in zip(image, tangential + [normal])]
            terms = face_terms(inner, outer, 0, s, JUMP, True)
            for f in range(4):
                adjoint[z, f, a] += terms[f]
        copies.append(pltpu.make_async_copy(adjoint.at[z], adjoint_out.at[z], done.at[z]))
        copies[-1].start()
        if z == 1:
            held = jnp.exp(-small[1, LOGK : LOGK + 1, 0:length])
            summed = jnp.sum(received[...], axis=0, keepdims=True)
            first, second = summed[:, length : 2 * length], summed[:, 2 * length : 3 * length]
            gradient[...] = -(SCALE / 64.0) * held * (first + SCALE * held * second)
            copies.append(pltpu.make_async_copy(gradient, gradient_out, done.at[2]))
            copies[-1].start()
    for copy in copies:
        copy.wait()


def call(kernel, operands, in_spec, shapes, out_spec, scratch, room):
    return pl.pallas_call(
        kernel,
        out_shape=[jax.ShapeDtypeStruct(shape, jnp.float32) for shape in shapes],
        in_specs=[in_spec] * len(operands),
        out_specs=[out_spec] * len(shapes),
        scratch_shapes=scratch,
        compiler_params=pltpu.CompilerParams(vmem_limit_bytes=room * 1024),
        cost_estimate=pl.CostEstimate(flops=2000000, bytes_accessed=800000, transcendentals=0),
    )(*operands)


def both_ways(pairs):
    return pairs + [(second, first) for first, second in pairs]


def along_z(payloads, nz):
    if nz == 2:
        return [lax.ppermute(payloads[0], "gz", [(0, 1), (1, 0)])]
    up = [(i, i + 1) for i in range(nz - 1)]
    down = [(second, first) for first, second in up]
    return [lax.ppermute(payloads[0], "gz", up), lax.ppermute(payloads[1], "gz", down)]


def shards(nx, nz, state, target, coarse_logk, cell_slot, cell_of, wall_flags_xaxis, z_wall):
    sizes = (nx, nz)
    shape = (2, 4, 4, 2, 8, LANES)
    length = coarse_logk.shape[0]
    state6, target6 = state.reshape(shape), target.reshape(shape)
    z_flags = z_wall.reshape(2, LANES)
    count = 1 if nz == 2 else 2
    x_shape, z_shape, w_shape = ((n, 8, LANES) for n in (X_BLOCKS, Z_BLOCKS, W_BLOCKS))
    held, first_a, first_b = call(
        faces_kernel,
        [state6, target6],
        HBM,
        [shape, x_shape, x_shape],
        VMEM,
        [pltpu.VMEM((2, 2, 4, 2, 8, LANES), jnp.float32), pltpu.SemaphoreType.DMA((3,))],
        54600,
    )
    pay_a, pay_b, positions = call(
        functools.partial(edges_kernel, sizes),
        [first_a, first_b, cell_of.reshape(2, LANES), cell_slot.reshape(-1, LANES), z_flags],
        VMEM,
        [x_shape, x_shape, (8, LANES)],
        VMEM,
        [],
        16 * 1024,
    )
    pairs_b = both_ways([(i, i + 1) for i in range(1, nx - 1, 2)])
    pairs_a = both_ways([(i, i + 1) for i in range(0, nx - 1, 2)])
    got_a = lax.ppermute(pay_a, "gx", pairs_a)
    got_b = lax.ppermute(pay_b, "gx", pairs_b)
    small, local, *z_pay = call(
        functools.partial(local_kernel, sizes),
        [held, positions, target6, wall_flags_xaxis, z_flags, coarse_logk.reshape(1, -1)],
        VMEM,
        [(3, 8, LANES), shape] + [z_shape] * count,
        VMEM,
        [],
        16 * 1024,
    )
    z_got = along_z(z_pay, nz)
    whole, send, *w_pay = call(
        functools.partial(sums_kernel, sizes, length),
        [held, small, local, got_a, got_b] + z_got,
        VMEM,
        [shape, (nx * nz, LANES)] + [w_shape] * count,
        VMEM,
        [],
        16 * 1024,
    )
    w_got = along_z(w_pay, nz)
    received = lax.all_to_all(send, ("gx", "gz"), 0, 0, tiled=True)
    adjoint, gradient = call(
        functools.partial(adjoint_kernel, sizes, length),
        [held, small, whole, got_a, got_b, received] + z_got + w_got,
        VMEM,
        [shape, (1, length)],
        HBM,
        [
            pltpu.VMEM(shape, jnp.float32),
            pltpu.VMEM((1, length), jnp.float32),
            pltpu.SemaphoreType.DMA((3,)),
        ],
        16 * 1024,
    )
    return adjoint.reshape(state.shape), gradient.reshape(-1)


def solution(mesh):
    placed = (
        P("gx", "gz", None, None, None),
        P("gx", "gz", None, None, None),
        P(("gx", "gz")),
        P(),
        P("gx", "gz", None),
        P(None, "gz", None),
        P(None, "gx", None),
    )
    return jax.shard_map(
        functools.partial(shards, mesh.shape["gx"], mesh.shape["gz"]),
        mesh=mesh,
        in_specs=placed,
        out_specs=(P("gx", "gz", None, None, None), P(("gx", "gz"))),
        check_vma=False,
    )
```
